256 devices in a mesh: lat: 16 (over z, y_lo), lon: 16 (over x, y_hi, core).
Axes of the slice: x: 4, y: 4 (y_hi: 2, y_lo: 2; y = y_hi * 2 + y_lo), z: 8, core: 2. Of those that a mesh axis runs over, the one named last changes fastest.
Arguments:
- fields: float32 [2, 192, 96, 512], P(None, 'lat', 'lon'), may hold values from -13 to 13, as said below
- grad_out: float32 [2, 192, 96, 512], P(None, 'lat', 'lon'), may hold values from -6 to 6
- region_ids: int32 [2, 192, 96], P(None, 'lat', 'lon'), may hold values from 0 to 2
- bias_index: int32 [144, 144], replicated, may hold values from 0 to 6335
- bias_table: float32 [6336, 16], replicated, may hold values from -4 to 4
- in_weight: float32 [512, 1536], replicated, may hold values from -5 to 5, as said below
- out_weight: float32 [512, 512], replicated, may hold values from -0.25 to 0.25
Outputs:
- grad_fields: float32 [2, 192, 96, 512], P(None, 'lat', 'lon')
- grad_in_weight: float32 [512, 1536], P('lon')
- grad_out_weight: float32 [512, 512], P('lon')
- grad_bias: float32 [6336, 16], P('lon')
The draws below stay inside these ranges and needn't reach their ends.
Inputs may be any that keep to these rules, and one draw needn't show every extreme that they name: `fields`: rows of the tokens have scales that differ widely. `in_weight`: Fan-in scaled; the query and key columns of each head carry a gain of their own.
All inputs are finite; a program needn't handle non-finite values.
Results may differ from the reference program's by a relative error of at most 0.0003.
Values sent between devices are 32-bit elements; how exact they have to be, the bound alone decides.
No kernel may reach another device: no remote copies, remote signals or barrier semaphores. Data moves between devices by JAX's collectives and lax.ppermute only.
A program may use at most 128 MiB of HBM per device.

```python
import math
import jax
import jax.numpy as jnp
from jax import lax

WIDTH = 512
HEADS = 16
HEAD_DIM = 32
LEVELS = 2
WIN_LAT = 12
WIN_LON = 6
BIAS_ROWS = 6336
LAT_CELLS = 192
LON_CELLS = 96
WIN_TOKENS = 144


def draw_fields(key, part):
    key = jax.random.fold_in(key, 11)
    key_base, key_scale = jax.random.split(key, 2)
    full_shape = (LEVELS, LAT_CELLS, LON_CELLS, WIDTH)
    raw_values = jax.random.truncated_normal(key_base, -4.0, 4.0, full_shape, jnp.float32)
    scales = jnp.exp(jax.random.uniform(key_scale, full_shape[:3] + (1,), jnp.float32, math.log(0.3), math.log(3.0)))
    return raw_values * scales


def draw_in_weight(key, part):
    key = jax.random.fold_in(key, 12)
    key_base, key_heads = jax.random.split(key, 2)
    raw_weight = jax.random.truncated_normal(key_base, -4.0, 4.0, (WIDTH, 3 * WIDTH), jnp.float32) * WIDTH ** (-0.5)
    log_low, log_high = (math.log(0.5), math.log(2.0))
    head_gain = jnp.exp(jax.random.uniform(key_heads, (2, HEADS), jnp.float32, log_low, log_high))
    head_gain = jnp.concatenate([head_gain, jnp.ones((1, HEADS), jnp.float32)], axis=0)
    column_gain = jnp.repeat(head_gain, HEAD_DIM, axis=1).reshape(3 * WIDTH)
    return raw_weight * column_gain[None, :]


def place_ends(entries, own_key, smallest, high):
    longest = entries.shape.index(max(entries.shape))
    spots = []
    for shift in (0, 1):
        where = [jax.random.randint(jax.random.fold_in(own_key, axis), (), 0, length) for axis, length in enumerate(entries.shape)]
        where[longest] = (where[longest] + shift) % entries.shape[longest]
        spots.append(tuple(where))
    return entries.at[spots[0]].set(smallest).at[spots[1]].set(high)


def levels(rng, dims, cuts, low, high):
    gain, own = 1.0, jax.random.fold_in(rng, 6)
    for position, blocks in cuts:
        steps = jnp.exp(jax.random.uniform(jax.random.fold_in(own, position), (blocks,), jnp.float32, low / len(cuts), high / len(cuts)))
        gain = gain * jnp.repeat(steps, dims[position] // blocks).reshape([-1 if axis == position else 1 for axis in range(len(dims))])
    return gain


def centred(stream_key, shape, spread, limit, cuts=(), kind=jnp.bfloat16):
    gain = levels(stream_key, shape, cuts, -0.22, 0.18) if cuts else 1.0
    values = jax.random.normal(stream_key, shape, jnp.float32) * spread * gain
    return jnp.minimum(jnp.maximum(values, -limit), limit).astype(kind)


def setup_inputs(seed: int = 0) -> dict:
    arg_keys = jax.random.split(jax.random.key(seed), 8)
    return {
        "fields": draw_fields(jax.random.fold_in(arg_keys[7], 71), 0),
        "grad_out": centred(arg_keys[1], (LEVELS, LAT_CELLS, LON_CELLS, WIDTH), 1.0, 6.0, ((1, 16), (2, 16)), jnp.float32),
        "region_ids": place_ends(jax.random.randint(arg_keys[2], (LEVELS, LAT_CELLS, LON_CELLS), 0, 3), jax.random.fold_in(arg_keys[2], 1), 0, 2).astype(jnp.int32),
        "bias_index": place_ends(jax.random.randint(arg_keys[3], (WIN_TOKENS, WIN_TOKENS), 0, BIAS_ROWS), jax.random.fold_in(arg_keys[3], 1), 0, BIAS_ROWS - 1).astype(jnp.int32),
        "bias_table": centred(arg_keys[4], (BIAS_ROWS, HEADS), 1.0, 4.0, (), jnp.float32),
        "in_weight": draw_in_weight(jax.random.fold_in(arg_keys[7], 71), 0),
        "out_weight": centred(arg_keys[6], (WIDTH, WIDTH), WIDTH ** -0.5, 0.25, (), jnp.float32),
    }


def split_windows(array):
    level_count, row_count, col_count = array.shape[:3]
    trailing = array.shape[3:]
    blocked = array.reshape((level_count, row_count // WIN_LAT, WIN_LAT, col_count // WIN_LON, WIN_LON) + trailing)
    axis_order = (1, 3, 0, 2, 4) + tuple(range(5, 5 + len(trailing)))
    blocked = jnp.transpose(blocked, axis_order)
    return blocked.reshape((row_count // WIN_LAT * (col_count // WIN_LON), level_count * WIN_LAT * WIN_LON) + trailing)

def join_windows(windows, level_count, row_count, col_count):
    trailing = windows.shape[2:]
    blocked = windows.reshape((row_count // WIN_LAT, col_count // WIN_LON, level_count, WIN_LAT, WIN_LON) + trailing)
    axis_order = (2, 0, 3, 1, 4) + tuple(range(5, 5 + len(trailing)))
    blocked = jnp.transpose(blocked, axis_order)
    return blocked.reshape((level_count, row_count, col_count) + trailing)

def window_pass(inputs, cotangent, labels, owned, in_weight, out_weight, bias_full):
    highest = lax.Precision.HIGHEST
    average = lax.optimization_barrier(jnp.mean(inputs, axis=-1, keepdims=True))
    centered = inputs - average
    variance = lax.optimization_barrier(jnp.mean(centered * centered, axis=-1, keepdims=True))
    inv_std = lax.rsqrt(variance + 1e-05)
    normed = centered * inv_std
    projected = jnp.einsum('wtc,cf->wtf', normed, in_weight, precision=highest)
    win_count, tok_count = (inputs.shape[0], inputs.shape[1])
    heads_split = projected.reshape(win_count, tok_count, 3, HEADS, HEAD_DIM)
    queries = heads_split[:, :, 0]
    key_vecs = heads_split[:, :, 1]
    value_vecs = heads_split[:, :, 2]
    factor = HEAD_DIM ** (-0.5)
    scores = jnp.einsum('wqhd,wkhd->whqk', queries, key_vecs, precision=highest) * factor + bias_full[None]
    allowed = (labels[:, :, None] == labels[:, None, :]) & (labels[:, None, :] > 0.5)
    scores = jnp.where(allowed[:, None], scores, -1000000000.0)
    peak = lax.optimization_barrier(jnp.max(scores, axis=-1, keepdims=True))
    exponent = jnp.exp(scores - peak)
    probs = exponent / lax.optimization_barrier(jnp.sum(exponent, axis=-1, keepdims=True))
    attended = jnp.einsum('whqk,wkhd->wqhd', probs, value_vecs, precision=highest).reshape(win_count, tok_count, WIDTH)
    grad_attended = jnp.einsum('wte,ce->wtc', cotangent, out_weight, precision=highest)
    grad_out_part = jnp.einsum('wtc,wte->ce', attended * owned[..., None], cotangent, precision=highest)
    grad_heads = grad_attended.reshape(win_count, tok_count, HEADS, HEAD_DIM)
    grad_probs = jnp.einsum('wqhd,wkhd->whqk', grad_heads, value_vecs, precision=highest)
    grad_values = jnp.einsum('whqk,wqhd->wkhd', probs, grad_heads, precision=highest)
    grad_scores = probs * (grad_probs - lax.optimization_barrier(jnp.sum(grad_probs * probs, axis=-1, keepdims=True)))
    grad_queries = jnp.einsum('whqk,wkhd->wqhd', grad_scores, key_vecs, precision=highest) * factor
    grad_keys = jnp.einsum('whqk,wqhd->wkhd', grad_scores, queries, precision=highest) * factor
    score_sum = jnp.einsum('whqk,wq->hqk', grad_scores, owned, precision=highest)
    grad_projected = jnp.stack([grad_queries, grad_keys, grad_values], axis=2).reshape(win_count, tok_count, 3 * WIDTH)
    grad_in_part = jnp.einsum('wtc,wtf->cf', normed * owned[..., None], grad_projected, precision=highest)
    grad_normed = jnp.einsum('wtf,cf->wtc', grad_projected, in_weight, precision=highest)
    grad_inputs = inv_std * (grad_normed - lax.optimization_barrier(jnp.mean(grad_normed, axis=-1, keepdims=True)) - normed * lax.optimization_barrier(jnp.mean(grad_normed * normed, axis=-1, keepdims=True)))
    return (grad_inputs, grad_in_part, grad_out_part, score_sum)

def reference(fields, grad_out, region_ids, bias_index, bias_table, in_weight, out_weight):
    level_count, row_count, col_count, width = fields.shape
    half_rows = WIN_LAT // 2
    half_cols = WIN_LON // 2

    def prepare(array):
        pad_widths = ((0, 0), (half_rows, half_rows)) + ((0, 0),) * (array.ndim - 2)
        return jnp.roll(jnp.pad(array, pad_widths), -half_cols, axis=2)
    padded_in = prepare(fields)
    padded_grad = prepare(grad_out)
    padded_labels = prepare((region_ids + 1).astype(jnp.float32))
    bias_full = jnp.transpose(bias_table[bias_index], (2, 0, 1))
    band_count = (row_count + 2 * half_rows) // WIN_LAT

    def band_step(totals_so_far, band_number):
        first_row = band_number * WIN_LAT
        band_in = lax.dynamic_slice_in_dim(padded_in, first_row, WIN_LAT, 1)
        band_grad = lax.dynamic_slice_in_dim(padded_grad, first_row, WIN_LAT, 1)
        band_labels = lax.dynamic_slice_in_dim(padded_labels, first_row, WIN_LAT, 1)
        win_labels = split_windows(band_labels)
        owned = jnp.ones(win_labels.shape, jnp.float32)
        grad_win, part_in, part_out, part_scores = window_pass(split_windows(band_in), split_windows(band_grad), win_labels, owned, in_weight, out_weight, bias_full)
        new_totals = (totals_so_far[0] + part_in, totals_so_far[1] + part_out, totals_so_far[2] + part_scores)
        return (new_totals, join_windows(grad_win, level_count, WIN_LAT, col_count))
    zero_totals = (jnp.zeros((width, 3 * width), jnp.float32), jnp.zeros((width, width), jnp.float32), jnp.zeros((HEADS, WIN_TOKENS, WIN_TOKENS), jnp.float32))
    totals, banded = lax.scan(band_step, zero_totals, jnp.arange(band_count, dtype=jnp.int32))
    stacked = jnp.transpose(banded, (1, 0, 2, 3, 4)).reshape(level_count, band_count * WIN_LAT, col_count, width)
    grad_attn = jnp.roll(stacked[:, half_rows:half_rows + row_count], half_cols, axis=2)
    grad_fields = grad_out + grad_attn
    flat_scores = jnp.transpose(totals[2], (1, 2, 0)).reshape(-1, HEADS)
    grad_bias = jax.ops.segment_sum(flat_scores, bias_index.reshape(-1), num_segments=BIAS_ROWS)
    return (grad_fields, totals[0], totals[1], grad_bias)
```

```python
import functools

import jax
import jax.numpy as jnp
import numpy as np
from jax import lax
from jax.experimental import pallas as pl
from jax.experimental.pallas import tpu as pltpu
from jax.sharding import PartitionSpec as P

WIDTH = 512
HEADS = 16
HEAD_DIM = 32
TOKENS = 144
QUAD = 36
BIAS_ROWS = 6336
HALF_SECTOR = 198
FACTOR = HEAD_DIM ** (-0.5)
F32 = jnp.float32
BF16 = jnp.bfloat16
MEGA = 1 << 20


def params(mib=48):
    return pltpu.CompilerParams(vmem_limit_bytes=mib * MEGA)


def whole(count):
    return [pl.BlockSpec(memory_space=pltpu.VMEM)] * count


def scalar():
    return pl.BlockSpec(memory_space=pltpu.SMEM)


def halves(x):
    high = x.astype(BF16)
    low = (x - high.astype(F32)).astype(BF16)
    return high, low


def dot(a, b, dims):
    return lax.dot_general(a, b, (dims, ((), ())), preferred_element_type=F32)


NN = ((1,), (0,))
NT = ((1,), (1,))
TN = ((0,), (0,))


def dot3(a, b, dims):
    ah, al = a
    bh, bl = b
    return dot(ah, bh, dims) + (dot(ah, bl, dims) + dot(al, bh, dims))


def token_order():
    grid = np.arange(TOKENS).reshape(2, 2, 6, 2, 3)
    return np.transpose(grid, (1, 3, 0, 2, 4)).reshape(-1)


def pack_kernel(last, fields, grads, ids, own, left, below, corner):
    lanes = lax.broadcasted_iota(jnp.int32, (6, WIDTH), 1)
    rows = lax.broadcasted_iota(jnp.int32, (6, WIDTH), 0)
    bump = last[0]
    plan = (
        (own, 0, 3, 2, None),
        (left, 0, 0, 3, None),
        (below, 6, 3, 0, bump),
        (corner, 6, 0, 1, bump),
    )
    for ref, row0, col0, quadrant, offset in plan:
        label = jnp.zeros((6, WIDTH), jnp.int32)
        for level in range(2):
            for row in range(6):
                spot = level * 18 + row * 3
                ref[spot : spot + 3, :] = fields[level, row0 + row, col0 : col0 + 3, :]
                ref[QUAD + spot : QUAD + spot + 3, :] = grads[
                    level, row0 + row, col0 : col0 + 3, :
                ]
            for col in range(3):
                column = ids[level, row0 : row0 + 6, col0 + col : col0 + col + 1] + 1
                if offset is not None:
                    column = column + offset
                place = quadrant * QUAD + level * 18 + col
                label = label + jnp.where(
                    lanes == rows * 3 + place, jnp.broadcast_to(column, (6, WIDTH)), 0
                )
        total = jnp.sum(label.astype(F32), axis=0, keepdims=True)
        ref[72:80, :] = jnp.broadcast_to(total, (8, WIDTH))


def pack(last, fields, grads, ids):
    shape = jax.ShapeDtypeStruct((80, WIDTH), F32)
    return pl.pallas_call(
        pack_kernel,
        out_shape=[shape] * 4,
        in_specs=[scalar()] + whole(3),
        out_specs=whole(4),
        compiler_params=params(),
        name="pack",
    )(last, fields, grads, ids)


def order_kernel(index, order, wide, narrow):
    value = index[...]
    high = (value >> 7).astype(F32).astype(BF16)
    low = (value & 127).astype(F32).astype(BF16)
    move = order[...]

    def moved(part):
        return dot(dot(move, part, NN).astype(BF16), move, NT)

    result = (moved(high) * 128.0 + moved(low)).astype(jnp.int32)
    wide[...] = result[:, :128]
    narrow[...] = result[:, 128:]


def ordered_index(bias_index):
    order = np.zeros((TOKENS, TOKENS), np.float32)
    order[np.arange(TOKENS), token_order()] = 1.0
    wide, narrow = pl.pallas_call(
        order_kernel,
        out_shape=[
            jax.ShapeDtypeStruct((TOKENS, 128), jnp.int32),
            jax.ShapeDtypeStruct((TOKENS, 16), jnp.int32),
        ],
        in_specs=whole(2),
        out_specs=whole(2),
        compiler_params=params(),
        name="order",
    )(bias_index, jnp.asarray(order, BF16))
    return wide, narrow.reshape(18, 128)


def lookup_kernel(wide, narrow, table, out_wide, out_narrow):
    spots = [(wide, out_wide, 8 * i, 8) for i in range(18)]
    spots += [(narrow, out_narrow, 8 * i, 8) for i in range(3)]
    groups = [spots[:7], spots[7:14], spots[14:]]

    def one_head(head, carry):
        for group in groups:
            lows = [src[at : at + size, :] & 127 for src, _, at, size in group]
            highs = [src[at : at + size, :] >> 7 for src, _, at, size in group]

            def step(block, found):
                row = jnp.broadcast_to(table[head, pl.ds(block, 1), :], (8, 128))
                new = []
                for low, high, value in zip(lows, highs, found):
                    pick = jnp.take_along_axis(row, low, axis=1, mode="promise_in_bounds")
                    new.append(jnp.where(high == block, pick, value))
                return tuple(new)

            found = lax.fori_loop(
                0, 50, step, tuple(jnp.zeros((8, 128), F32) for _ in group), unroll=5
            )
            for value, (_, dst, at, size) in zip(found, group):
                dst[head, at : at + size, :] = value
        return carry

    lax.fori_loop(0, HEADS, one_head, 0)


def lookup(wide, narrow, bias_table):
    table = jnp.pad(bias_table.T, ((0, 0), (0, 6400 - BIAS_ROWS))).reshape(HEADS, 50, 128)
    narrow = jnp.pad(narrow, ((0, 6), (0, 0)))
    out_wide, out_narrow = pl.pallas_call(
        lookup_kernel,
        out_shape=[
            jax.ShapeDtypeStruct((HEADS, TOKENS, 128), F32),
            jax.ShapeDtypeStruct((HEADS, 24, 128), F32),
        ],
        in_specs=whole(3),
        out_specs=whole(2),
        compiler_params=params(),
        name="lookup",
    )(wide, narrow, table)
    return out_wide, out_narrow[:, :18].reshape(HEADS, TOKENS, 16)


def main_kernel(
    core_ref,
    own,
    quad0,
    quad1,
    quad3,
    bias_wide,
    bias_narrow,
    in_weight,
    out_weight,
    keep,
    send,
    keep_wide,
    send_wide,
    keep_narrow,
    send_narrow,
    grad0,
    grad1,
    grad2,
    grad3,
    tokens,
    cotangent,
    proj,
    gatt,
    gproj,
    att,
    normed_t,
):
    core = core_ref[0]
    for slot, quad in enumerate((quad0, quad1, own, quad3)):
        at = slot * QUAD
        tokens[at : at + QUAD, :] = quad[0:QUAD, :]
        cotangent[at : at + QUAD, :] = quad[QUAD : 2 * QUAD, :]
    row = (quad0[72:73, :] + quad1[72:73, :] + own[72:73, :] + quad3[72:73, :])[:, :TOKENS]
    side = lax.broadcasted_iota(jnp.int32, (TOKENS, TOKENS), 0)
    along = lax.broadcasted_iota(jnp.int32, (TOKENS, TOKENS), 1)
    spread = jnp.broadcast_to(row, (TOKENS, TOKENS))
    column = jnp.sum(jnp.where(side == along, spread, 0.0), axis=1, keepdims=True)
    allowed = column == spread

    inputs = tokens[...]
    centered = inputs - jnp.mean(inputs, axis=1, keepdims=True)
    variance = jnp.mean(centered * centered, axis=1, keepdims=True)
    inv_std = lax.rsqrt(variance + 1e-05)
    normed = centered * inv_std
    tokens[...] = normed
    normed_t[...] = normed.T
    halves_normed = halves(normed)
    for part in range(3):
        at = part * WIDTH
        weight = halves(in_weight[:, at : at + WIDTH])
        proj[at : at + WIDTH, :] = dot3(halves_normed, weight, NN).T
    halves_cotangent = halves(cotangent[...])
    gatt[...] = dot3(halves(out_weight[...]), halves_cotangent, NT)

    def one_head(head):
        at = pl.multiple_of(head * HEAD_DIM, HEAD_DIM)
        qh, ql = halves(proj[pl.ds(at, HEAD_DIM), :] * FACTOR)
        kh, kl = halves(proj[pl.ds(at + WIDTH, HEAD_DIM), :])
        vh, vl = halves(proj[pl.ds(at + 2 * WIDTH, HEAD_DIM), :])
        gh, gl = halves(gatt[pl.ds(at, HEAD_DIM), :])
        bias = jnp.concatenate([bias_wide[head], bias_narrow[head]], axis=1)

        def stacked(*parts):
            return jnp.concatenate(parts, axis=0)

        scores = dot(stacked(qh, qh, ql), stacked(kh, kl, kh), TN) + bias
        scores = jnp.where(allowed, scores, -1000000000.0)
        peak = jnp.max(scores, axis=1, keepdims=True)
        exponent = jnp.exp(scores - peak)
        probs = exponent * (1.0 / jnp.sum(exponent, axis=1, keepdims=True))
        grad_probs = dot(stacked(gh, gh, gl), stacked(vh, vl, vh), TN)
        inner = jnp.sum(grad_probs * probs, axis=1, keepdims=True)
        grad_scores = probs * (grad_probs - inner)
        ph, plow = halves(probs)
        sh, sl = halves(grad_scores)

        def product(high, low, right_high, right_low, dims):
            both = dot(stacked(high, low), right_high, dims)
            return both[:HEAD_DIM] + (both[HEAD_DIM:] + dot(high, right_low, dims))

        att[pl.ds(at, HEAD_DIM), :] = product(vh, vl, ph, plow, NT)
        gproj[pl.ds(at + 2 * WIDTH, HEAD_DIM), :] = product(gh, gl, ph, plow, NN)
        gproj[pl.ds(at, HEAD_DIM), :] = product(kh, kl, sh, sl, NT) * FACTOR
        gproj[pl.ds(at + WIDTH, HEAD_DIM), :] = product(qh, ql, sh, sl, NN)
        return grad_scores

    for slot in range(8):
        grad_scores = one_head((1 - core) * 8 + slot)
        send_wide[:, slot, :] = grad_scores[:, :128]
        send_narrow[slot] = grad_scores[:, 128:]
        grad_scores = one_head(core * 8 + slot)
        keep_wide[:, slot, :] = grad_scores[:, :128]
        keep_narrow[slot] = grad_scores[:, 128:]

    for target, bit in ((send, 1 - core), (keep, core)):
        rows = [pl.ds(pl.multiple_of(64 * i + 32 * bit, 32), 32) for i in range(8)]
        left = halves(jnp.concatenate([normed_t[r, :] for r in rows], axis=0))
        for part in range(3):
            at = part * WIDTH
            target[:, at : at + WIDTH] = dot3(left, halves(gproj[at : at + WIDTH, :]), NT)
        left = halves(jnp.concatenate([att[r, :] for r in rows], axis=0))
        target[:, 3 * WIDTH :] = dot3(left, halves_cotangent, NN)

    grad_normed = jnp.zeros((WIDTH, TOKENS), F32)
    for part in range(3):
        at = part * WIDTH
        grad_normed = grad_normed + dot3(
            halves(in_weight[:, at : at + WIDTH]), halves(gproj[at : at + WIDTH, :]), NN
        )
    grad_normed = grad_normed.T
    normed = tokens[...]
    result = inv_std * (
        grad_normed
        - jnp.mean(grad_normed, axis=1, keepdims=True)
        - normed * jnp.mean(grad_normed * normed, axis=1, keepdims=True)
    )
    tokens[...] = result
    for slot, target in enumerate((grad0, grad1, grad2, grad3)):
        target[...] = tokens[slot * QUAD : slot * QUAD + QUAD, :]


def window(core, own, quad0, quad1, quad3, bias_wide, bias_narrow, in_weight, out_weight):
    def shape(*dims):
        return jax.ShapeDtypeStruct(dims, F32)

    grad = shape(QUAD, WIDTH)
    return pl.pallas_call(
        main_kernel,
        out_shape=[
            shape(256, 4 * WIDTH),
            shape(256, 4 * WIDTH),
            shape(TOKENS, 8, 128),
            shape(TOKENS, 8, 128),
            shape(8, TOKENS, 16),
            shape(8, TOKENS, 16),
            grad,
            grad,
            grad,
            grad,
        ],
        in_specs=[scalar()] + whole(8),
        out_specs=whole(10),
        scratch_shapes=[
            pltpu.VMEM((TOKENS, WIDTH), F32),
            pltpu.VMEM((TOKENS, WIDTH), F32),
            pltpu.VMEM((3 * WIDTH, TOKENS), F32),
            pltpu.VMEM((WIDTH, TOKENS), F32),
            pltpu.VMEM((3 * WIDTH, TOKENS), F32),
            pltpu.VMEM((WIDTH, TOKENS), F32),
            pltpu.VMEM((WIDTH, TOKENS), F32),
        ],
        compiler_params=params(56),
        name="window",
    )(core, own, quad0, quad1, quad3, bias_wide, bias_narrow, in_weight, out_weight)


def scatter_kernel(
    wide, narrow, keep_wide, came_wide, keep_narrow, came_narrow, out, total, wide_sum
):
    total[...] = jnp.zeros_like(total)
    wide_sum[...] = keep_wide[...] + came_wide[...]
    lines = lax.broadcasted_iota(jnp.int32, (256, 128), 0).astype(F32).astype(BF16)

    def sides(index, values):
        block = jnp.zeros_like(index)
        for edge in range(1, 32):
            block = block + jnp.where(index >= edge * HALF_SECTOR, 1, 0)
        inside = (index - block * HALF_SECTOR).astype(F32).astype(BF16)
        block = block.astype(F32).astype(BF16)
        high, low = halves(values)
        both = jnp.concatenate([high, low], axis=0)
        spread = jnp.broadcast_to(block, (16, 128))
        left = jnp.concatenate(
            [jnp.where(spread == float(b), both, jnp.zeros_like(both)) for b in range(32)], axis=0
        )
        hit = lines == jnp.broadcast_to(inside, (256, 128))
        right = jnp.where(hit, jnp.ones((256, 128), BF16), jnp.zeros((256, 128), BF16))
        return left, right

    def add(pieces):
        left = jnp.concatenate([p[0] for p in pieces], axis=1)
        right = jnp.concatenate([p[1] for p in pieces], axis=1)
        total[...] += dot(left, right, NT)

    def wide_step(step, carry):
        base = pl.multiple_of(step * 8, 8)
        index = wide[pl.ds(base, 8), :]
        for pair in range(4):
            add(
                [
                    sides(index[j : j + 1, :], wide_sum[base + j])
                    for j in (2 * pair, 2 * pair + 1)
                ]
            )
        return carry

    lax.fori_loop(0, 18, wide_step, 0)
    for pair in range(9):
        add(
            [
                sides(narrow[j : j + 1, :], keep_narrow[:, j, :] + came_narrow[:, j, :])
                for j in (2 * pair, 2 * pair + 1)
            ]
        )
    for block in range(32):
        chip, core, half = block // 4, block // 2 % 2, block % 2
        value = total[block * 16 : block * 16 + 8, :] + total[block * 16 + 8 : block * 16 + 16, :]
        out[chip, half * 16 + core * 8 : half * 16 + core * 8 + 8, :] = value


def scatter(wide, narrow, keep_wide, came_wide, keep_narrow, came_narrow):
    return pl.pallas_call(
        scatter_kernel,
        out_shape=jax.ShapeDtypeStruct((8, 32, 256), F32),
        in_specs=whole(6),
        out_specs=pl.BlockSpec(memory_space=pltpu.VMEM),
        scratch_shapes=[pltpu.VMEM((512, 256), F32), pltpu.VMEM((TOKENS, 8, 128), F32)],
        compiler_params=params(),
        name="scatter",
    )(
        wide,
        narrow,
        keep_wide,
        came_wide,
        keep_narrow.reshape(8, 18, 128),
        came_narrow.reshape(8, 18, 128),
    )


def join_kernel(keep, came, table, out):
    for i in range(8):
        out[i, :, : 4 * WIDTH] = keep[i * 32 : i * 32 + 32, :] + came[i * 32 : i * 32 + 32, :]
        out[i, :, 4 * WIDTH :] = table[i]


def join(keep, came, table):
    return pl.pallas_call(
        join_kernel,
        out_shape=jax.ShapeDtypeStruct((8, 32, 2304), F32),
        in_specs=whole(3),
        out_specs=pl.BlockSpec(memory_space=pltpu.VMEM),
        compiler_params=params(),
        name="join",
    )(keep, came, table)


def fold_lon_kernel(parts, out):
    def rows(at):
        total = parts[0, at : at + 8, :]
        for i in range(1, 8):
            total = total + parts[i, at : at + 8, :]
        return total

    for group in range(4):
        total = rows(group * 8)
        for col in range(4):
            if col < 3:
                out[group * 4 + col] = total[:, col * 640 : col * 640 + 640]
            else:
                out[group * 4 + col, :, :384] = total[:, 1920:2304]
                out[group * 4 + col, :, 384:] = jnp.zeros((8, 256), F32)


def fold_lon(parts):
    return pl.pallas_call(
        fold_lon_kernel,
        out_shape=jax.ShapeDtypeStruct((16, 8, 640), F32),
        in_specs=whole(1),
        out_specs=pl.BlockSpec(memory_space=pltpu.VMEM),
        compiler_params=params(),
        name="fold_lon",
    )(parts)


def fold_lat_kernel(parts, out):
    total = parts[0]
    for i in range(1, 16):
        total = total + parts[i]
    for i in range(16):
        out[i] = total


def fold_lat(parts):
    return pl.pallas_call(
        fold_lat_kernel,
        out_shape=jax.ShapeDtypeStruct((16, 8, 640), F32),
        in_specs=whole(1),
        out_specs=pl.BlockSpec(memory_space=pltpu.VMEM),
        compiler_params=params(),
        name="fold_lat",
    )(parts)


def unpack_kernel(core_ref, parts, grad_in, grad_out, keep, send):
    core = core_ref[0]
    for group in range(4):
        rows = slice(group * 8, group * 8 + 8)
        base = group * 4
        grad_in[rows, 0:640] = parts[base]
        grad_in[rows, 640:1280] = parts[base + 1]
        grad_in[rows, 1280:1536] = parts[base + 2, :, :256]
        grad_out[rows, 0:384] = parts[base + 2, :, 256:]
        grad_out[rows, 384:512] = parts[base + 3, :, :128]
    for half in range(2):
        keep[half] = parts[half * 8 + core * 4 + 3, :, 128:384]
        send[half] = parts[half * 8 + (1 - core) * 4 + 3, :, 128:384]


def unpack(core, parts):
    table = jax.ShapeDtypeStruct((2, 8, 256), F32)
    return pl.pallas_call(
        unpack_kernel,
        out_shape=[
            jax.ShapeDtypeStruct((32, 3 * WIDTH), F32),
            jax.ShapeDtypeStruct((32, WIDTH), F32),
            table,
            table,
        ],
        in_specs=[scalar()] + whole(1),
        out_specs=whole(4),
        compiler_params=params(),
        name="unpack",
    )(core, parts)


def place_kernel(grad_out, own, left, below, corner, out):
    for ref, row0, col0 in ((own, 0, 3), (left, 0, 0), (below, 6, 3), (corner, 6, 0)):
        for level in range(2):
            for row in range(6):
                spot = level * 18 + row * 3
                here = (level, row0 + row, slice(col0, col0 + 3), slice(None))
                out[here] = grad_out[here] + ref[spot : spot + 3, :]


def place(grad_out, own, left, below, corner):
    return pl.pallas_call(
        place_kernel,
        out_shape=jax.ShapeDtypeStruct(grad_out.shape, F32),
        in_specs=whole(5),
        out_specs=pl.BlockSpec(memory_space=pltpu.VMEM),
        compiler_params=params(),
        name="place",
    )(grad_out, own, left, below, corner)


def body(fields, grad_out, region_ids, bias_index, bias_table, in_weight, out_weight):
    lat_count = lax.axis_size("lat")
    lon_count = lax.axis_size("lon")
    both = ("lat", "lon")
    lat = lax.axis_index("lat")
    core = lax.rem(lax.axis_index("lon"), 2).reshape(1)

    def moves(down, right):
        return [
            (i * lon_count + j, (i + down) % lat_count * lon_count + (j + right) % lon_count)
            for i in range(lat_count)
            for j in range(lon_count)
        ]

    swap = [(j, j ^ 1) for j in range(lon_count)]
    last = jnp.where(lat == lat_count - 1, 3, 0).reshape(1)
    own, left, below, corner = pack(last, fields, grad_out, region_ids)
    quad3 = lax.ppermute(left, both, moves(0, -1))
    quad0 = lax.ppermute(below, both, moves(1, 0))
    quad1 = lax.ppermute(corner, both, moves(1, -1))
    wide, narrow = ordered_index(bias_index)
    bias_wide, bias_narrow = lookup(wide, narrow, bias_table)
    (
        keep,
        send,
        keep_wide,
        send_wide,
        keep_narrow,
        send_narrow,
        grad0,
        grad1,
        grad2,
        grad3,
    ) = window(core, own, quad0, quad1, quad3, bias_wide, bias_narrow, in_weight, out_weight)
    came_wide = lax.ppermute(send_wide, "lon", swap)
    came_narrow = lax.ppermute(send_narrow, "lon", swap)
    came = lax.ppermute(send, "lon", swap)
    back_left = lax.ppermute(grad3, both, moves(0, 1))
    back_below = lax.ppermute(grad0, both, moves(-1, 0))
    back_corner = lax.ppermute(grad1, both, moves(-1, 1))
    table = scatter(wide, narrow, keep_wide, came_wide, keep_narrow, came_narrow)
    joined = join(keep, came, table)
    chips = [[j for j in range(lon_count) if j % 2 == bit] for bit in range(2)]
    parts = lax.all_to_all(joined, "lon", 0, 0, axis_index_groups=chips)
    parts = lax.all_to_all(fold_lon(parts), "lat", 0, 0)
    parts = lax.all_to_all(fold_lat(parts), "lat", 0, 0)
    grad_in_weight, grad_out_weight, table_keep, table_send = unpack(core, parts)
    table_came = lax.ppermute(table_send, "lon", swap)
    first = jnp.where(core[0] == 0, table_keep, table_came)
    second = jnp.where(core[0] == 0, table_came, table_keep)
    table = jnp.concatenate([first, second], axis=1)[:, :, :HALF_SECTOR]
    grad_bias = jnp.transpose(table, (0, 2, 1)).reshape(2 * HALF_SECTOR, HEADS)
    grad_fields = place(grad_out, grad2, back_left, back_below, back_corner)
    return grad_fields, grad_in_weight, grad_out_weight, grad_bias


def solution(mesh):
    tokens = P(None, "lat", "lon", None)
    in_specs = (tokens, tokens, P(None, "lat", "lon"), P(), P(), P(), P())
    out_specs = (tokens, P("lon", None), P("lon", None), P("lon", None))
    return jax.shard_map(body, mesh=mesh, in_specs=in_specs, out_specs=out_specs, check_vma=False)
```

```python
import functools

import jax
import jax.numpy as jnp
import numpy as np
from jax import lax
from jax.experimental import pallas as pl
from jax.experimental.pallas import tpu as pltpu
from jax.sharding import Mesh
from jax.sharding import PartitionSpec as P

WIDTH = 512
HEADS = 16
HEAD_DIM = 32
TOKENS = 144
QUAD = 36
BIAS_ROWS = 6336
HALF_SECTOR = 198
BLOCKS = 25
FACTOR = HEAD_DIM ** (-0.5)
F32 = jnp.float32
BF16 = jnp.bfloat16
MEGA = 1 << 20


def params(mib=16):
    return pltpu.CompilerParams(vmem_limit_bytes=mib * MEGA)


def whole(count):
    return [pl.BlockSpec(memory_space=pltpu.VMEM)] * count


def scalar():
    return pl.BlockSpec(memory_space=pltpu.SMEM)


def halves(x):
    high = x.astype(BF16)
    low = (x - high.astype(F32)).astype(BF16)
    return high, low


def dot(a, b, dims):
    return lax.dot_general(a, b, (dims, ((), ())), preferred_element_type=F32)


NN = ((1,), (0,))
NT = ((1,), (1,))
TN = ((0,), (0,))


def dot3(a, b, dims):
    ah, al = a
    bh, bl = b
    return dot(ah, bh, dims) + (dot(ah, bl, dims) + dot(al, bh, dims))


def token_order():
    grid = np.arange(TOKENS).reshape(2, 2, 6, 2, 3)
    return np.transpose(grid, (1, 3, 2, 4, 0)).reshape(-1)


def pack_kernel(last, fields, grads, ids, own, left, below, corner):
    lanes = lax.broadcasted_iota(jnp.int32, (2, WIDTH), 1)
    level = lax.broadcasted_iota(jnp.int32, (2, WIDTH), 0)
    bump = last[0]
    plan = (
        (own, 0, 3, 2, None),
        (left, 0, 0, 3, None),
        (below, 6, 3, 0, bump),
        (corner, 6, 0, 1, bump),
    )
    for ref, row0, col0, quadrant, offset in plan:
        label = jnp.zeros((2, WIDTH), jnp.int32)
        for row in range(6):
            for col in range(3):
                spot = row * 6 + col * 2
                ref[spot : spot + 2, :] = fields[row0 + row, col0 + col]
                ref[QUAD + spot : QUAD + spot + 2, :] = grads[row0 + row, col0 + col]
                value = ids[col0 + col, :, row0 + row : row0 + row + 1] + 1
                if offset is not None:
                    value = value + offset
                place = quadrant * QUAD + spot
                label = jnp.where(
                    lanes == level + place, jnp.broadcast_to(value, (2, WIDTH)), label
                )
        total = jnp.sum(label.astype(F32), axis=0, keepdims=True)
        ref[72:80, :] = jnp.broadcast_to(total, (8, WIDTH))


def pack(last, fields, grads, ids):
    shape = jax.ShapeDtypeStruct((80, WIDTH), F32)
    return pl.pallas_call(
        pack_kernel,
        out_shape=[shape] * 4,
        in_specs=[scalar()] + whole(3),
        out_specs=whole(4),
        compiler_params=params(),
        name="pack",
    )(last, fields, grads, ids)


def one_hot(row, lines):
    low = (row & 255).astype(F32).astype(BF16)
    hit = lines == jnp.broadcast_to(low, (256, 128))
    return jnp.where(hit, jnp.ones((256, 128), BF16), jnp.zeros((256, 128), BF16))


def line_numbers():
    return lax.broadcasted_iota(jnp.int32, (256, 128), 0).astype(F32).astype(BF16)


def lookup_kernel(core_ref, index, order, table, bias, wide, narrow, left):
    value = index[...]
    high = (value >> 7).astype(F32).astype(BF16)
    low = (value & 127).astype(F32).astype(BF16)
    move = order[...]

    def moved(part):
        return dot(dot(move, part, NN).astype(BF16), move, NT)

    result = moved(high) * 128.0 + moved(low)
    wide[...] = result[:, :128].astype(jnp.int32)
    tail = jnp.concatenate([result[:, 128:], jnp.zeros((TOKENS, 112), F32)], axis=1)
    for i in range(18):
        spread = pltpu.roll(tail[8 * i : 8 * i + 8, :], 0, 1, stride=16, stride_axis=0)
        narrow[i : i + 1, :] = jnp.sum(spread, axis=0, keepdims=True).astype(jnp.int32)

    first = core_ref[0] == 0
    for block in range(BLOCKS):
        count = min(256, BIAS_ROWS - block * 256)
        top = table[0:8, block * 256 : block * 256 + count]
        bottom = table[8:16, block * 256 : block * 256 + count]
        part = jnp.concatenate(
            [jnp.where(first, bottom, top), jnp.where(first, top, bottom)], axis=0
        )
        if count < 256:
            part = jnp.concatenate([part, jnp.zeros((16, 256 - count), F32)], axis=1)
        left[block * 32 : block * 32 + 16, :], left[block * 32 + 16 : block * 32 + 32, :] = halves(
            part
        )
    lines = line_numbers()
    matrix = left[...]

    def find(rows):
        right = jnp.concatenate([one_hot(row, lines) for row in rows], axis=1)
        found = dot(matrix, right, NN)
        block = jnp.concatenate([row >> 8 for row in rows], axis=1)
        block = jnp.broadcast_to(block, (32, 256))
        total = jnp.zeros((32, 256), F32)
        for b in range(BLOCKS):
            total = jnp.where(block == b, found[b * 32 : b * 32 + 32], total)
        return total[:16] + total[16:]

    def step(i, carry):
        base = pl.multiple_of(i * 8, 8)
        rows = wide[pl.ds(base, 8), :]
        for pair in range(4):
            found = find([rows[2 * pair + j : 2 * pair + j + 1, :] for j in range(2)])
            for j in range(2):
                bias[base + 2 * pair + j, :, 0:128] = found[:, j * 128 : j * 128 + 128]
        return carry

    lax.fori_loop(0, 18, step, 0)
    for pair in range(9):
        found = find([narrow[2 * pair + j : 2 * pair + j + 1, :] for j in range(2)])
        for j in range(16):
            bias[16 * pair + j, :, 128:144] = found[:, 16 * j : 16 * j + 16]


def lookup(core, bias_index, bias_table):
    order = np.zeros((TOKENS, TOKENS), np.float32)
    order[np.arange(TOKENS), token_order()] = 1.0
    return pl.pallas_call(
        lookup_kernel,
        out_shape=[
            jax.ShapeDtypeStruct((TOKENS, HEADS, TOKENS), F32),
            jax.ShapeDtypeStruct((TOKENS, 128), jnp.int32),
            jax.ShapeDtypeStruct((18, 128), jnp.int32),
        ],
        in_specs=[scalar()] + whole(3),
        out_specs=whole(3),
        scratch_shapes=[pltpu.VMEM((BLOCKS * 32, 256), BF16)],
        compiler_params=params(),
        name="lookup",
    )(core, bias_index, jnp.asarray(order, BF16), bias_table.T)


def main_kernel(
    core_ref,
    own,
    quad0,
    quad1,
    quad3,
    bias,
    in_weight,
    out_weight,
    keep,
    send,
    keep_wide,
    send_wide,
    keep_narrow,
    send_narrow,
    grad0,
    grad1,
    grad2,
    grad3,
    tokens,
    cotangent,
    proj,
    gatt,
    gproj,
    att,
    normed_t,
    tails,
):
    core = core_ref[0]
    for slot, quad in enumerate((quad0, quad1, own, quad3)):
        at = slot * QUAD
        tokens[at : at + QUAD, :] = quad[0:QUAD, :]
        cotangent[at : at + QUAD, :] = quad[QUAD : 2 * QUAD, :]
    row = (quad0[72:73, :] + quad1[72:73, :] + own[72:73, :] + quad3[72:73, :])[:, :TOKENS]
    side = lax.broadcasted_iota(jnp.int32, (TOKENS, TOKENS), 0)
    along = lax.broadcasted_iota(jnp.int32, (TOKENS, TOKENS), 1)
    spread = jnp.broadcast_to(row, (TOKENS, TOKENS))
    column = jnp.sum(jnp.where(side == along, spread, 0.0), axis=1, keepdims=True)
    allowed = column == spread

    inputs = tokens[...]
    centered = inputs - jnp.mean(inputs, axis=1, keepdims=True)
    variance = jnp.mean(centered * centered, axis=1, keepdims=True)
    inv_std = lax.rsqrt(variance + 1e-05)
    normed = centered * inv_std
    tokens[...] = normed
    normed_t[...] = normed.T
    halves_normed = halves(normed)
    for part in range(3):
        at = part * WIDTH
        weight = halves(in_weight[:, at : at + WIDTH])
        proj[at : at + WIDTH, :] = dot3(halves_normed, weight, NN).T
    halves_cotangent = halves(cotangent[...])
    gatt[...] = dot3(halves(out_weight[...]), halves_cotangent, NT)

    def one_head(head, slot):
        at = pl.multiple_of(head * HEAD_DIM, HEAD_DIM)
        qh, ql = halves(proj[pl.ds(at, HEAD_DIM), :] * FACTOR)
        kh, kl = halves(proj[pl.ds(at + WIDTH, HEAD_DIM), :])
        vh, vl = halves(proj[pl.ds(at + 2 * WIDTH, HEAD_DIM), :])
        gh, gl = halves(gatt[pl.ds(at, HEAD_DIM), :])

        def stacked(*parts):
            return jnp.concatenate(parts, axis=0)

        scores = dot(stacked(qh, qh, ql), stacked(kh, kl, kh), TN) + bias[:, slot, :]
        scores = jnp.where(allowed, scores, -1000000000.0)
        peak = jnp.max(scores, axis=1, keepdims=True)
        exponent = jnp.exp(scores - peak)
        probs = exponent * (1.0 / jnp.sum(exponent, axis=1, keepdims=True))
        grad_probs = dot(stacked(gh, gh, gl), stacked(vh, vl, vh), TN)
        inner = jnp.sum(grad_probs * probs, axis=1, keepdims=True)
        grad_scores = probs * (grad_probs - inner)
        ph, plow = halves(probs)
        sh, sl = halves(grad_scores)

        def product(high, low, right_high, right_low, dims):
            both = dot(stacked(high, low), right_high, dims)
            return both[:HEAD_DIM] + (both[HEAD_DIM:] + dot(high, right_low, dims))

        att[pl.ds(at, HEAD_DIM), :] = product(vh, vl, ph, plow, NT)
        gproj[pl.ds(at + 2 * WIDTH, HEAD_DIM), :] = product(gh, gl, ph, plow, NN)
        gproj[pl.ds(at, HEAD_DIM), :] = product(kh, kl, sh, sl, NT) * FACTOR
        gproj[pl.ds(at + WIDTH, HEAD_DIM), :] = product(qh, ql, sh, sl, NN)
        return grad_scores

    tails[...] = jnp.zeros_like(tails)
    for slot in range(8):
        grad_scores = one_head((1 - core) * 8 + slot, slot)
        send_wide[:, slot, :] = grad_scores[:, :128]
        tails[:, slot, 0:16] = grad_scores[:, 128:]
        grad_scores = one_head(core * 8 + slot, 8 + slot)
        keep_wide[:, slot, :] = grad_scores[:, :128]
        tails[:, 8 + slot, 0:16] = grad_scores[:, 128:]
    for i in range(18):
        total = tails[8 * i]
        for j in range(1, 8):
            total = total + pltpu.roll(tails[8 * i + j], 16 * j, 1)
        send_narrow[i] = total[0:8]
        keep_narrow[i] = total[8:16]

    for target, bit in ((send, 1 - core), (keep, core)):
        rows = [pl.ds(pl.multiple_of(64 * i + 32 * bit, 32), 32) for i in range(8)]
        left = halves(jnp.concatenate([normed_t[r, :] for r in rows], axis=0))
        for part in range(3):
            at = part * WIDTH
            target[:, at : at + WIDTH] = dot3(left, halves(gproj[at : at + WIDTH, :]), NT)
        left = halves(jnp.concatenate([att[r, :] for r in rows], axis=0))
        target[:, 3 * WIDTH :] = dot3(left, halves_cotangent, NN)

    grad_normed = jnp.zeros((WIDTH, TOKENS), F32)
    for part in range(3):
        at = part * WIDTH
        grad_normed = grad_normed + dot3(
            halves(in_weight[:, at : at + WIDTH]), halves(gproj[at : at + WIDTH, :]), NN
        )
    grad_normed = grad_normed.T
    normed = tokens[...]
    result = inv_std * (
        grad_normed
        - jnp.mean(grad_normed, axis=1, keepdims=True)
        - normed * jnp.mean(grad_normed * normed, axis=1, keepdims=True)
    )
    tokens[...] = result
    for slot, target in enumerate((grad0, grad1, grad2, grad3)):
        target[...] = tokens[slot * QUAD : slot * QUAD + QUAD, :]


def window(core, own, quad0, quad1, quad3, bias, in_weight, out_weight):
    def shape(*dims):
        return jax.ShapeDtypeStruct(dims, F32)

    grad = shape(QUAD, WIDTH)
    return pl.pallas_call(
        main_kernel,
        out_shape=[
            shape(256, 4 * WIDTH),
            shape(256, 4 * WIDTH),
            shape(TOKENS, 8, 128),
            shape(TOKENS, 8, 128),
            shape(18, 8, 128),
            shape(18, 8, 128),
            grad,
            grad,
            grad,
            grad,
        ],
        in_specs=[scalar()] + whole(7),
        out_specs=whole(10),
        scratch_shapes=[
            pltpu.VMEM((TOKENS, WIDTH), F32),
            pltpu.VMEM((TOKENS, WIDTH), F32),
            pltpu.VMEM((3 * WIDTH, TOKENS), F32),
            pltpu.VMEM((WIDTH, TOKENS), F32),
            pltpu.VMEM((3 * WIDTH, TOKENS), F32),
            pltpu.VMEM((WIDTH, TOKENS), F32),
            pltpu.VMEM((WIDTH, TOKENS), F32),
            pltpu.VMEM((TOKENS, HEADS, 128), F32),
        ],
        compiler_params=params(26),
        name="window",
    )(core, own, quad0, quad1, quad3, bias, in_weight, out_weight)


def scatter_kernel(
    wide, narrow, keep_wide, came_wide, keep_narrow, came_narrow, out, total, line
):
    total[...] = jnp.zeros_like(total)
    lines = line_numbers()

    def sides(row, values):
        block = (row >> 8).astype(F32).astype(BF16)
        both = jnp.concatenate(halves(values), axis=0)
        spread = jnp.broadcast_to(block, (16, 128))
        left = jnp.concatenate(
            [jnp.where(spread == float(b), both, jnp.zeros_like(both)) for b in range(BLOCKS)],
            axis=0,
        )
        return left, one_hot(row, lines)

    def add(pieces):
        left = jnp.concatenate([p[0] for p in pieces], axis=1)
        right = jnp.concatenate([p[1] for p in pieces], axis=1)
        total[...] += dot(left, right, NT)

    def step(i, carry):
        base = pl.multiple_of(i * 8, 8)
        rows = wide[pl.ds(base, 8), :]
        for pair in range(4):
            add(
                [
                    sides(rows[j : j + 1, :], keep_wide[base + j] + came_wide[base + j])
                    for j in (2 * pair, 2 * pair + 1)
                ]
            )
        return carry

    lax.fori_loop(0, 18, step, 0)
    for pair in range(9):
        add(
            [
                sides(narrow[j : j + 1, :], keep_narrow[j] + came_narrow[j])
                for j in (2 * pair, 2 * pair + 1)
            ]
        )
    for b in range(BLOCKS):
        line[:, b * 256 : b * 256 + 256] = (
            total[b * 16 : b * 16 + 8, :] + total[b * 16 + 8 : b * 16 + 16, :]
        )
    line[:, BLOCKS * 256 :] = jnp.zeros((8, 256), F32)
    for m in range(32):
        chip, core, half = m // 4, m // 2 % 2, m % 2
        start = m * HALF_SECTOR
        base, shift = start // 128 * 128, start % 128
        piece = line[:, base : base + 512]
        if shift:
            piece = pltpu.roll(piece, 512 - shift, 1)
        out[chip, half * 16 + core * 8 : half * 16 + core * 8 + 8, :] = piece[:, :256]


def scatter(wide, narrow, keep_wide, came_wide, keep_narrow, came_narrow):
    return pl.pallas_call(
        scatter_kernel,
        out_shape=jax.ShapeDtypeStruct((8, 32, 256), F32),
        in_specs=whole(6),
        out_specs=pl.BlockSpec(memory_space=pltpu.VMEM),
        scratch_shapes=[
            pltpu.VMEM((BLOCKS * 16, 256), F32),
            pltpu.VMEM((8, BLOCKS * 256 + 256), F32),
        ],
        compiler_params=params(),
        name="scatter",
    )(wide, narrow, keep_wide, came_wide, keep_narrow, came_narrow)


def join_kernel(keep, came, table, out):
    out[0, :, : 4 * WIDTH] = keep[...] + came[...]
    out[0, :, 4 * WIDTH :] = table[0]


def join(keep, came, table):
    block = pl.BlockSpec((32, 4 * WIDTH), lambda i: (i, 0))
    return pl.pallas_call(
        join_kernel,
        out_shape=jax.ShapeDtypeStruct((8, 32, 2304), F32),
        grid=(8,),
        in_specs=[block, block, pl.BlockSpec((1, 32, 256), lambda i: (i, 0, 0))],
        out_specs=pl.BlockSpec((1, 32, 2304), lambda i: (i, 0, 0)),
        compiler_params=params(),
        name="join",
    )(keep, came, table)


def fold_lon_kernel(parts, out):
    def rows(at):
        total = parts[0, at : at + 8, :]
        for i in range(1, 8):
            total = total + parts[i, at : at + 8, :]
        return total

    for group in range(4):
        total = rows(group * 8)
        for col in range(4):
            if col < 3:
                out[group * 4 + col] = total[:, col * 640 : col * 640 + 640]
            else:
                out[group * 4 + col, :, :384] = total[:, 1920:2304]
                out[group * 4 + col, :, 384:] = jnp.zeros((8, 256), F32)


def fold_lon(parts):
    return pl.pallas_call(
        fold_lon_kernel,
        out_shape=jax.ShapeDtypeStruct((16, 8, 640), F32),
        in_specs=whole(1),
        out_specs=pl.BlockSpec(memory_space=pltpu.VMEM),
        compiler_params=params(),
        name="fold_lon",
    )(parts)


def fold_lat_kernel(parts, out):
    total = parts[0]
    for i in range(1, 16):
        total = total + parts[i]
    for i in range(32):
        out[i] = total


def fold_lat(parts):
    return pl.pallas_call(
        fold_lat_kernel,
        out_shape=jax.ShapeDtypeStruct((32, 8, 640), F32),
        in_specs=whole(1),
        out_specs=pl.BlockSpec(memory_space=pltpu.VMEM),
        compiler_params=params(),
        name="fold_lat",
    )(parts)


def unpack_kernel(core_ref, parts, grad_in, grad_out, grad_bias):
    core = core_ref[0]
    for group in range(4):
        rows = slice(group * 8, group * 8 + 8)
        base = group * 8 + core
        grad_in[rows, 0:640] = parts[base]
        grad_in[rows, 640:1280] = parts[base + 2]
        grad_in[rows, 1280:1536] = parts[base + 4, :, :256]
        grad_out[rows, 0:384] = parts[base + 4, :, 256:]
        grad_out[rows, 384:512] = parts[base + 6, :, :128]
    for other in range(2):
        rows = slice(other * 8, other * 8 + 8)
        for half in range(2):
            piece = parts[(half * 2 + core) * 8 + 6 + other, :, 128:384]
            grad_bias[rows, half * HALF_SECTOR : half * HALF_SECTOR + HALF_SECTOR] = piece[
                :, :HALF_SECTOR
            ]


def unpack(core, parts):
    return pl.pallas_call(
        unpack_kernel,
        out_shape=[
            jax.ShapeDtypeStruct((32, 3 * WIDTH), F32),
            jax.ShapeDtypeStruct((32, WIDTH), F32),
            jax.ShapeDtypeStruct((HEADS, 2 * HALF_SECTOR), F32),
        ],
        in_specs=[scalar()] + whole(1),
        out_specs=whole(3),
        compiler_params=params(),
        name="unpack",
    )(core, parts)


def place_kernel(grad_out, own, left, below, corner, out):
    for ref, row0, col0 in ((own, 0, 3), (left, 0, 0), (below, 6, 3), (corner, 6, 0)):
        for row in range(6):
            for col in range(3):
                spot = row * 6 + col * 2
                out[row0 + row, col0 + col] = (
                    grad_out[row0 + row, col0 + col] + ref[spot : spot + 2, :]
                )


def place(grad_out, own, left, below, corner):
    return pl.pallas_call(
        place_kernel,
        out_shape=jax.ShapeDtypeStruct(grad_out.shape, F32),
        in_specs=whole(5),
        out_specs=pl.BlockSpec(memory_space=pltpu.VMEM),
        compiler_params=params(),
        name="place",
    )(grad_out, own, left, below, corner)


LAT = ("z", "y_lo")
LON = ("x", "y_hi", "core")


def body(fields, grad_out, region_ids, bias_index, bias_table, in_weight, out_weight):
    everything = LAT + LON
    lat = lax.axis_index(LAT)
    core = lax.axis_index("core").reshape(1)

    def moves(down, right):
        return [
            (i * 16 + j, (i + down) % 16 * 16 + (j + right) % 16)
            for i in range(16)
            for j in range(16)
        ]

    swap = [(0, 1), (1, 0)]
    last = jnp.where(lat == 15, 3, 0).reshape(1)
    grad_out = jnp.transpose(grad_out, (1, 2, 0, 3))
    own, left, below, corner = pack(
        last, jnp.transpose(fields, (1, 2, 0, 3)), grad_out, jnp.transpose(region_ids, (2, 0, 1))
    )
    quad3 = lax.ppermute(left, everything, moves(0, -1))
    quad0 = lax.ppermute(below, everything, moves(1, 0))
    quad1 = lax.ppermute(corner, everything, moves(1, -1))
    bias, wide, narrow = lookup(core, bias_index, bias_table)
    (
        keep,
        send,
        keep_wide,
        send_wide,
        keep_narrow,
        send_narrow,
        grad0,
        grad1,
        grad2,
        grad3,
    ) = window(core, own, quad0, quad1, quad3, bias, in_weight, out_weight)
    came_wide = lax.ppermute(send_wide, "core", swap)
    came_narrow = lax.ppermute(send_narrow, "core", swap)
    came = lax.ppermute(send, "core", swap)
    back_left = lax.ppermute(grad3, everything, moves(0, 1))
    back_below = lax.ppermute(grad0, everything, moves(-1, 0))
    back_corner = lax.ppermute(grad1, everything, moves(-1, 1))
    table = scatter(wide, narrow, keep_wide, came_wide, keep_narrow, came_narrow)
    grad_fields = place(grad_out, grad2, back_left, back_below, back_corner)
    joined = join(keep, came, table)
    joined, grad_fields = lax.optimization_barrier((joined, grad_fields))
    parts = lax.all_to_all(joined, ("x", "y_hi"), 0, 0)
    parts = lax.all_to_all(fold_lon(parts), LAT, 0, 0)
    parts = lax.all_to_all(fold_lat(parts), LAT + ("core",), 0, 0)
    grad_in_weight, grad_out_weight, grad_bias = unpack(core, parts)
    return jnp.transpose(grad_fields, (2, 0, 1, 3)), grad_in_weight, grad_out_weight, grad_bias.T


def solution(mesh):
    split = Mesh(mesh.devices.reshape(8, 2, 4, 2, 2), LAT + LON)
    tokens = P(None, LAT, LON, None)
    in_specs = (tokens, tokens, P(None, LAT, LON), P(), P(), P(), P())
    out_specs = (tokens, P(LON, None), P(LON, None), P(LON, None))
    return jax.shard_map(body, mesh=split, in_specs=in_specs, out_specs=out_specs, check_vma=False)
```

```python
import functools

import jax
import jax.numpy as jnp
import numpy as np
from jax import lax
from jax.experimental import pallas as pl
from jax.experimental.pallas import tpu as pltpu
from jax.sharding import Mesh
from jax.sharding import PartitionSpec as P

WIDTH = 512
HEADS = 16
HEAD_DIM = 32
TOKENS = 144
QUAD = 36
BIAS_ROWS = 6336
HALF_SECTOR = 198
BLOCKS = 25
FACTOR = HEAD_DIM ** (-0.5)
F32 = jnp.float32
BF16 = jnp.bfloat16
MEGA = 1 << 20


def params(mib=16):
    return pltpu.CompilerParams(vmem_limit_bytes=mib * MEGA)


def cost(micros):
    return pl.CostEstimate(flops=int(micros * 1e9), bytes_accessed=0, transcendentals=0)


def hbm(count):
    return [pl.BlockSpec(memory_space=pltpu.HBM)] * count


def whole(count):
    return [pl.BlockSpec(memory_space=pltpu.VMEM)] * count


def scalar():
    return pl.BlockSpec(memory_space=pltpu.SMEM)


def halves(x):
    high = x.astype(BF16)
    low = (x - high.astype(F32)).astype(BF16)
    return high, low


def dot(a, b, dims):
    return lax.dot_general(a, b, (dims, ((), ())), preferred_element_type=F32)


NN = ((1,), (0,))
NT = ((1,), (1,))
TN = ((0,), (0,))


def dot3(a, b, dims):
    ah, al = a
    bh, bl = b
    return dot(ah, bh, dims) + (dot(ah, bl, dims) + dot(al, bh, dims))


def token_order():
    grid = np.arange(TOKENS).reshape(2, 2, 6, 2, 3)
    return np.transpose(grid, (1, 3, 2, 4, 0)).reshape(-1)


def pack_kernel(
    last, fields_in, grads_in, ids_in, own, left, below, corner, fields, grads, ids, arrived
):
    copies = [
        pltpu.make_async_copy(source, target, arrived.at[i])
        for i, (source, target) in enumerate(
            ((fields_in, fields), (grads_in, grads), (ids_in, ids))
        )
    ]
    for copy in copies:
        copy.start()
    for copy in copies:
        copy.wait()
    lanes = lax.broadcasted_iota(jnp.int32, (2, WIDTH), 1)
    level = lax.broadcasted_iota(jnp.int32, (2, WIDTH), 0)
    bump = last[0]
    plan = (
        (own, 0, 3, 2, None),
        (left, 0, 0, 3, None),
        (below, 6, 3, 0, bump),
        (corner, 6, 0, 1, bump),
    )
    for ref, row0, col0, quadrant, offset in plan:
        label = jnp.zeros((2, WIDTH), jnp.int32)
        for row in range(6):
            for col in range(3):
                spot = row * 6 + col * 2
                ref[spot : spot + 2, :] = fields[row0 + row, col0 + col]
                ref[QUAD + spot : QUAD + spot + 2, :] = grads[row0 + row, col0 + col]
                value = ids[col0 + col, :, row0 + row : row0 + row + 1] + 1
                if offset is not None:
                    value = value + offset
                place = quadrant * QUAD + spot
                label = jnp.where(
                    lanes == level + place, jnp.broadcast_to(value, (2, WIDTH)), label
                )
        total = jnp.sum(label.astype(F32), axis=0, keepdims=True)
        ref[72:80, :] = jnp.broadcast_to(total, (8, WIDTH))


def pack(last, fields, grads, ids):
    shape = jax.ShapeDtypeStruct((80, WIDTH), F32)
    return pl.pallas_call(
        pack_kernel,
        out_shape=[shape] * 4,
        in_specs=[scalar()] + hbm(3),
        out_specs=whole(4),
        scratch_shapes=[
            pltpu.VMEM(fields.shape, F32),
            pltpu.VMEM(grads.shape, F32),
            pltpu.VMEM(ids.shape, jnp.int32),
            pltpu.SemaphoreType.DMA((3,)),
        ],
        compiler_params=params(8),
        cost_estimate=cost(2),
        name="pack",
    )(last, fields, grads, ids)


def one_hot(row, lines):
    low = (row & 255).astype(F32).astype(BF16)
    hit = lines == jnp.broadcast_to(low, (256, 128))
    return jnp.where(hit, jnp.ones((256, 128), BF16), jnp.zeros((256, 128), BF16))


def line_numbers():
    return lax.broadcasted_iota(jnp.int32, (256, 128), 0).astype(F32).astype(BF16)


def lookup_kernel(
    core_ref,
    index,
    order,
    table,
    in_hbm,
    out_hbm,
    bias,
    wide,
    narrow,
    in_high,
    in_low,
    out_high,
    out_low,
    left,
    in_weight,
    out_weight,
    arrived,
):
    copies = [
        pltpu.make_async_copy(in_hbm, in_weight, arrived.at[0]),
        pltpu.make_async_copy(out_hbm, out_weight, arrived.at[1]),
    ]
    for copy in copies:
        copy.start()
    value = index[...]
    high = (value >> 7).astype(F32).astype(BF16)
    low = (value & 127).astype(F32).astype(BF16)
    move = order[...]

    def moved(part):
        return dot(dot(move, part, NN).astype(BF16), move, NT)

    result = moved(high) * 128.0 + moved(low)
    wide[...] = result[:, :128].astype(jnp.int32)
    tail = jnp.concatenate([result[:, 128:], jnp.zeros((TOKENS, 112), F32)], axis=1)
    for i in range(18):
        spread = pltpu.roll(tail[8 * i : 8 * i + 8, :], 0, 1, stride=16, stride_axis=0)
        narrow[i : i + 1, :] = jnp.sum(spread, axis=0, keepdims=True).astype(jnp.int32)

    first = core_ref[0] == 0
    for block in range(BLOCKS):
        count = min(256, BIAS_ROWS - block * 256)
        top = table[0:8, block * 256 : block * 256 + count]
        bottom = table[8:16, block * 256 : block * 256 + count]
        part = jnp.concatenate(
            [jnp.where(first, bottom, top), jnp.where(first, top, bottom)], axis=0
        )
        if count < 256:
            part = jnp.concatenate([part, jnp.zeros((16, 256 - count), F32)], axis=1)
        left[block * 32 : block * 32 + 16, :], left[block * 32 + 16 : block * 32 + 32, :] = halves(
            part
        )
    lines = line_numbers()
    matrix = left[...]

    def find(rows):
        right = jnp.concatenate([one_hot(row, lines) for row in rows], axis=1)
        found = dot(matrix, right, NN)
        block = jnp.concatenate([row >> 8 for row in rows], axis=1)
        block = jnp.broadcast_to(block, (32, 256))
        total = jnp.zeros((32, 256), F32)
        for b in range(BLOCKS):
            total = jnp.where(block == b, found[b * 32 : b * 32 + 32], total)
        return total[:16] + total[16:]

    def step(i, carry):
        base = pl.multiple_of(i * 8, 8)
        rows = wide[pl.ds(base, 8), :]
        for pair in range(4):
            found = find([rows[2 * pair + j : 2 * pair + j + 1, :] for j in range(2)])
            for j in range(2):
                bias[base + 2 * pair + j, :, 0:128] = found[:, j * 128 : j * 128 + 128]
        return carry

    lax.fori_loop(0, 18, step, 0)
    for pair in range(9):
        found = find([narrow[2 * pair + j : 2 * pair + j + 1, :] for j in range(2)])
        for j in range(16):
            bias[16 * pair + j, :, 128:144] = found[:, 16 * j : 16 * j + 16]
    for copy in copies:
        copy.wait()
    for part in range(3):
        cols = slice(part * WIDTH, part * WIDTH + WIDTH)
        in_high[:, cols], in_low[:, cols] = halves(in_weight[:, cols])
    out_high[...], out_low[...] = halves(out_weight[...])


def lookup(core, bias_index, bias_table, in_weight, out_weight):
    order = np.zeros((TOKENS, TOKENS), np.float32)
    order[np.arange(TOKENS), token_order()] = 1.0
    return pl.pallas_call(
        lookup_kernel,
        out_shape=[
            jax.ShapeDtypeStruct((TOKENS, HEADS, TOKENS), F32),
            jax.ShapeDtypeStruct((TOKENS, 128), jnp.int32),
            jax.ShapeDtypeStruct((18, 128), jnp.int32),
        ]
        + [jax.ShapeDtypeStruct(in_weight.shape, BF16)] * 2
        + [jax.ShapeDtypeStruct(out_weight.shape, BF16)] * 2,
        in_specs=[scalar()] + whole(3) + hbm(2),
        out_specs=whole(7),
        scratch_shapes=[
            pltpu.VMEM((BLOCKS * 32, 256), BF16),
            pltpu.VMEM(in_weight.shape, F32),
            pltpu.VMEM(out_weight.shape, F32),
            pltpu.SemaphoreType.DMA((2,)),
        ],
        compiler_params=params(20),
        cost_estimate=cost(13),
        name="lookup",
    )(core, bias_index, jnp.asarray(order, BF16), bias_table.T, in_weight, out_weight)


def attend_kernel(
    core_ref,
    own,
    quad0,
    quad1,
    quad3,
    bias,
    in_high,
    in_low,
    out_high,
    out_low,
    keep_wide,
    send_wide,
    keep_narrow,
    send_narrow,
    normed_high,
    normed_low,
    att_high,
    att_low,
    gproj_high,
    gproj_low,
    cot_high,
    cot_low,
    normed_out,
    inv_std_out,
    tokens,
    cotangent,
    proj,
    gatt,
    tails,
):
    core = core_ref[0]
    for slot, quad in enumerate((quad0, quad1, own, quad3)):
        at = slot * QUAD
        tokens[at : at + QUAD, :] = quad[0:QUAD, :]
        cotangent[at : at + QUAD, :] = quad[QUAD : 2 * QUAD, :]
    row = (quad0[72:73, :] + quad1[72:73, :] + own[72:73, :] + quad3[72:73, :])[:, :TOKENS]
    side = lax.broadcasted_iota(jnp.int32, (TOKENS, TOKENS), 0)
    along = lax.broadcasted_iota(jnp.int32, (TOKENS, TOKENS), 1)
    spread = jnp.broadcast_to(row, (TOKENS, TOKENS))
    column = jnp.sum(jnp.where(side == along, spread, 0.0), axis=1, keepdims=True)
    allowed = column == spread

    inputs = tokens[...]
    centered = inputs - jnp.mean(inputs, axis=1, keepdims=True)
    variance = jnp.mean(centered * centered, axis=1, keepdims=True)
    inv_std = lax.rsqrt(variance + 1e-05)
    normed = centered * inv_std
    normed_out[...] = normed
    inv_std_out[...] = jnp.broadcast_to(inv_std, (TOKENS, 128))
    normed_high[...], normed_low[...] = halves(normed.T)
    halves_normed = halves(normed)
    for part in range(3):
        cols = slice(part * WIDTH, part * WIDTH + WIDTH)
        proj[cols, :] = dot3(halves_normed, (in_high[:, cols], in_low[:, cols]), NN).T
    halves_cotangent = halves(cotangent[...])
    cot_high[...], cot_low[...] = halves_cotangent
    gatt[...] = dot3((out_high[...], out_low[...]), halves_cotangent, NT)

    def one_head(head, slot):
        at = pl.multiple_of(head * HEAD_DIM, HEAD_DIM)
        qh, ql = halves(proj[pl.ds(at, HEAD_DIM), :] * FACTOR)
        kh, kl = halves(proj[pl.ds(at + WIDTH, HEAD_DIM), :])
        vh, vl = halves(proj[pl.ds(at + 2 * WIDTH, HEAD_DIM), :])
        gh, gl = halves(gatt[pl.ds(at, HEAD_DIM), :])

        def stacked(*parts):
            return jnp.concatenate(parts, axis=0)

        scores = dot(stacked(qh, qh, ql), stacked(kh, kl, kh), TN) + bias[:, slot, :]
        scores = jnp.where(allowed, scores, -1000000000.0)
        peak = jnp.max(scores, axis=1, keepdims=True)
        exponent = jnp.exp(scores - peak)
        probs = exponent * (1.0 / jnp.sum(exponent, axis=1, keepdims=True))
        grad_probs = dot(stacked(gh, gh, gl), stacked(vh, vl, vh), TN)
        inner = jnp.sum(grad_probs * probs, axis=1, keepdims=True)
        grad_scores = probs * (grad_probs - inner)
        ph, plow = halves(probs)
        sh, sl = halves(grad_scores)

        def product(high, low, right_high, right_low, dims):
            both = dot(stacked(high, low), right_high, dims)
            return both[:HEAD_DIM] + (both[HEAD_DIM:] + dot(high, right_low, dims))

        def store(high, low, offset, value):
            rows = pl.ds(at + offset, HEAD_DIM)
            high[rows, :], low[rows, :] = halves(value)

        store(att_high, att_low, 0, product(vh, vl, ph, plow, NT))
        store(gproj_high, gproj_low, 2 * WIDTH, product(gh, gl, ph, plow, NN))
        store(gproj_high, gproj_low, 0, product(kh, kl, sh, sl, NT) * FACTOR)
        store(gproj_high, gproj_low, WIDTH, product(qh, ql, sh, sl, NN))
        return grad_scores

    tails[...] = jnp.zeros_like(tails)
    for slot in range(8):
        grad_scores = one_head((1 - core) * 8 + slot, slot)
        send_wide[:, slot, :] = grad_scores[:, :128]
        tails[:, slot, 0:16] = grad_scores[:, 128:]
        grad_scores = one_head(core * 8 + slot, 8 + slot)
        keep_wide[:, slot, :] = grad_scores[:, :128]
        tails[:, 8 + slot, 0:16] = grad_scores[:, 128:]
    for i in range(18):
        total = tails[8 * i]
        for j in range(1, 8):
            total = total + pltpu.roll(tails[8 * i + j], 16 * j, 1)
        send_narrow[i] = total[0:8]
        keep_narrow[i] = total[8:16]


def shape(*dims, dtype=F32):
    return jax.ShapeDtypeStruct(dims, dtype)


def attend(core, own, quad0, quad1, quad3, bias, *weights):
    thin = shape(WIDTH, TOKENS, dtype=BF16)
    return pl.pallas_call(
        attend_kernel,
        out_shape=[
            shape(TOKENS, 8, 128),
            shape(TOKENS, 8, 128),
            shape(18, 8, 128),
            shape(18, 8, 128),
            thin,
            thin,
            thin,
            thin,
            shape(3 * WIDTH, TOKENS, dtype=BF16),
            shape(3 * WIDTH, TOKENS, dtype=BF16),
            shape(TOKENS, WIDTH, dtype=BF16),
            shape(TOKENS, WIDTH, dtype=BF16),
            shape(TOKENS, WIDTH),
            shape(TOKENS, 128),
        ],
        in_specs=[scalar()] + whole(9),
        out_specs=whole(14),
        scratch_shapes=[
            pltpu.VMEM((TOKENS, WIDTH), F32),
            pltpu.VMEM((TOKENS, WIDTH), F32),
            pltpu.VMEM((3 * WIDTH, TOKENS), F32),
            pltpu.VMEM((WIDTH, TOKENS), F32),
            pltpu.VMEM((TOKENS, HEADS, 128), F32),
        ],
        compiler_params=params(24),
        cost_estimate=cost(10),
        name="attend",
    )(core, own, quad0, quad1, quad3, bias, *weights)


def weights_kernel(
    core_ref,
    normed_high,
    normed_low,
    att_high,
    att_low,
    gproj_high,
    gproj_low,
    cot_high,
    cot_low,
    keep,
    send,
):
    core = core_ref[0]
    for target, bit in ((send, 1 - core), (keep, core)):
        rows = [pl.ds(pl.multiple_of(64 * i + 32 * bit, 32), 32) for i in range(8)]

        def gathered(ref):
            return jnp.concatenate([ref[r, :] for r in rows], axis=0)

        left = (gathered(normed_high), gathered(normed_low))
        for part in range(3):
            cols = slice(part * WIDTH, part * WIDTH + WIDTH)
            target[:, cols] = dot3(left, (gproj_high[cols, :], gproj_low[cols, :]), NT)
        left = (gathered(att_high), gathered(att_low))
        target[:, 3 * WIDTH :] = dot3(left, (cot_high[...], cot_low[...]), NN)


def weights(core, *parts):
    return pl.pallas_call(
        weights_kernel,
        out_shape=[shape(256, 4 * WIDTH)] * 2,
        in_specs=[scalar()] + whole(8),
        out_specs=whole(2),
        compiler_params=params(),
        cost_estimate=cost(3),
        name="weights",
    )(core, *parts)


def inputs_kernel(
    gproj_high,
    gproj_low,
    in_high,
    in_low,
    normed_in,
    inv_std_in,
    grad0,
    grad1,
    grad2,
    grad3,
    tokens,
):
    grad_normed = dot3(
        (in_high[...], in_low[...]), (gproj_high[...], gproj_low[...]), NN
    ).T
    normed = normed_in[...]
    result = inv_std_in[:, 0:1] * (
        grad_normed
        - jnp.mean(grad_normed, axis=1, keepdims=True)
        - normed * jnp.mean(grad_normed * normed, axis=1, keepdims=True)
    )
    tokens[...] = result
    for slot, target in enumerate((grad0, grad1, grad2, grad3)):
        target[...] = tokens[slot * QUAD : slot * QUAD + QUAD, :]


def input_grads(*parts):
    return pl.pallas_call(
        inputs_kernel,
        out_shape=[shape(QUAD, WIDTH)] * 4,
        in_specs=whole(6),
        out_specs=whole(4),
        scratch_shapes=[pltpu.VMEM((TOKENS, WIDTH), F32)],
        compiler_params=params(),
        cost_estimate=cost(3),
        name="input_grads",
    )(*parts)


def scatter_kernel(
    core_ref,
    wide,
    narrow,
    keep_wide,
    came_wide,
    keep_narrow,
    came_narrow,
    keep,
    send,
    total,
    line,
    sectors,
):
    total[...] = jnp.zeros_like(total)
    lines = line_numbers()

    def sides(row, values):
        block = (row >> 8).astype(F32).astype(BF16)
        both = jnp.concatenate(halves(values), axis=0)
        spread = jnp.broadcast_to(block, (16, 128))
        left = jnp.concatenate(
            [jnp.where(spread == float(b), both, jnp.zeros_like(both)) for b in range(BLOCKS)],
            axis=0,
        )
        return left, one_hot(row, lines)

    def add(pieces):
        left = jnp.concatenate([p[0] for p in pieces], axis=1)
        right = jnp.concatenate([p[1] for p in pieces], axis=1)
        total[...] += dot(left, right, NT)

    def step(i, carry):
        base = pl.multiple_of(i * 8, 8)
        rows = wide[pl.ds(base, 8), :]
        for pair in range(4):
            add(
                [
                    sides(rows[j : j + 1, :], keep_wide[base + j] + came_wide[base + j])
                    for j in (2 * pair, 2 * pair + 1)
                ]
            )
        return carry

    lax.fori_loop(0, 18, step, 0)
    for pair in range(9):
        add(
            [
                sides(narrow[j : j + 1, :], keep_narrow[j] + came_narrow[j])
                for j in (2 * pair, 2 * pair + 1)
            ]
        )
    for b in range(BLOCKS):
        line[:, b * 256 : b * 256 + 256] = (
            total[b * 16 : b * 16 + 8, :] + total[b * 16 + 8 : b * 16 + 16, :]
        )
    line[:, BLOCKS * 256 :] = jnp.zeros((8, 256), F32)
    for m in range(32):
        chip, core, half = m // 4, m // 2 % 2, m % 2
        start = m * HALF_SECTOR
        base, shift = start // 128 * 128, start % 128
        piece = line[:, base : base + 512]
        if shift:
            piece = pltpu.roll(piece, 512 - shift, 1)
        sectors[core, chip, half * 8 : half * 8 + 8, :] = piece[:, :256]
    keep[...] = sectors[core_ref[0]]
    send[...] = sectors[1 - core_ref[0]]


def scatter(core, wide, narrow, keep_wide, came_wide, keep_narrow, came_narrow):
    return pl.pallas_call(
        scatter_kernel,
        out_shape=[shape(8, 16, 256)] * 2,
        in_specs=[scalar()] + whole(6),
        out_specs=whole(2),
        scratch_shapes=[
            pltpu.VMEM((BLOCKS * 16, 256), F32),
            pltpu.VMEM((8, BLOCKS * 256 + 256), F32),
            pltpu.VMEM((2, 8, 16, 256), F32),
        ],
        compiler_params=params(),
        cost_estimate=cost(9),
        name="scatter",
    )(core, wide, narrow, keep_wide, came_wide, keep_narrow, came_narrow)


SIZE_A, SIZE_C = 384, 256


def split_kernel(bits, keep, came, own, send_a, send_b, send_c):
    odd, low = bits[0], bits[1]

    def columns(base, size, bit):
        cols = pl.ds(pl.multiple_of(base + size * bit, 128), size)
        return keep[:, cols] + came[:, cols]

    own[:, 0:384] = columns(0, SIZE_A, odd)
    own[:, 384:768] = columns(768, SIZE_A, 1 - odd)
    own[:, 768:1024] = columns(1536, SIZE_C, low)
    send_a[...] = columns(0, SIZE_A, 1 - odd)
    send_b[...] = columns(768, SIZE_A, odd)
    send_c[...] = columns(1536, SIZE_C, 1 - low)


def split(bits, keep, came):
    return pl.pallas_call(
        split_kernel,
        out_shape=[shape(256, 1024), shape(256, SIZE_A), shape(256, SIZE_A), shape(256, SIZE_C)],
        in_specs=[scalar()] + whole(2),
        out_specs=whole(4),
        compiler_params=params(),
        cost_estimate=cost(1),
        name="split",
    )(bits, keep, came)


def join_kernel(core_ref, own, came_a, came_b, came_c, table_keep, table_came, out):
    for i in range(8):
        rows = slice(i * 32, i * 32 + 32)
        out[i, :, 0:384] = own[rows, 0:384] + came_a[rows, :]
        out[i, :, 384:768] = own[rows, 384:768] + came_b[rows, :]
        out[i, :, 768:1024] = own[rows, 768:1024] + came_c[rows, :]
    first = core_ref[0] == 0
    mine, other = table_keep[...], table_came[...]
    out[:, 0:16, 1024:] = jnp.where(first, mine, other)
    out[:, 16:32, 1024:] = jnp.where(first, other, mine)


def join(core, *parts):
    return pl.pallas_call(
        join_kernel,
        out_shape=shape(8, 32, 1280),
        in_specs=[scalar()] + whole(6),
        out_specs=pl.BlockSpec(memory_space=pltpu.VMEM),
        compiler_params=params(),
        cost_estimate=cost(1),
        name="join",
    )(core, *parts)


def fold_lon_kernel(parts, out, total):
    value = parts[0]
    for i in range(1, 8):
        value = value + parts[i]
    total[...] = value
    for p in range(16):
        z, y = p // 2, p % 2
        rank = (z // 2) * 2 + y
        out[p, :, 0:768] = total[4 * rank : 4 * rank + 4, 0:768]
        out[p, :, 768:1024] = total[4 * z : 4 * z + 4, 768:1024]
        out[p, :, 1024:1152] = total[4 * z : 4 * z + 4, 1024 + 128 * y : 1152 + 128 * y]


def fold_lon(parts):
    return pl.pallas_call(
        fold_lon_kernel,
        out_shape=shape(16, 4, 1152),
        in_specs=whole(1),
        out_specs=pl.BlockSpec(memory_space=pltpu.VMEM),
        scratch_shapes=[pltpu.VMEM((32, 1280), F32)],
        compiler_params=params(),
        name="fold_lon",
    )(parts)


def fold_lat_kernel(bits, parts, out):
    odd, low = bits[0], bits[1]

    def summed(sources, cols):
        total = parts[sources[0], :, cols]
        for source in sources[1:]:
            total = total + parts[source, :, cols]
        return total

    same_z = [(2 * k + odd) * 2 + y for k in range(4) for y in range(2)]
    same_y = [2 * z + low for z in range(8)]
    total = jnp.concatenate(
        [
            summed(same_z, slice(0, 768)),
            summed(same_y, slice(768, 1024)),
            summed(list(range(16)), slice(1024, 1152)),
        ],
        axis=1,
    )
    for i in range(16):
        out[i] = total


def fold_lat(bits, parts):
    return pl.pallas_call(
        fold_lat_kernel,
        out_shape=shape(16, 4, 1152),
        in_specs=[scalar()] + whole(1),
        out_specs=pl.BlockSpec(memory_space=pltpu.VMEM),
        compiler_params=params(),
        name="fold_lat",
    )(bits, parts)


def unpack_kernel(parts, grad_in, grad_out, grad_bias, table):
    for p in range(16):
        z, y = p // 2, p % 2
        odd = z % 2
        rank = (z // 2) * 2 + y
        rows = slice(4 * rank, 4 * rank + 4)
        grad_in[rows, 384 * odd : 384 * odd + 384] = parts[p, :, 0:384]
        start = 768 + 384 * (1 - odd)
        grad_in[rows, start : start + 384] = parts[p, :, 384:768]
        rows = slice(4 * z, 4 * z + 4)
        grad_out[rows, 256 * y : 256 * y + 256] = parts[p, :, 768:1024]
        table[rows, 128 * y : 128 * y + 128] = parts[p, :, 1024:1152]
    for core in range(2):
        for half in range(2):
            base = core * 16 + half * 8
            grad_bias[core * 8 : core * 8 + 8, half * HALF_SECTOR : (half + 1) * HALF_SECTOR] = (
                table[base : base + 8, :HALF_SECTOR]
            )


def unpack(parts):
    return pl.pallas_call(
        unpack_kernel,
        out_shape=[shape(32, 3 * WIDTH), shape(32, WIDTH), shape(HEADS, 2 * HALF_SECTOR)],
        in_specs=whole(1),
        out_specs=whole(3),
        scratch_shapes=[pltpu.VMEM((32, 256), F32)],
        compiler_params=params(),
        name="unpack",
    )(parts)


def place_kernel(grad_out, own, left, below, corner, out):
    for ref, row0, col0 in ((own, 0, 3), (left, 0, 0), (below, 6, 3), (corner, 6, 0)):
        for row in range(6):
            for col in range(3):
                spot = row * 6 + col * 2
                out[row0 + row, col0 + col] = (
                    grad_out[row0 + row, col0 + col] + ref[spot : spot + 2, :]
                )


def place(grad_out, own, left, below, corner):
    return pl.pallas_call(
        place_kernel,
        out_shape=jax.ShapeDtypeStruct(grad_out.shape, F32),
        in_specs=whole(5),
        out_specs=pl.BlockSpec(memory_space=pltpu.VMEM),
        compiler_params=params(),
        name="place",
    )(grad_out, own, left, below, corner)


LAT = ("z", "y_lo")
LON = ("x", "y_hi", "core")


def body(fields, grad_out, region_ids, bias_index, bias_table, in_weight, out_weight):
    everything = LAT + LON
    lat = lax.axis_index(LAT)
    core = lax.axis_index("core").reshape(1)
    bits = jnp.stack([lax.rem(lax.axis_index("z"), 2), lax.axis_index("y_lo")])

    def moves(down, right):
        return [
            (i * 16 + j, (i + down) % 16 * 16 + (j + right) % 16)
            for i in range(16)
            for j in range(16)
        ]

    swap = [(0, 1), (1, 0)]
    last = jnp.where(lat == 15, 3, 0).reshape(1)
    grad_out = jnp.transpose(grad_out, (1, 2, 0, 3))
    own, left, below, corner = pack(
        last, jnp.transpose(fields, (1, 2, 0, 3)), grad_out, jnp.transpose(region_ids, (2, 0, 1))
    )
    quad3 = lax.ppermute(left, everything, moves(0, -1))
    quad0 = lax.ppermute(below, everything, moves(1, 0))
    quad1 = lax.ppermute(corner, everything, moves(1, -1))
    bias, wide, narrow, *halved = lookup(core, bias_index, bias_table, in_weight, out_weight)
    (
        keep_wide,
        send_wide,
        keep_narrow,
        send_narrow,
        normed_high,
        normed_low,
        att_high,
        att_low,
        gproj_high,
        gproj_low,
        cot_high,
        cot_low,
        normed,
        inv_std,
    ) = attend(core, own, quad0, quad1, quad3, bias, *halved)
    came_wide = lax.ppermute(send_wide, "core", swap)
    came_narrow = lax.ppermute(send_narrow, "core", swap)
    keep, send = weights(
        core,
        normed_high,
        normed_low,
        att_high,
        att_low,
        gproj_high,
        gproj_low,
        cot_high,
        cot_low,
    )
    came = lax.ppermute(send, "core", swap)
    normed, send = lax.optimization_barrier((normed, send))
    grad0, grad1, grad2, grad3 = input_grads(
        gproj_high, gproj_low, halved[0], halved[1], normed, inv_std
    )
    back_left = lax.ppermute(grad3, everything, moves(0, 1))
    back_below = lax.ppermute(grad0, everything, moves(-1, 0))
    back_corner = lax.ppermute(grad1, everything, moves(-1, 1))
    keep, grad2 = lax.optimization_barrier((keep, grad2))
    part, send_a, send_b, send_c = split(bits, keep, came)
    came_a = lax.ppermute(send_a, "z", [(i, i ^ 1) for i in range(8)])
    came_b = lax.ppermute(send_b, "z", [(i, ((i + 1) % 8 ^ 1) + 7 & 7) for i in range(8)])
    came_c = lax.ppermute(send_c, "y_lo", swap)
    wide, part = lax.optimization_barrier((wide, part))
    table_keep, table_send = scatter(
        core, wide, narrow, keep_wide, came_wide, keep_narrow, came_narrow
    )
    table_came = lax.ppermute(table_send, "core", swap)
    grad2, table_send = lax.optimization_barrier((grad2, table_send))
    grad_fields = place(grad_out, grad2, back_left, back_below, back_corner)
    part, grad_fields = lax.optimization_barrier((part, grad_fields))
    joined = join(core, part, came_a, came_b, came_c, table_keep, table_came)
    parts = lax.all_to_all(joined, ("x", "y_hi"), 0, 0)
    parts = lax.all_to_all(fold_lon(parts), LAT, 0, 0)
    parts = lax.all_to_all(fold_lat(bits, parts), LAT, 0, 0)
    grad_in_weight, grad_out_weight, grad_bias = unpack(parts)
    return jnp.transpose(grad_fields, (2, 0, 1, 3)), grad_in_weight, grad_out_weight, grad_bias.T


def solution(mesh):
    split = Mesh(mesh.devices.reshape(8, 2, 4, 2, 2), LAT + LON)
    tokens = P(None, LAT, LON, None)
    in_specs = (tokens, tokens, P(None, LAT, LON), P(), P(), P(), P())
    out_specs = (tokens, P(LON, None), P(LON, None), P(LON, None))
    return jax.shard_map(body, mesh=split, in_specs=in_specs, out_specs=out_specs, check_vma=False)
```

```python
import jax
import jax.numpy as jnp
from jax import lax
from jax.experimental import pallas as pl
from jax.experimental.pallas import tpu as pltpu
from jax.sharding import Mesh
from jax.sharding import PartitionSpec as P

WIDTH = 512
HEADS = 16
HEAD_DIM = 32
TOKENS = 144
QUAD = 36
BIAS_ROWS = 6336
HALF_SECTOR = 198
BLOCKS = 25
PACK_MIB = 4
ROWS = 162
FACTOR = HEAD_DIM ** (-0.5)
F32 = jnp.float32
BF16 = jnp.bfloat16
MEGA = 1 << 20


def params(mib=8):
    return pltpu.CompilerParams(vmem_limit_bytes=mib * MEGA)


def cost(micros):
    return pl.CostEstimate(flops=int(micros * 1e9), bytes_accessed=0, transcendentals=0)


def whole(count):
    return [pl.BlockSpec(memory_space=pltpu.VMEM)] * count


def scalar():
    return pl.BlockSpec(memory_space=pltpu.SMEM)


def halves(x):
    high = x.astype(BF16)
    low = (x - high.astype(F32)).astype(BF16)
    return high, low


def dot(a, b, dims):
    return lax.dot_general(a, b, (dims, ((), ())), preferred_element_type=F32)


NN = ((1,), (0,))
NT = ((1,), (1,))
TN = ((0,), (0,))


def dot3(a, b, dims):
    ah, al = a
    bh, bl = b
    return dot(ah, bh, dims) + (dot(ah, bl, dims) + dot(al, bh, dims))


def token_order():
    place = lax.broadcasted_iota(jnp.int32, (TOKENS, TOKENS), 0)
    token = lax.broadcasted_iota(jnp.int32, (TOKENS, TOKENS), 1)

    def steps(value, size, count):
        total = jnp.zeros_like(value)
        for i in range(1, count):
            total = total + jnp.where(value >= i * size, 1, 0)
        return total

    quad = steps(place, QUAD, 4)
    rest = place - QUAD * quad
    row = steps(rest, 6, 6)
    rest = rest - 6 * row
    col = steps(rest, 2, 3)
    level = rest - 2 * col
    row_half = steps(quad, 2, 2)
    col_half = quad - 2 * row_half
    source = level * 72 + (6 * row_half + row) * 6 + 3 * col_half + col
    return jnp.where(source == token, 1.0, 0.0).astype(BF16)


def pack_kernel(last, fields, grads, ids, own, left, below, corner):
    lanes = lax.broadcasted_iota(jnp.int32, (2, WIDTH), 1)
    level = lax.broadcasted_iota(jnp.int32, (2, WIDTH), 0)
    bump = last[0]
    plan = (
        (own, 0, 3, 2, None),
        (left, 0, 0, 3, None),
        (below, 6, 3, 0, bump),
        (corner, 6, 0, 1, bump),
    )
    for ref, row0, col0, quadrant, offset in plan:
        label = jnp.zeros((2, WIDTH), jnp.int32)
        for row in range(6):
            for col in range(3):
                spot = row * 6 + col * 2
                ref[spot : spot + 2, :] = fields[row0 + row, col0 + col]
                ref[QUAD + spot : QUAD + spot + 2, :] = grads[row0 + row, col0 + col]
                value = ids[col0 + col, :, row0 + row : row0 + row + 1] + 1
                if offset is not None:
                    value = value + offset
                place = quadrant * QUAD + spot
                label = jnp.where(
                    lanes == level + place, jnp.broadcast_to(value, (2, WIDTH)), label
                )
        total = jnp.sum(label.astype(F32), axis=0, keepdims=True)
        ref[72:80, :] = jnp.broadcast_to(total, (8, WIDTH))


def pack(last, fields, grads, ids):
    shape = jax.ShapeDtypeStruct((80, WIDTH), F32)
    return pl.pallas_call(
        pack_kernel,
        out_shape=[shape] * 4,
        in_specs=[scalar()] + whole(3),
        out_specs=whole(4),
        compiler_params=params(PACK_MIB),
        cost_estimate=cost(1),
        name="pack",
    )(last, fields, grads, ids)


def one_hot(row, lines):
    low = (row & 255).astype(F32).astype(BF16)
    hit = lines == jnp.broadcast_to(low, (256, 128))
    return jnp.where(hit, jnp.ones((256, 128), BF16), jnp.zeros((256, 128), BF16))


def line_numbers():
    return lax.broadcasted_iota(jnp.int32, (256, 128), 0).astype(F32).astype(BF16)


def lookup_kernel(core_ref, index, table, bias, places, left):
    value = index[...]
    high = (value >> 7).astype(F32).astype(BF16)
    low = (value & 127).astype(F32).astype(BF16)
    move = token_order()

    def moved(part):
        return dot(dot(move, part, NN).astype(BF16), move, NT)

    result = moved(high) * 128.0 + moved(low)
    places[0:TOKENS, :] = result[:, :128].astype(jnp.int32)
    tail = jnp.concatenate([result[:, 128:], jnp.zeros((TOKENS, 112), F32)], axis=1)
    for i in range(18):
        spread = pltpu.roll(tail[8 * i : 8 * i + 8, :], 0, 1, stride=16, stride_axis=0)
        places[TOKENS + i : TOKENS + i + 1, :] = jnp.sum(spread, axis=0, keepdims=True).astype(jnp.int32)

    first = core_ref[0] == 0
    for block in range(BLOCKS):
        count = min(256, BIAS_ROWS - block * 256)
        top = table[0:8, block * 256 : block * 256 + count]
        bottom = table[8:16, block * 256 : block * 256 + count]
        part = jnp.concatenate(
            [jnp.where(first, bottom, top), jnp.where(first, top, bottom)], axis=0
        )
        if count < 256:
            part = jnp.concatenate([part, jnp.zeros((16, 256 - count), F32)], axis=1)
        left[block * 32 : block * 32 + 16, :], left[block * 32 + 16 : block * 32 + 32, :] = halves(
            part
        )
    lines = line_numbers()
    matrix = left[...]

    def find(rows):
        right = jnp.concatenate([one_hot(row, lines) for row in rows], axis=1)
        found = dot(matrix, right, NN)
        block = jnp.concatenate([row >> 8 for row in rows], axis=1)
        block = jnp.broadcast_to(block, (32, 256))
        total = jnp.zeros((32, 256), F32)
        for b in range(BLOCKS):
            total = jnp.where(block == b, found[b * 32 : b * 32 + 32], total)
        return total[:16] + total[16:]

    def step(i, carry):
        base = pl.multiple_of(i * 8, 8)
        rows = places[pl.ds(base, 8), :]
        for pair in range(4):
            found = find([rows[2 * pair + j : 2 * pair + j + 1, :] for j in range(2)])
            for j in range(2):
                bias[base + 2 * pair + j, :, 0:128] = found[:, j * 128 : j * 128 + 128]
        return carry

    lax.fori_loop(0, 18, step, 0)
    for pair in range(9):
        at = TOKENS + 2 * pair
        found = find([places[at + j : at + j + 1, :] for j in range(2)])
        for j in range(16):
            bias[16 * pair + j, :, 128:144] = found[:, 16 * j : 16 * j + 16]


def lookup(core, bias_index, bias_table):
    return pl.pallas_call(
        lookup_kernel,
        out_shape=[
            jax.ShapeDtypeStruct((TOKENS, HEADS, TOKENS), F32),
            jax.ShapeDtypeStruct((ROWS, 128), jnp.int32),
        ],
        in_specs=[scalar()] + whole(2),
        out_specs=whole(2),
        scratch_shapes=[pltpu.VMEM((BLOCKS * 32, 256), BF16)],
        compiler_params=params(6),
        cost_estimate=cost(13),
        name="lookup",
    )(core, bias_index, bias_table.T)


def main_kernel(
    core_ref,
    own,
    quad0,
    quad1,
    quad3,
    bias,
    in_weight,
    out_weight,
    keep,
    send,
    keep_scores,
    send_scores,
    grad0,
    grad1,
    grad2,
    grad3,
    tokens,
    cotangent,
    proj,
    gatt,
    gproj,
    att,
    normed_t,
    tails,
):
    core = core_ref[0]
    for slot, quad in enumerate((quad0, quad1, own, quad3)):
        at = slot * QUAD
        tokens[at : at + QUAD, :] = quad[0:QUAD, :]
        cotangent[at : at + QUAD, :] = quad[QUAD : 2 * QUAD, :]
    row = (quad0[72:73, :] + quad1[72:73, :] + own[72:73, :] + quad3[72:73, :])[:, :TOKENS]
    side = lax.broadcasted_iota(jnp.int32, (TOKENS, TOKENS), 0)
    along = lax.broadcasted_iota(jnp.int32, (TOKENS, TOKENS), 1)
    spread = jnp.broadcast_to(row, (TOKENS, TOKENS))
    column = jnp.sum(jnp.where(side == along, spread, 0.0), axis=1, keepdims=True)
    allowed = column == spread

    inputs = tokens[...]
    centered = inputs - jnp.mean(inputs, axis=1, keepdims=True)
    variance = jnp.mean(centered * centered, axis=1, keepdims=True)
    inv_std = lax.rsqrt(variance + 1e-05)
    normed = centered * inv_std
    tokens[...] = normed
    normed_t[...] = normed.T
    halves_normed = halves(normed)
    for part in range(3):
        at = part * WIDTH
        weight = halves(in_weight[:, at : at + WIDTH])
        proj[at : at + WIDTH, :] = dot3(halves_normed, weight, NN).T
    halves_cotangent = halves(cotangent[...])
    gatt[...] = dot3(halves(out_weight[...]), halves_cotangent, NT)

    def one_head(head, slot):
        at = pl.multiple_of(head * HEAD_DIM, HEAD_DIM)
        qh, ql = halves(proj[pl.ds(at, HEAD_DIM), :] * FACTOR)
        kh, kl = halves(proj[pl.ds(at + WIDTH, HEAD_DIM), :])
        vh, vl = halves(proj[pl.ds(at + 2 * WIDTH, HEAD_DIM), :])
        gh, gl = halves(gatt[pl.ds(at, HEAD_DIM), :])

        def stacked(*parts):
            return jnp.concatenate(parts, axis=0)

        scores = dot(stacked(qh, qh, ql), stacked(kh, kl, kh), TN) + bias[:, slot, :]
        scores = jnp.where(allowed, scores, -1000000000.0)
        peak = jnp.max(scores, axis=1, keepdims=True)
        exponent = jnp.exp(scores - peak)
        probs = exponent * (1.0 / jnp.sum(exponent, axis=1, keepdims=True))
        grad_probs = dot(stacked(gh, gh, gl), stacked(vh, vl, vh), TN)
        inner = jnp.sum(grad_probs * probs, axis=1, keepdims=True)
        grad_scores = probs * (grad_probs - inner)
        ph, plow = halves(probs)
        sh, sl = halves(grad_scores)

        def product(high, low, right_high, right_low, dims):
            both = dot(stacked(high, low), right_high, dims)
            return both[:HEAD_DIM] + (both[HEAD_DIM:] + dot(high, right_low, dims))

        att[pl.ds(at, HEAD_DIM), :] = product(vh, vl, ph, plow, NT)
        gproj[pl.ds(at + 2 * WIDTH, HEAD_DIM), :] = product(gh, gl, ph, plow, NN)
        gproj[pl.ds(at, HEAD_DIM), :] = product(kh, kl, sh, sl, NT) * FACTOR
        gproj[pl.ds(at + WIDTH, HEAD_DIM), :] = product(qh, ql, sh, sl, NN)
        return grad_scores

    tails[...] = jnp.zeros_like(tails)
    for slot in range(8):
        grad_scores = one_head((1 - core) * 8 + slot, slot)
        send_scores[0:TOKENS, slot, :] = grad_scores[:, :128]
        tails[:, slot, 0:16] = grad_scores[:, 128:]
        grad_scores = one_head(core * 8 + slot, 8 + slot)
        keep_scores[0:TOKENS, slot, :] = grad_scores[:, :128]
        tails[:, 8 + slot, 0:16] = grad_scores[:, 128:]
    for i in range(18):
        total = tails[8 * i]
        for j in range(1, 8):
            total = total + pltpu.roll(tails[8 * i + j], 16 * j, 1)
        send_scores[TOKENS + i] = total[0:8]
        keep_scores[TOKENS + i] = total[8:16]

    for target, bit in ((send, 1 - core), (keep, core)):
        rows = [pl.ds(pl.multiple_of(64 * i + 32 * bit, 32), 32) for i in range(8)]
        left = halves(jnp.concatenate([normed_t[r, :] for r in rows], axis=0))
        for part in range(3):
            at = part * WIDTH
            target[:, at : at + WIDTH] = dot3(left, halves(gproj[at : at + WIDTH, :]), NT)
        left = halves(jnp.concatenate([att[r, :] for r in rows], axis=0))
        target[:, 3 * WIDTH :] = dot3(left, halves_cotangent, NN)

    grad_normed = jnp.zeros((WIDTH, TOKENS), F32)
    for part in range(3):
        at = part * WIDTH
        grad_normed = grad_normed + dot3(
            halves(in_weight[:, at : at + WIDTH]), halves(gproj[at : at + WIDTH, :]), NN
        )
    grad_normed = grad_normed.T
    normed = tokens[...]
    result = inv_std * (
        grad_normed
        - jnp.mean(grad_normed, axis=1, keepdims=True)
        - normed * jnp.mean(grad_normed * normed, axis=1, keepdims=True)
    )
    tokens[...] = result
    for slot, target in enumerate((grad0, grad1, grad2, grad3)):
        target[...] = tokens[slot * QUAD : slot * QUAD + QUAD, :]


def shape(*dims):
    return jax.ShapeDtypeStruct(dims, F32)


def window(core, own, quad0, quad1, quad3, bias, in_weight, out_weight):
    grad = shape(QUAD, WIDTH)
    return pl.pallas_call(
        main_kernel,
        out_shape=[
            shape(256, 4 * WIDTH),
            shape(256, 4 * WIDTH),
            shape(ROWS, 8, 128),
            shape(ROWS, 8, 128),
            grad,
            grad,
            grad,
            grad,
        ],
        in_specs=[scalar()] + whole(7),
        out_specs=whole(8),
        scratch_shapes=[
            pltpu.VMEM((TOKENS, WIDTH), F32),
            pltpu.VMEM((TOKENS, WIDTH), F32),
            pltpu.VMEM((3 * WIDTH, TOKENS), F32),
            pltpu.VMEM((WIDTH, TOKENS), F32),
            pltpu.VMEM((3 * WIDTH, TOKENS), F32),
            pltpu.VMEM((WIDTH, TOKENS), F32),
            pltpu.VMEM((WIDTH, TOKENS), F32),
            pltpu.VMEM((TOKENS, HEADS, 128), F32),
        ],
        compiler_params=params(14),
        cost_estimate=cost(14),
        name="window",
    )(core, own, quad0, quad1, quad3, bias, in_weight, out_weight)


def add_pairs(places, keep, came, total, first, last):
    lines = line_numbers()

    def sides(row, values):
        block = (row >> 8).astype(F32).astype(BF16)
        both = jnp.concatenate(halves(values), axis=0)
        spread = jnp.broadcast_to(block, (16, 128))
        left = jnp.concatenate(
            [jnp.where(spread == float(b), both, jnp.zeros_like(both)) for b in range(BLOCKS)],
            axis=0,
        )
        return left, one_hot(row, lines)

    def add(rows, base, pair):
        pieces = [
            sides(rows[j : j + 1, :], keep[base + j] + came[base + j])
            for j in (2 * pair, 2 * pair + 1)
        ]
        left = jnp.concatenate([p[0] for p in pieces], axis=1)
        right = jnp.concatenate([p[1] for p in pieces], axis=1)
        total[...] += dot(left, right, NT)

    def step(i, carry):
        base = pl.multiple_of(i * 8, 8)
        rows = places[pl.ds(base, 8), :]
        for pair in range(4):
            add(rows, base, pair)
        return carry

    lax.fori_loop(first // 8, last // 8, step, 0)
    if last % 8:
        base = last // 8 * 8
        rows = places[base:last, :]
        for pair in range(last % 8 // 2):
            add(rows, base, pair)


def scatter_start_kernel(places, keep, came, total):
    total[...] = jnp.zeros_like(total)
    add_pairs(places, keep, came, total, 0, 80)


def scatter_start(places, keep, came):
    return pl.pallas_call(
        scatter_start_kernel,
        out_shape=shape(BLOCKS * 16, 256),
        in_specs=whole(3),
        out_specs=pl.BlockSpec(memory_space=pltpu.VMEM),
        compiler_params=params(6),
        cost_estimate=cost(4.2),
        name="scatter_start",
    )(places, keep, came)


def scatter_end_kernel(core_ref, places, keep, came, start, mine, other, total, line, sectors):
    total[...] = start[...]
    add_pairs(places, keep, came, total, 80, ROWS)
    for b in range(BLOCKS):
        line[:, b * 256 : b * 256 + 256] = (
            total[b * 16 : b * 16 + 8, :] + total[b * 16 + 8 : b * 16 + 16, :]
        )
    line[:, BLOCKS * 256 :] = jnp.zeros((8, 256), F32)
    for m in range(32):
        chip, core, half = m // 4, m // 2 % 2, m % 2
        start_at = m * HALF_SECTOR
        base, shift = start_at // 128 * 128, start_at % 128
        piece = line[:, base : base + 512]
        if shift:
            piece = pltpu.roll(piece, 512 - shift, 1)
        sectors[core, chip, half * 8 : half * 8 + 8, :] = piece[:, :256]
    mine[...] = sectors[core_ref[0]]
    other[...] = sectors[1 - core_ref[0]]


def scatter_end(core, places, keep, came, start):
    return pl.pallas_call(
        scatter_end_kernel,
        out_shape=[shape(8, 16, 256)] * 2,
        in_specs=[scalar()] + whole(4),
        out_specs=whole(2),
        scratch_shapes=[
            pltpu.VMEM((BLOCKS * 16, 256), F32),
            pltpu.VMEM((8, BLOCKS * 256 + 256), F32),
            pltpu.VMEM((2, 8, 16, 256), F32),
        ],
        compiler_params=params(6),
        cost_estimate=cost(4.6),
        name="scatter_end",
    )(core, places, keep, came, start)


SIZE_A, SIZE_C = 384, 256


def split_kernel(bits, keep, came, own, send_a, send_b, send_c):
    def columns(base, size, bit):
        cols = slice(base + size * bit, base + size * bit + size)
        return keep[:, cols] + came[:, cols]

    for bit in range(2):

        @pl.when(bits[0] == bit)
        def _():
            own[:, 0:384] = columns(0, SIZE_A, bit)
            own[:, 384:768] = columns(768, SIZE_A, 1 - bit)
            send_a[...] = columns(0, SIZE_A, 1 - bit)
            send_b[...] = columns(768, SIZE_A, bit)

        @pl.when(bits[1] == bit)
        def _():
            own[:, 768:1024] = columns(1536, SIZE_C, bit)
            send_c[...] = columns(1536, SIZE_C, 1 - bit)


def split(bits, keep, came):
    return pl.pallas_call(
        split_kernel,
        out_shape=[shape(256, 1024), shape(256, SIZE_A), shape(256, SIZE_A), shape(256, SIZE_C)],
        in_specs=[scalar()] + whole(2),
        out_specs=whole(4),
        compiler_params=params(),
        cost_estimate=cost(1),
        name="split",
    )(bits, keep, came)


def join_kernel(core_ref, own, came_a, came_b, came_c, table_keep, table_came, out):
    for i in range(8):
        rows = slice(i * 32, i * 32 + 32)
        out[i, :, 0:384] = own[rows, 0:384] + came_a[rows, :]
        out[i, :, 384:768] = own[rows, 384:768] + came_b[rows, :]
        out[i, :, 768:1024] = own[rows, 768:1024] + came_c[rows, :]
    first = core_ref[0] == 0
    mine, other = table_keep[...], table_came[...]
    out[:, 0:16, 1024:] = jnp.where(first, mine, other)
    out[:, 16:32, 1024:] = jnp.where(first, other, mine)


def join(core, *parts):
    return pl.pallas_call(
        join_kernel,
        out_shape=shape(8, 32, 1280),
        in_specs=[scalar()] + whole(6),
        out_specs=pl.BlockSpec(memory_space=pltpu.VMEM),
        compiler_params=params(),
        cost_estimate=cost(1),
        name="join",
    )(core, *parts)


def fold_lon_kernel(parts, out, total):
    value = parts[0]
    for i in range(1, 8):
        value = value + parts[i]
    total[...] = value
    for p in range(16):
        z, y = p // 2, p % 2
        rank = (z // 2) * 2 + y
        out[p, :, 0:768] = total[4 * rank : 4 * rank + 4, 0:768]
        out[p, :, 768:1024] = total[4 * z : 4 * z + 4, 768:1024]
        out[p, :, 1024:1152] = total[4 * z : 4 * z + 4, 1024 + 128 * y : 1152 + 128 * y]


def fold_lon(parts):
    return pl.pallas_call(
        fold_lon_kernel,
        out_shape=shape(16, 4, 1152),
        in_specs=whole(1),
        out_specs=pl.BlockSpec(memory_space=pltpu.VMEM),
        scratch_shapes=[pltpu.VMEM((32, 1280), F32)],
        compiler_params=params(),
        name="fold_lon",
    )(parts)


def fold_lat_kernel(bits, parts, out):
    odd, low = bits[0], bits[1]

    def summed(sources, cols):
        total = parts[sources[0], :, cols]
        for source in sources[1:]:
            total = total + parts[source, :, cols]
        return total

    same_z = [(2 * k + odd) * 2 + y for k in range(4) for y in range(2)]
    same_y = [2 * z + low for z in range(8)]
    total = jnp.concatenate(
        [
            summed(same_z, slice(0, 768)),
            summed(same_y, slice(768, 1024)),
            summed(list(range(16)), slice(1024, 1152)),
        ],
        axis=1,
    )
    for i in range(16):
        out[i] = total


def fold_lat(bits, parts):
    return pl.pallas_call(
        fold_lat_kernel,
        out_shape=shape(16, 4, 1152),
        in_specs=[scalar()] + whole(1),
        out_specs=pl.BlockSpec(memory_space=pltpu.VMEM),
        compiler_params=params(),
        name="fold_lat",
    )(bits, parts)


def unpack_kernel(parts, grad_in, grad_out, grad_bias, table):
    for p in range(16):
        z, y = p // 2, p % 2
        odd = z % 2
        rank = (z // 2) * 2 + y
        rows = slice(4 * rank, 4 * rank + 4)
        grad_in[rows, 384 * odd : 384 * odd + 384] = parts[p, :, 0:384]
        start = 768 + 384 * (1 - odd)
        grad_in[rows, start : start + 384] = parts[p, :, 384:768]
        rows = slice(4 * z, 4 * z + 4)
        grad_out[rows, 256 * y : 256 * y + 256] = parts[p, :, 768:1024]
        table[rows, 128 * y : 128 * y + 128] = parts[p, :, 1024:1152]
    for core in range(2):
        for half in range(2):
            base = core * 16 + half * 8
            grad_bias[core * 8 : core * 8 + 8, half * HALF_SECTOR : (half + 1) * HALF_SECTOR] = (
                table[base : base + 8, :HALF_SECTOR]
            )


def unpack(parts):
    return pl.pallas_call(
        unpack_kernel,
        out_shape=[shape(32, 3 * WIDTH), shape(32, WIDTH), shape(HEADS, 2 * HALF_SECTOR)],
        in_specs=whole(1),
        out_specs=whole(3),
        scratch_shapes=[pltpu.VMEM((32, 256), F32)],
        compiler_params=params(),
        name="unpack",
    )(parts)


def place_kernel(grad_out, own, left, below, corner, out):
    for ref, row0, col0 in ((own, 0, 3), (left, 0, 0), (below, 6, 3), (corner, 6, 0)):
        for row in range(6):
            for col in range(3):
                spot = row * 6 + col * 2
                out[row0 + row, col0 + col] = (
                    grad_out[row0 + row, col0 + col] + ref[spot : spot + 2, :]
                )


def place(grad_out, own, left, below, corner):
    return pl.pallas_call(
        place_kernel,
        out_shape=jax.ShapeDtypeStruct(grad_out.shape, F32),
        in_specs=whole(5),
        out_specs=pl.BlockSpec(memory_space=pltpu.VMEM),
        compiler_params=params(),
        name="place",
    )(grad_out, own, left, below, corner)


LAT = ("z", "y_lo")
LON = ("x", "y_hi", "core")


def body(fields, grad_out, region_ids, bias_index, bias_table, in_weight, out_weight):
    everything = LAT + LON
    lat = lax.axis_index(LAT)
    core = lax.axis_index("core").reshape(1)
    bits = jnp.stack([lax.rem(lax.axis_index("z"), 2), lax.axis_index("y_lo")])

    def moves(down, right):
        return [
            (i * 16 + j, (i + down) % 16 * 16 + (j + right) % 16)
            for i in range(16)
            for j in range(16)
        ]

    swap = [(0, 1), (1, 0)]
    last = jnp.where(lat == 15, 3, 0).reshape(1)
    grad_out = jnp.transpose(grad_out, (1, 2, 0, 3))
    own, left, below, corner = pack(
        last, jnp.transpose(fields, (1, 2, 0, 3)), grad_out, jnp.transpose(region_ids, (2, 0, 1))
    )
    quad3 = lax.ppermute(left, everything, moves(0, -1))
    quad0 = lax.ppermute(below, everything, moves(1, 0))
    quad1 = lax.ppermute(corner, everything, moves(1, -1))
    bias, places = lookup(core, bias_index, bias_table)
    keep, send, keep_scores, send_scores, grad0, grad1, grad2, grad3 = window(
        core, own, quad0, quad1, quad3, bias, in_weight, out_weight
    )
    came_scores = lax.ppermute(send_scores, "core", swap)
    came = lax.ppermute(send, "core", swap)
    start = scatter_start(places, keep_scores, came_scores)
    keep, start = lax.optimization_barrier((keep, start))
    part, send_a, send_b, send_c = split(bits, keep, came)
    came_a = lax.ppermute(send_a, "z", [(i, i ^ 1) for i in range(8)])
    came_b = lax.ppermute(send_b, "z", [(i, ((i + 1) % 8 ^ 1) + 7 & 7) for i in range(8)])
    came_c = lax.ppermute(send_c, "y_lo", swap)
    part, start = lax.optimization_barrier((part, start))
    mine, other = scatter_end(core, places, keep_scores, came_scores, start)
    came_table = lax.ppermute(other, "core", swap)
    back_left = lax.ppermute(grad3, everything, moves(0, 1))
    back_below = lax.ppermute(grad0, everything, moves(-1, 0))
    back_corner = lax.ppermute(grad1, everything, moves(-1, 1))
    joined = join(core, part, came_a, came_b, came_c, mine, came_table)
    parts = lax.all_to_all(joined, ("x", "y_hi"), 0, 0)
    parts, grad2 = lax.optimization_barrier((parts, grad2))
    grad_fields = place(grad_out, grad2, back_left, back_below, back_corner)
    parts = lax.all_to_all(fold_lon(parts), LAT, 0, 0)
    parts = lax.all_to_all(fold_lat(bits, parts), LAT, 0, 0)
    grad_in_weight, grad_out_weight, grad_bias = unpack(parts)
    return jnp.transpose(grad_fields, (2, 0, 1, 3)), grad_in_weight, grad_out_weight, grad_bias.T


def solution(mesh):
    split = Mesh(mesh.devices.reshape(8, 2, 4, 2, 2), LAT + LON)
    tokens = P(None, LAT, LON, None)
    in_specs = (tokens, tokens, P(None, LAT, LON), P(), P(), P(), P())
    out_specs = (tokens, P(LON, None), P(LON, None), P(LON, None))
    return jax.shard_map(body, mesh=split, in_specs=in_specs, out_specs=out_specs, check_vma=False)
```

```python
import jax
import jax.numpy as jnp
from jax import lax
from jax.experimental import pallas as pl
from jax.experimental.pallas import tpu as pltpu
from jax.sharding import Mesh
from jax.sharding import PartitionSpec as P

WIDTH = 512
HEADS = 16
HEAD_DIM = 32
TOKENS = 144
QUAD = 36
BIAS_ROWS = 6336
HALF_SECTOR = 198
BLOCKS = 25
PACK_MIB = 56
ROWS = 162
FACTOR = HEAD_DIM ** (-0.5)
F32 = jnp.float32
BF16 = jnp.bfloat16
MEGA = 1 << 20


def params(mib=16):
    return pltpu.CompilerParams(vmem_limit_bytes=mib * MEGA)


def cost(micros):
    return pl.CostEstimate(flops=int(micros * 1e9), bytes_accessed=0, transcendentals=0)


def whole(count):
    return [pl.BlockSpec(memory_space=pltpu.VMEM)] * count


def scalar():
    return pl.BlockSpec(memory_space=pltpu.SMEM)


def halves(x):
    high = x.astype(BF16)
    low = (x - high.astype(F32)).astype(BF16)
    return high, low


def dot(a, b, dims):
    return lax.dot_general(a, b, (dims, ((), ())), preferred_element_type=F32)


NN = ((1,), (0,))
NT = ((1,), (1,))
TN = ((0,), (0,))


def dot3(a, b, dims):
    ah, al = a
    bh, bl = b
    return dot(ah, bh, dims) + (dot(ah, bl, dims) + dot(al, bh, dims))


def token_order():
    place = lax.broadcasted_iota(jnp.int32, (TOKENS, TOKENS), 0)
    token = lax.broadcasted_iota(jnp.int32, (TOKENS, TOKENS), 1)

    def steps(value, size, count):
        total = jnp.zeros_like(value)
        for i in range(1, count):
            total = total + jnp.where(value >= i * size, 1, 0)
        return total

    quad = steps(place, QUAD, 4)
    rest = place - QUAD * quad
    row = steps(rest, 6, 6)
    rest = rest - 6 * row
    col = steps(rest, 2, 3)
    level = rest - 2 * col
    row_half = steps(quad, 2, 2)
    col_half = quad - 2 * row_half
    source = level * 72 + (6 * row_half + row) * 6 + 3 * col_half + col
    return jnp.where(source == token, 1.0, 0.0).astype(BF16)


def pack_kernel(last, fields, grads, ids, own, left, below, corner):
    lanes = lax.broadcasted_iota(jnp.int32, (2, WIDTH), 1)
    level = lax.broadcasted_iota(jnp.int32, (2, WIDTH), 0)
    bump = last[0]
    plan = (
        (own, 0, 3, 2, None),
        (left, 0, 0, 3, None),
        (below, 6, 3, 0, bump),
        (corner, 6, 0, 1, bump),
    )
    for ref, row0, col0, quadrant, offset in plan:
        label = jnp.zeros((2, WIDTH), jnp.int32)
        for row in range(6):
            for col in range(3):
                spot = row * 6 + col * 2
                ref[spot : spot + 2, :] = fields[row0 + row, col0 + col]
                ref[QUAD + spot : QUAD + spot + 2, :] = grads[row0 + row, col0 + col]
                value = ids[col0 + col, :, row0 + row : row0 + row + 1] + 1
                if offset is not None:
                    value = value + offset
                place = quadrant * QUAD + spot
                label = jnp.where(
                    lanes == level + place, jnp.broadcast_to(value, (2, WIDTH)), label
                )
        total = jnp.sum(label.astype(F32), axis=0, keepdims=True)
        ref[72:80, :] = jnp.broadcast_to(total, (8, WIDTH))


def pack(last, fields, grads, ids):
    shape = jax.ShapeDtypeStruct((80, WIDTH), F32)
    return pl.pallas_call(
        pack_kernel,
        out_shape=[shape] * 4,
        in_specs=[scalar()] + whole(3),
        out_specs=whole(4),
        compiler_params=params(PACK_MIB),
        cost_estimate=cost(1),
        name="pack",
    )(last, fields, grads, ids)


def one_hot(row, lines):
    low = (row & 255).astype(F32).astype(BF16)
    hit = lines == jnp.broadcast_to(low, (256, 128))
    return jnp.where(hit, jnp.ones((256, 128), BF16), jnp.zeros((256, 128), BF16))


def line_numbers():
    return lax.broadcasted_iota(jnp.int32, (256, 128), 0).astype(F32).astype(BF16)


def lookup_kernel(core_ref, index, table, bias, places, left):
    value = index[...]
    high = (value >> 7).astype(F32).astype(BF16)
    low = (value & 127).astype(F32).astype(BF16)
    move = token_order()

    def moved(part):
        return dot(dot(move, part, NN).astype(BF16), move, NT)

    result = moved(high) * 128.0 + moved(low)
    places[0:TOKENS, :] = result[:, :128].astype(jnp.int32)
    tail = jnp.concatenate([result[:, 128:], jnp.zeros((TOKENS, 112), F32)], axis=1)
    for i in range(18):
        spread = pltpu.roll(tail[8 * i : 8 * i + 8, :], 0, 1, stride=16, stride_axis=0)
        places[TOKENS + i : TOKENS + i + 1, :] = jnp.sum(spread, axis=0, keepdims=True).astype(jnp.int32)

    first = core_ref[0] == 0
    for block in range(BLOCKS):
        count = min(256, BIAS_ROWS - block * 256)
        top = table[0:8, block * 256 : block * 256 + count]
        bottom = table[8:16, block * 256 : block * 256 + count]
        part = jnp.concatenate(
            [jnp.where(first, bottom, top), jnp.where(first, top, bottom)], axis=0
        )
        if count < 256:
            part = jnp.concatenate([part, jnp.zeros((16, 256 - count), F32)], axis=1)
        left[block * 32 : block * 32 + 16, :], left[block * 32 + 16 : block * 32 + 32, :] = halves(
            part
        )
    lines = line_numbers()
    matrix = left[...]

    def find(rows):
        right = jnp.concatenate([one_hot(row, lines) for row in rows], axis=1)
        found = dot(matrix, right, NN)
        block = jnp.concatenate([row >> 8 for row in rows], axis=1)
        block = jnp.broadcast_to(block, (32, 256))
        total = jnp.zeros((32, 256), F32)
        for b in range(BLOCKS):
            total = jnp.where(block == b, found[b * 32 : b * 32 + 32], total)
        return total[:16] + total[16:]

    def step(i, carry):
        base = pl.multiple_of(i * 8, 8)
        rows = places[pl.ds(base, 8), :]
        for pair in range(4):
            found = find([rows[2 * pair + j : 2 * pair + j + 1, :] for j in range(2)])
            for j in range(2):
                bias[base + 2 * pair + j, :, 0:128] = found[:, j * 128 : j * 128 + 128]
        return carry

    lax.fori_loop(0, 18, step, 0)
    for pair in range(9):
        at = TOKENS + 2 * pair
        found = find([places[at + j : at + j + 1, :] for j in range(2)])
        for j in range(16):
            bias[16 * pair + j, :, 128:144] = found[:, 16 * j : 16 * j + 16]


def lookup(core, bias_index, bias_table):
    return pl.pallas_call(
        lookup_kernel,
        out_shape=[
            jax.ShapeDtypeStruct((TOKENS, HEADS, TOKENS), F32),
            jax.ShapeDtypeStruct((ROWS, 128), jnp.int32),
        ],
        in_specs=[scalar()] + whole(2),
        out_specs=whole(2),
        scratch_shapes=[pltpu.VMEM((BLOCKS * 32, 256), BF16)],
        compiler_params=params(),
        cost_estimate=cost(13),
        name="lookup",
    )(core, bias_index, bias_table.T)


def main_kernel(
    core_ref,
    own,
    quad0,
    quad1,
    quad3,
    bias,
    in_weight,
    out_weight,
    keep,
    send,
    keep_scores,
    send_scores,
    grad0,
    grad1,
    grad2,
    grad3,
    tokens,
    cotangent,
    proj,
    gatt,
    gproj,
    att,
    normed_t,
    tails,
):
    core = core_ref[0]
    for slot, quad in enumerate((quad0, quad1, own, quad3)):
        at = slot * QUAD
        tokens[at : at + QUAD, :] = quad[0:QUAD, :]
        cotangent[at : at + QUAD, :] = quad[QUAD : 2 * QUAD, :]
    row = (quad0[72:73, :] + quad1[72:73, :] + own[72:73, :] + quad3[72:73, :])[:, :TOKENS]
    side = lax.broadcasted_iota(jnp.int32, (TOKENS, TOKENS), 0)
    along = lax.broadcasted_iota(jnp.int32, (TOKENS, TOKENS), 1)
    spread = jnp.broadcast_to(row, (TOKENS, TOKENS))
    column = jnp.sum(jnp.where(side == along, spread, 0.0), axis=1, keepdims=True)
    allowed = column == spread

    inputs = tokens[...]
    centered = inputs - jnp.mean(inputs, axis=1, keepdims=True)
    variance = jnp.mean(centered * centered, axis=1, keepdims=True)
    inv_std = lax.rsqrt(variance + 1e-05)
    normed = centered * inv_std
    tokens[...] = normed
    normed_t[...] = normed.T
    halves_normed = halves(normed)
    for part in range(3):
        at = part * WIDTH
        weight = halves(in_weight[:, at : at + WIDTH])
        proj[at : at + WIDTH, :] = dot3(halves_normed, weight, NN).T
    halves_cotangent = halves(cotangent[...])
    gatt[...] = dot3(halves(out_weight[...]), halves_cotangent, NT)

    def stacked(*parts):
        return jnp.concatenate(parts, axis=0)

    def product(high, low, right_high, right_low, dims):
        both = dot(stacked(high, low), right_high, dims)
        return both[:HEAD_DIM] + (both[HEAD_DIM:] + dot(high, right_low, dims))

    def some_heads(heads):
        ats = [pl.multiple_of(head * HEAD_DIM, HEAD_DIM) for head, _ in heads]
        q = [halves(proj[pl.ds(at, HEAD_DIM), :] * FACTOR) for at in ats]
        k = [halves(proj[pl.ds(at + WIDTH, HEAD_DIM), :]) for at in ats]
        v = [halves(proj[pl.ds(at + 2 * WIDTH, HEAD_DIM), :]) for at in ats]
        g = [halves(gatt[pl.ds(at, HEAD_DIM), :]) for at in ats]

        def outer(left, right):
            return dot(
                stacked(left[0], left[0], left[1]), stacked(right[0], right[1], right[0]), TN
            )

        scores = [outer(q[i], k[i]) + bias[:, slot, :] for i, (_, slot) in enumerate(heads)]
        grad_probs = [outer(g[i], v[i]) for i in range(len(heads))]
        scores = [jnp.where(allowed, x, -1000000000.0) for x in scores]
        exponent = [jnp.exp(x - jnp.max(x, axis=1, keepdims=True)) for x in scores]
        probs = [x * (1.0 / jnp.sum(x, axis=1, keepdims=True)) for x in exponent]
        p = [halves(x) for x in probs]
        for i, at in enumerate(ats):
            att[pl.ds(at, HEAD_DIM), :] = product(*v[i], *p[i], NT)
            gproj[pl.ds(at + 2 * WIDTH, HEAD_DIM), :] = product(*g[i], *p[i], NN)
        grad_scores = [
            x * (y - jnp.sum(x * y, axis=1, keepdims=True)) for x, y in zip(probs, grad_probs)
        ]
        s = [halves(x) for x in grad_scores]
        for i, at in enumerate(ats):
            gproj[pl.ds(at, HEAD_DIM), :] = product(*k[i], *s[i], NT) * FACTOR
            gproj[pl.ds(at + WIDTH, HEAD_DIM), :] = product(*q[i], *s[i], NN)
        for i, (_, slot) in enumerate(heads):
            target = send_scores if slot < 8 else keep_scores
            target[0:TOKENS, slot % 8, :] = grad_scores[i][:, :128]
            tails[:, slot, 0:16] = grad_scores[i][:, 128:]

    tails[...] = jnp.zeros_like(tails)
    order = [((1 - core) * 8 + slot, slot) for slot in range(8)]
    order += [(core * 8 + slot, 8 + slot) for slot in range(8)]
    for first in range(0, 16, 4):
        some_heads(order[first : first + 4])

    for i in range(18):
        total = tails[8 * i]
        for j in range(1, 8):
            total = total + pltpu.roll(tails[8 * i + j], 16 * j, 1)
        send_scores[TOKENS + i] = total[0:8]
        keep_scores[TOKENS + i] = total[8:16]

    for target, bit in ((send, 1 - core), (keep, core)):
        rows = [pl.ds(pl.multiple_of(64 * i + 32 * bit, 32), 32) for i in range(8)]
        left = halves(jnp.concatenate([normed_t[r, :] for r in rows], axis=0))
        for part in range(3):
            at = part * WIDTH
            target[:, at : at + WIDTH] = dot3(left, halves(gproj[at : at + WIDTH, :]), NT)
        left = halves(jnp.concatenate([att[r, :] for r in rows], axis=0))
        target[:, 3 * WIDTH :] = dot3(left, halves_cotangent, NN)

    grad_normed = jnp.zeros((WIDTH, TOKENS), F32)
    for part in range(3):
        at = part * WIDTH
        grad_normed = grad_normed + dot3(
            halves(in_weight[:, at : at + WIDTH]), halves(gproj[at : at + WIDTH, :]), NN
        )
    grad_normed = grad_normed.T
    normed = tokens[...]
    result = inv_std * (
        grad_normed
        - jnp.mean(grad_normed, axis=1, keepdims=True)
        - normed * jnp.mean(grad_normed * normed, axis=1, keepdims=True)
    )
    tokens[...] = result
    for slot, target in enumerate((grad0, grad1, grad2, grad3)):
        target[...] = tokens[slot * QUAD : slot * QUAD + QUAD, :]


def shape(*dims):
    return jax.ShapeDtypeStruct(dims, F32)


def window(core, own, quad0, quad1, quad3, bias, in_weight, out_weight):
    grad = shape(QUAD, WIDTH)
    return pl.pallas_call(
        main_kernel,
        out_shape=[
            shape(256, 4 * WIDTH),
            shape(256, 4 * WIDTH),
            shape(ROWS, 8, 128),
            shape(ROWS, 8, 128),
            grad,
            grad,
            grad,
            grad,
        ],
        in_specs=[scalar()] + whole(7),
        out_specs=whole(8),
        scratch_shapes=[
            pltpu.VMEM((TOKENS, WIDTH), F32),
            pltpu.VMEM((TOKENS, WIDTH), F32),
            pltpu.VMEM((3 * WIDTH, TOKENS), F32),
            pltpu.VMEM((WIDTH, TOKENS), F32),
            pltpu.VMEM((3 * WIDTH, TOKENS), F32),
            pltpu.VMEM((WIDTH, TOKENS), F32),
            pltpu.VMEM((WIDTH, TOKENS), F32),
            pltpu.VMEM((TOKENS, HEADS, 128), F32),
        ],
        compiler_params=params(26),
        cost_estimate=cost(14),
        name="window",
    )(core, own, quad0, quad1, quad3, bias, in_weight, out_weight)


def add_pairs(places, keep, came, total, first, last):
    lines = line_numbers()

    def sides(row, values):
        block = (row >> 8).astype(F32).astype(BF16)
        both = jnp.concatenate(halves(values), axis=0)
        spread = jnp.broadcast_to(block, (16, 128))
        left = jnp.concatenate(
            [jnp.where(spread == float(b), both, jnp.zeros_like(both)) for b in range(BLOCKS)],
            axis=0,
        )
        return left, one_hot(row, lines)

    def add(rows, base, pair):
        pieces = [
            sides(rows[j : j + 1, :], keep[base + j] + came[base + j])
            for j in (2 * pair, 2 * pair + 1)
        ]
        left = jnp.concatenate([p[0] for p in pieces], axis=1)
        right = jnp.concatenate([p[1] for p in pieces], axis=1)
        total[...] += dot(left, right, NT)

    def step(i, carry):
        base = pl.multiple_of(i * 8, 8)
        rows = places[pl.ds(base, 8), :]
        for pair in range(4):
            add(rows, base, pair)
        return carry

    lax.fori_loop(first // 8, last // 8, step, 0)
    if last % 8:
        base = last // 8 * 8
        rows = places[base:last, :]
        for pair in range(last % 8 // 2):
            add(rows, base, pair)


def scatter_start_kernel(places, keep, came, total):
    total[...] = jnp.zeros_like(total)
    add_pairs(places, keep, came, total, 0, 80)


def scatter_start(places, keep, came):
    return pl.pallas_call(
        scatter_start_kernel,
        out_shape=shape(BLOCKS * 16, 256),
        in_specs=whole(3),
        out_specs=pl.BlockSpec(memory_space=pltpu.VMEM),
        compiler_params=params(),
        cost_estimate=cost(4.2),
        name="scatter_start",
    )(places, keep, came)


def scatter_end_kernel(core_ref, places, keep, came, start, mine, other, total, line, sectors):
    total[...] = start[...]
    add_pairs(places, keep, came, total, 80, ROWS)
    for b in range(BLOCKS):
        line[:, b * 256 : b * 256 + 256] = (
            total[b * 16 : b * 16 + 8, :] + total[b * 16 + 8 : b * 16 + 16, :]
        )
    line[:, BLOCKS * 256 :] = jnp.zeros((8, 256), F32)
    for m in range(32):
        chip, core, half = m // 4, m // 2 % 2, m % 2
        start_at = m * HALF_SECTOR
        base, shift = start_at // 128 * 128, start_at % 128
        piece = line[:, base : base + 512]
        if shift:
            piece = pltpu.roll(piece, 512 - shift, 1)
        sectors[core, chip, half * 8 : half * 8 + 8, :] = piece[:, :256]
    mine[...] = sectors[core_ref[0]]
    other[...] = sectors[1 - core_ref[0]]


def scatter_end(core, places, keep, came, start):
    return pl.pallas_call(
        scatter_end_kernel,
        out_shape=[shape(8, 16, 256)] * 2,
        in_specs=[scalar()] + whole(4),
        out_specs=whole(2),
        scratch_shapes=[
            pltpu.VMEM((BLOCKS * 16, 256), F32),
            pltpu.VMEM((8, BLOCKS * 256 + 256), F32),
            pltpu.VMEM((2, 8, 16, 256), F32),
        ],
        compiler_params=params(),
        cost_estimate=cost(4.6),
        name="scatter_end",
    )(core, places, keep, came, start)


SIZE_A, SIZE_C = 384, 256


def split_kernel(bits, keep, came, own, send_a, send_b, send_c):
    def columns(base, size, bit):
        cols = slice(base + size * bit, base + size * bit + size)
        return keep[:, cols] + came[:, cols]

    for bit in range(2):

        @pl.when(bits[0] == bit)
        def _():
            own[:, 0:384] = columns(0, SIZE_A, bit)
            own[:, 384:768] = columns(768, SIZE_A, 1 - bit)
            send_a[...] = columns(0, SIZE_A, 1 - bit)
            send_b[...] = columns(768, SIZE_A, bit)

        @pl.when(bits[1] == bit)
        def _():
            own[:, 768:1024] = columns(1536, SIZE_C, bit)
            send_c[...] = columns(1536, SIZE_C, 1 - bit)


def split(bits, keep, came):
    return pl.pallas_call(
        split_kernel,
        out_shape=[shape(256, 1024), shape(256, SIZE_A), shape(256, SIZE_A), shape(256, SIZE_C)],
        in_specs=[scalar()] + whole(2),
        out_specs=whole(4),
        compiler_params=params(),
        cost_estimate=cost(1),
        name="split",
    )(bits, keep, came)


def join_kernel(core_ref, own, came_a, came_b, came_c, table_keep, table_came, out):
    for i in range(8):
        rows = slice(i * 32, i * 32 + 32)
        out[i, :, 0:384] = own[rows, 0:384] + came_a[rows, :]
        out[i, :, 384:768] = own[rows, 384:768] + came_b[rows, :]
        out[i, :, 768:1024] = own[rows, 768:1024] + came_c[rows, :]
    first = core_ref[0] == 0
    mine, other = table_keep[...], table_came[...]
    out[:, 0:16, 1024:] = jnp.where(first, mine, other)
    out[:, 16:32, 1024:] = jnp.where(first, other, mine)


def join(core, *parts):
    return pl.pallas_call(
        join_kernel,
        out_shape=shape(8, 32, 1280),
        in_specs=[scalar()] + whole(6),
        out_specs=pl.BlockSpec(memory_space=pltpu.VMEM),
        compiler_params=params(),
        cost_estimate=cost(1),
        name="join",
    )(core, *parts)


def fold_lon_kernel(parts, out, total):
    value = parts[0]
    for i in range(1, 8):
        value = value + parts[i]
    total[...] = value
    for p in range(16):
        z, y = p // 2, p % 2
        rank = (z // 2) * 2 + y
        out[p, :, 0:768] = total[4 * rank : 4 * rank + 4, 0:768]
        out[p, :, 768:1024] = total[4 * z : 4 * z + 4, 768:1024]
        out[p, :, 1024:1152] = total[4 * z : 4 * z + 4, 1024 + 128 * y : 1152 + 128 * y]


def fold_lon(parts):
    return pl.pallas_call(
        fold_lon_kernel,
        out_shape=shape(16, 4, 1152),
        in_specs=whole(1),
        out_specs=pl.BlockSpec(memory_space=pltpu.VMEM),
        scratch_shapes=[pltpu.VMEM((32, 1280), F32)],
        compiler_params=params(),
        name="fold_lon",
    )(parts)


def fold_lat_kernel(bits, parts, out):
    odd, low = bits[0], bits[1]

    def summed(sources, cols):
        total = parts[sources[0], :, cols]
        for source in sources[1:]:
            total = total + parts[source, :, cols]
        return total

    same_z = [(2 * k + odd) * 2 + y for k in range(4) for y in range(2)]
    same_y = [2 * z + low for z in range(8)]
    total = jnp.concatenate(
        [
            summed(same_z, slice(0, 768)),
            summed(same_y, slice(768, 1024)),
            summed(list(range(16)), slice(1024, 1152)),
        ],
        axis=1,
    )
    for i in range(16):
        out[i] = total


def fold_lat(bits, parts):
    return pl.pallas_call(
        fold_lat_kernel,
        out_shape=shape(16, 4, 1152),
        in_specs=[scalar()] + whole(1),
        out_specs=pl.BlockSpec(memory_space=pltpu.VMEM),
        compiler_params=params(),
        name="fold_lat",
    )(bits, parts)


def unpack_kernel(parts, grad_in, grad_out, grad_bias, table):
    for p in range(16):
        z, y = p // 2, p % 2
        odd = z % 2
        rank = (z // 2) * 2 + y
        rows = slice(4 * rank, 4 * rank + 4)
        grad_in[rows, 384 * odd : 384 * odd + 384] = parts[p, :, 0:384]
        start = 768 + 384 * (1 - odd)
        grad_in[rows, start : start + 384] = parts[p, :, 384:768]
        rows = slice(4 * z, 4 * z + 4)
        grad_out[rows, 256 * y : 256 * y + 256] = parts[p, :, 768:1024]
        table[rows, 128 * y : 128 * y + 128] = parts[p, :, 1024:1152]
    for core in range(2):
        for half in range(2):
            base = core * 16 + half * 8
            grad_bias[core * 8 : core * 8 + 8, half * HALF_SECTOR : (half + 1) * HALF_SECTOR] = (
                table[base : base + 8, :HALF_SECTOR]
            )


def unpack(parts):
    return pl.pallas_call(
        unpack_kernel,
        out_shape=[shape(32, 3 * WIDTH), shape(32, WIDTH), shape(HEADS, 2 * HALF_SECTOR)],
        in_specs=whole(1),
        out_specs=whole(3),
        scratch_shapes=[pltpu.VMEM((32, 256), F32)],
        compiler_params=params(),
        name="unpack",
    )(parts)


def place_kernel(grad_out, own, left, below, corner, out):
    for ref, row0, col0 in ((own, 0, 3), (left, 0, 0), (below, 6, 3), (corner, 6, 0)):
        for row in range(6):
            for col in range(3):
                spot = row * 6 + col * 2
                out[row0 + row, col0 + col] = (
                    grad_out[row0 + row, col0 + col] + ref[spot : spot + 2, :]
                )


def place(grad_out, own, left, below, corner):
    return pl.pallas_call(
        place_kernel,
        out_shape=jax.ShapeDtypeStruct(grad_out.shape, F32),
        in_specs=whole(5),
        out_specs=pl.BlockSpec(memory_space=pltpu.VMEM),
        compiler_params=params(),
        name="place",
    )(grad_out, own, left, below, corner)


LAT = ("z", "y_lo")
LON = ("x", "y_hi", "core")


def body(fields, grad_out, region_ids, bias_index, bias_table, in_weight, out_weight):
    everything = LAT + LON
    lat = lax.axis_index(LAT)
    core = lax.axis_index("core").reshape(1)
    bits = jnp.stack([lax.rem(lax.axis_index("z"), 2), lax.axis_index("y_lo")])

    def moves(down, right):
        return [
            (i * 16 + j, (i + down) % 16 * 16 + (j + right) % 16)
            for i in range(16)
            for j in range(16)
        ]

    swap = [(0, 1), (1, 0)]
    last = jnp.where(lat == 15, 3, 0).reshape(1)
    grad_out = jnp.transpose(grad_out, (1, 2, 0, 3))
    own, left, below, corner = pack(
        last, jnp.transpose(fields, (1, 2, 0, 3)), grad_out, jnp.transpose(region_ids, (2, 0, 1))
    )
    quad3 = lax.ppermute(left, everything, moves(0, -1))
    quad0 = lax.ppermute(below, everything, moves(1, 0))
    quad1 = lax.ppermute(corner, everything, moves(1, -1))
    bias, places = lookup(core, bias_index, bias_table)
    keep, send, keep_scores, send_scores, grad0, grad1, grad2, grad3 = window(
        core, own, quad0, quad1, quad3, bias, in_weight, out_weight
    )
    came_scores = lax.ppermute(send_scores, "core", swap)
    came = lax.ppermute(send, "core", swap)
    back = (
        lax.ppermute(grad3, everything, moves(0, 1)),
        lax.ppermute(grad0, everything, moves(-1, 0)),
        lax.ppermute(grad1, everything, moves(-1, 1)),
    )
    start = scatter_start(places, keep_scores, came_scores)
    keep, start = lax.optimization_barrier((keep, start))
    part, send_a, send_b, send_c = split(bits, keep, came)
    came_a = lax.ppermute(send_a, "z", [(i, i ^ 1) for i in range(8)])
    came_b = lax.ppermute(send_b, "z", [(i, ((i + 1) % 8 ^ 1) + 7 & 7) for i in range(8)])
    came_c = lax.ppermute(send_c, "y_lo", swap)
    part, start, back = lax.optimization_barrier((part, start, back))
    mine, other = scatter_end(core, places, keep_scores, came_scores, start)
    came_table = lax.ppermute(other, "core", swap)
    mine, grad2 = lax.optimization_barrier((mine, grad2))
    grad_fields = place(grad_out, grad2, *back)
    part, grad_fields = lax.optimization_barrier((part, grad_fields))
    joined = join(core, part, came_a, came_b, came_c, mine, came_table)
    parts = lax.all_to_all(joined, ("x", "y_hi"), 0, 0)
    parts = lax.all_to_all(fold_lon(parts), LAT, 0, 0)
    parts = lax.all_to_all(fold_lat(bits, parts), LAT, 0, 0)
    grad_in_weight, grad_out_weight, grad_bias = unpack(parts)
    return jnp.transpose(grad_fields, (2, 0, 1, 3)), grad_in_weight, grad_out_weight, grad_bias.T


def solution(mesh):
    split = Mesh(mesh.devices.reshape(8, 2, 4, 2, 2), LAT + LON)
    tokens = P(None, LAT, LON, None)
    in_specs = (tokens, tokens, P(None, LAT, LON), P(), P(), P(), P())
    out_specs = (tokens, P(LON, None), P(LON, None), P(LON, None))
    return jax.shard_map(body, mesh=split, in_specs=in_specs, out_specs=out_specs, check_vma=False)
```

```python
import functools

import jax
import jax.numpy as jnp
from jax import lax
from jax.experimental import pallas as pl
from jax.experimental.pallas import tpu as pltpu
from jax.sharding import Mesh
from jax.sharding import PartitionSpec as P

WIDTH = 512
HEADS = 16
HEAD_DIM = 32
TOKENS = 144
QUAD = 36
BIAS_ROWS = 6336
HALF_SECTOR = 198
BLOCKS = 25
PACK_MIB = 56
ROWS = 162
SPLIT = 64
LOOKUP_COST = 6
WINDOW_COST = 0
SCATTER_COST = 9
FACTOR = HEAD_DIM ** (-0.5)
F32 = jnp.float32
BF16 = jnp.bfloat16
MEGA = 1 << 20


def params(mib=16):
    return pltpu.CompilerParams(vmem_limit_bytes=mib * MEGA)


def cost(micros):
    return pl.CostEstimate(flops=int(micros * 1e9), bytes_accessed=0, transcendentals=0)


def whole(count):
    return [pl.BlockSpec(memory_space=pltpu.VMEM)] * count


def scalar():
    return pl.BlockSpec(memory_space=pltpu.SMEM)


def halves(x):
    high = x.astype(BF16)
    low = (x - high.astype(F32)).astype(BF16)
    return high, low


def dot(a, b, dims):
    return lax.dot_general(a, b, (dims, ((), ())), preferred_element_type=F32)


NN = ((1,), (0,))
NT = ((1,), (1,))
TN = ((0,), (0,))


def dot3(a, b, dims):
    ah, al = a
    bh, bl = b
    return dot(ah, bh, dims) + (dot(ah, bl, dims) + dot(al, bh, dims))


def token_order():
    place = lax.broadcasted_iota(jnp.int32, (TOKENS, TOKENS), 0)
    token = lax.broadcasted_iota(jnp.int32, (TOKENS, TOKENS), 1)

    def steps(value, size, count):
        total = jnp.zeros_like(value)
        for i in range(1, count):
            total = total + jnp.where(value >= i * size, 1, 0)
        return total

    quad = steps(place, QUAD, 4)
    rest = place - QUAD * quad
    row = steps(rest, 6, 6)
    rest = rest - 6 * row
    col = steps(rest, 2, 3)
    level = rest - 2 * col
    row_half = steps(quad, 2, 2)
    col_half = quad - 2 * row_half
    source = level * 72 + (6 * row_half + row) * 6 + 3 * col_half + col
    return jnp.where(source == token, 1.0, 0.0).astype(BF16)


def pack_kernel(last, fields, grads, ids, own, down, left):
    lanes = lax.broadcasted_iota(jnp.int32, (2, WIDTH), 1)
    level = lax.broadcasted_iota(jnp.int32, (2, WIDTH), 0)
    bump = last[0]
    plan = (
        (own, 0, 0, 3, 2, None),
        (left, 0, 0, 0, 3, None),
        (down, 0, 6, 3, 0, bump),
        (down, 80, 6, 0, 1, bump),
    )
    for ref, base, row0, col0, quadrant, offset in plan:
        label = jnp.zeros((2, WIDTH), jnp.int32)
        for row in range(6):
            for col in range(3):
                spot = row * 6 + col * 2
                at = base + spot
                ref[at : at + 2, :] = fields[row0 + row, col0 + col]
                ref[QUAD + at : QUAD + at + 2, :] = grads[row0 + row, col0 + col]
                value = ids[col0 + col, :, row0 + row : row0 + row + 1] + 1
                if offset is not None:
                    value = value + offset
                place = quadrant * QUAD + spot
                label = jnp.where(
                    lanes == level + place, jnp.broadcast_to(value, (2, WIDTH)), label
                )
        total = jnp.sum(label.astype(F32), axis=0, keepdims=True)
        ref[base + 72 : base + 80, :] = jnp.broadcast_to(total, (8, WIDTH))


def pack(last, fields, grads, ids):
    return pl.pallas_call(
        pack_kernel,
        out_shape=[
            jax.ShapeDtypeStruct((80, WIDTH), F32),
            jax.ShapeDtypeStruct((160, WIDTH), F32),
            jax.ShapeDtypeStruct((80, WIDTH), F32),
        ],
        in_specs=[scalar()] + whole(3),
        out_specs=whole(3),
        compiler_params=params(PACK_MIB),
        cost_estimate=cost(1),
        name="pack",
    )(last, fields, grads, ids)


def stack_kernel(spans, first, second, out):
    (start1, stop1), (start2, stop2) = spans
    out[0 : stop1 - start1, :] = first[start1:stop1, :]
    out[stop1 - start1 :, :] = second[start2:stop2, :]


def stack(first, span1, second, span2):
    rows = span1[1] - span1[0] + span2[1] - span2[0]
    return pl.pallas_call(
        functools.partial(stack_kernel, (span1, span2)),
        out_shape=jax.ShapeDtypeStruct((rows, WIDTH), F32),
        in_specs=whole(2),
        out_specs=pl.BlockSpec(memory_space=pltpu.VMEM),
        compiler_params=params(),
        name="stack",
    )(first, second)


def one_hot(row, lines):
    low = (row & 255).astype(F32).astype(BF16)
    hit = lines == jnp.broadcast_to(low, (256, 128))
    return jnp.where(hit, jnp.ones((256, 128), BF16), jnp.zeros((256, 128), BF16))


def line_numbers():
    return lax.broadcasted_iota(jnp.int32, (256, 128), 0).astype(F32).astype(BF16)


def find_pairs(matrix, places, bias, steps, pairs, first):
    lines = line_numbers()
    left = matrix[...]

    def find(rows):
        right = jnp.concatenate([one_hot(row, lines) for row in rows], axis=1)
        found = dot(left, right, NN)
        block = jnp.concatenate([row >> 8 for row in rows], axis=1)
        block = jnp.broadcast_to(block, (32, 256))
        total = jnp.zeros((32, 256), F32)
        for b in range(BLOCKS):
            total = jnp.where(block == b, found[b * 32 : b * 32 + 32], total)
        return total[:16] + total[16:]

    def step(i, carry):
        base = pl.multiple_of(i * 8, 8)
        rows = places[pl.ds(base + first, 8), :]
        for pair in range(4):
            found = find([rows[2 * pair + j : 2 * pair + j + 1, :] for j in range(2)])
            for j in range(2):
                bias[base + 2 * pair + j, :, 0:128] = found[:, j * 128 : j * 128 + 128]
        return carry

    lax.fori_loop(0, steps, step, 0)
    for pair in range(pairs):
        at = TOKENS + first // 8 + 2 * pair
        found = find([places[at + j : at + j + 1, :] for j in range(2)])
        for j in range(16):
            bias[16 * pair + j, :, 128:144] = found[:, 16 * j : 16 * j + 16]


def lookup_start_kernel(core_ref, index, table, bias, places, left):
    value = index[...]
    high = (value >> 7).astype(F32).astype(BF16)
    low = (value & 127).astype(F32).astype(BF16)
    move = token_order()

    def moved(part):
        return dot(dot(move, part, NN).astype(BF16), move, NT)

    result = moved(high) * 128.0 + moved(low)
    places[0:TOKENS, :] = result[:, :128].astype(jnp.int32)
    tail = jnp.concatenate([result[:, 128:], jnp.zeros((TOKENS, 112), F32)], axis=1)
    for i in range(18):
        spread = pltpu.roll(tail[8 * i : 8 * i + 8, :], 0, 1, stride=16, stride_axis=0)
        places[TOKENS + i : TOKENS + i + 1, :] = jnp.sum(spread, axis=0, keepdims=True).astype(
            jnp.int32
        )

    first = core_ref[0] == 0
    for block in range(BLOCKS):
        count = min(256, BIAS_ROWS - block * 256)
        top = table[0:8, block * 256 : block * 256 + count]
        bottom = table[8:16, block * 256 : block * 256 + count]
        part = jnp.concatenate(
            [jnp.where(first, bottom, top), jnp.where(first, top, bottom)], axis=0
        )
        if count < 256:
            part = jnp.concatenate([part, jnp.zeros((16, 256 - count), F32)], axis=1)
        left[block * 32 : block * 32 + 16, :], left[block * 32 + 16 : block * 32 + 32, :] = halves(
            part
        )
    find_pairs(left, places, bias, SPLIT // 8, SPLIT // 16, 0)


def lookup_start(core, bias_index, bias_table):
    return pl.pallas_call(
        lookup_start_kernel,
        out_shape=[
            jax.ShapeDtypeStruct((SPLIT, HEADS, TOKENS), F32),
            jax.ShapeDtypeStruct((ROWS, 128), jnp.int32),
            jax.ShapeDtypeStruct((BLOCKS * 32, 256), BF16),
        ],
        in_specs=[scalar()] + whole(2),
        out_specs=whole(3),
        compiler_params=params(),
        cost_estimate=cost(LOOKUP_COST),
        name="lookup_start",
    )(core, bias_index, bias_table.T)


def lookup_end_kernel(places, left, bias):
    find_pairs(left, places, bias, (TOKENS - SPLIT) // 8, (TOKENS - SPLIT) // 16, SPLIT)


def lookup_end(places, left):
    return pl.pallas_call(
        lookup_end_kernel,
        out_shape=jax.ShapeDtypeStruct((TOKENS - SPLIT, HEADS, TOKENS), F32),
        in_specs=whole(2),
        out_specs=pl.BlockSpec(memory_space=pltpu.VMEM),
        compiler_params=params(),
        cost_estimate=cost(LOOKUP_COST),
        name="lookup_end",
    )(places, left)


def main_kernel(
    core_ref,
    own,
    above,
    beside,
    bias_start,
    bias_end,
    in_weight,
    out_weight,
    keep,
    send,
    keep_scores,
    send_scores,
    grad_above,
    grad_own,
    grad_beside,
    tokens,
    cotangent,
    proj,
    gatt,
    gproj,
    att,
    normed_t,
    tails,
):
    core = core_ref[0]
    row = jnp.zeros((1, WIDTH), F32)
    for slot, (quad, start) in enumerate(((above, 0), (beside, 0), (own, 0), (beside, 80))):
        at = slot * QUAD
        tokens[at : at + QUAD, :] = quad[start : start + QUAD, :]
        cotangent[at : at + QUAD, :] = quad[start + QUAD : start + 2 * QUAD, :]
        row = row + quad[start + 72 : start + 73, :]
    row = row[:, :TOKENS]
    side = lax.broadcasted_iota(jnp.int32, (TOKENS, TOKENS), 0)
    along = lax.broadcasted_iota(jnp.int32, (TOKENS, TOKENS), 1)
    spread = jnp.broadcast_to(row, (TOKENS, TOKENS))
    column = jnp.sum(jnp.where(side == along, spread, 0.0), axis=1, keepdims=True)
    allowed = column == spread

    inputs = tokens[...]
    centered = inputs - jnp.mean(inputs, axis=1, keepdims=True)
    variance = jnp.mean(centered * centered, axis=1, keepdims=True)
    inv_std = lax.rsqrt(variance + 1e-05)
    normed = centered * inv_std
    tokens[...] = normed
    normed_t[...] = normed.T
    halves_normed = halves(normed)
    for part in range(3):
        at = part * WIDTH
        weight = halves(in_weight[:, at : at + WIDTH])
        proj[at : at + WIDTH, :] = dot3(halves_normed, weight, NN).T
    halves_cotangent = halves(cotangent[...])
    gatt[...] = dot3(halves(out_weight[...]), halves_cotangent, NT)

    def stacked(*parts):
        return jnp.concatenate(parts, axis=0)

    def product(high, low, right_high, right_low, dims):
        both = dot(stacked(high, low), right_high, dims)
        return both[:HEAD_DIM] + (both[HEAD_DIM:] + dot(high, right_low, dims))

    def some_heads(heads):
        ats = [pl.multiple_of(head * HEAD_DIM, HEAD_DIM) for head, _ in heads]
        q = [halves(proj[pl.ds(at, HEAD_DIM), :] * FACTOR) for at in ats]
        k = [halves(proj[pl.ds(at + WIDTH, HEAD_DIM), :]) for at in ats]
        v = [halves(proj[pl.ds(at + 2 * WIDTH, HEAD_DIM), :]) for at in ats]
        g = [halves(gatt[pl.ds(at, HEAD_DIM), :]) for at in ats]

        def outer(left, right):
            return dot(
                stacked(left[0], left[0], left[1]), stacked(right[0], right[1], right[0]), TN
            )

        scores = [
            outer(q[i], k[i])
            + jnp.concatenate([bias_start[:, slot, :], bias_end[:, slot, :]], axis=0)
            for i, (_, slot) in enumerate(heads)
        ]
        grad_probs = [outer(g[i], v[i]) for i in range(len(heads))]
        scores = [jnp.where(allowed, x, -1000000000.0) for x in scores]
        exponent = [jnp.exp(x - jnp.max(x, axis=1, keepdims=True)) for x in scores]
        probs = [x * (1.0 / jnp.sum(x, axis=1, keepdims=True)) for x in exponent]
        p = [halves(x) for x in probs]
        for i, at in enumerate(ats):
            att[pl.ds(at, HEAD_DIM), :] = product(*v[i], *p[i], NT)
            gproj[pl.ds(at + 2 * WIDTH, HEAD_DIM), :] = product(*g[i], *p[i], NN)
        grad_scores = [
            x * (y - jnp.sum(x * y, axis=1, keepdims=True)) for x, y in zip(probs, grad_probs)
        ]
        s = [halves(x) for x in grad_scores]
        for i, at in enumerate(ats):
            gproj[pl.ds(at, HEAD_DIM), :] = product(*k[i], *s[i], NT) * FACTOR
            gproj[pl.ds(at + WIDTH, HEAD_DIM), :] = product(*q[i], *s[i], NN)
        for i, (_, slot) in enumerate(heads):
            target = send_scores if slot < 8 else keep_scores
            target[0:TOKENS, slot % 8, :] = grad_scores[i][:, :128]
            tails[:, slot, 0:16] = grad_scores[i][:, 128:]

    tails[...] = jnp.zeros_like(tails)
    order = [((1 - core) * 8 + slot, slot) for slot in range(8)]
    order += [(core * 8 + slot, 8 + slot) for slot in range(8)]
    for first in range(0, 16, 4):
        some_heads(order[first : first + 4])

    for i in range(18):
        total = tails[8 * i]
        for j in range(1, 8):
            total = total + pltpu.roll(tails[8 * i + j], 16 * j, 1)
        send_scores[TOKENS + i] = total[0:8]
        keep_scores[TOKENS + i] = total[8:16]

    for target, bit in ((send, 1 - core), (keep, core)):
        rows = [pl.ds(pl.multiple_of(64 * i + 32 * bit, 32), 32) for i in range(8)]
        left = halves(jnp.concatenate([normed_t[r, :] for r in rows], axis=0))
        for part in range(3):
            at = part * WIDTH
            target[:, at : at + WIDTH] = dot3(left, halves(gproj[at : at + WIDTH, :]), NT)
        left = halves(jnp.concatenate([att[r, :] for r in rows], axis=0))
        target[:, 3 * WIDTH :] = dot3(left, halves_cotangent, NN)

    grad_normed = jnp.zeros((WIDTH, TOKENS), F32)
    for part in range(3):
        at = part * WIDTH
        grad_normed = grad_normed + dot3(
            halves(in_weight[:, at : at + WIDTH]), halves(gproj[at : at + WIDTH, :]), NN
        )
    grad_normed = grad_normed.T
    normed = tokens[...]
    result = inv_std * (
        grad_normed
        - jnp.mean(grad_normed, axis=1, keepdims=True)
        - normed * jnp.mean(grad_normed * normed, axis=1, keepdims=True)
    )
    tokens[...] = result
    grad_above[...] = tokens[0:QUAD, :]
    grad_beside[0:QUAD, :] = tokens[QUAD : 2 * QUAD, :]
    grad_own[...] = tokens[2 * QUAD : 3 * QUAD, :]
    grad_beside[QUAD:, :] = tokens[3 * QUAD :, :]


def shape(*dims):
    return jax.ShapeDtypeStruct(dims, F32)


def window(core, own, above, beside, bias_start, bias_end, in_weight, out_weight):
    grad = shape(QUAD, WIDTH)
    return pl.pallas_call(
        main_kernel,
        out_shape=[
            shape(256, 4 * WIDTH),
            shape(256, 4 * WIDTH),
            shape(ROWS, 8, 128),
            shape(ROWS, 8, 128),
            grad,
            grad,
            shape(2 * QUAD, WIDTH),
        ],
        in_specs=[scalar()] + whole(7),
        out_specs=whole(7),
        scratch_shapes=[
            pltpu.VMEM((TOKENS, WIDTH), F32),
            pltpu.VMEM((TOKENS, WIDTH), F32),
            pltpu.VMEM((3 * WIDTH, TOKENS), F32),
            pltpu.VMEM((WIDTH, TOKENS), F32),
            pltpu.VMEM((3 * WIDTH, TOKENS), F32),
            pltpu.VMEM((WIDTH, TOKENS), F32),
            pltpu.VMEM((WIDTH, TOKENS), F32),
            pltpu.VMEM((TOKENS, HEADS, 128), F32),
        ],
        compiler_params=params(26),
        cost_estimate=cost(WINDOW_COST),
        name="window",
    )(core, own, above, beside, bias_start, bias_end, in_weight, out_weight)


def add_pairs(places, keep, came, total):
    lines = line_numbers()

    def sides(row, values):
        block = (row >> 8).astype(F32).astype(BF16)
        both = jnp.concatenate(halves(values), axis=0)
        spread = jnp.broadcast_to(block, (16, 128))
        left = jnp.concatenate(
            [jnp.where(spread == float(b), both, jnp.zeros_like(both)) for b in range(BLOCKS)],
            axis=0,
        )
        return left, one_hot(row, lines)

    def add(rows, base, pair):
        pieces = [
            sides(rows[j : j + 1, :], keep[base + j] + came[base + j])
            for j in (2 * pair, 2 * pair + 1)
        ]
        left = jnp.concatenate([p[0] for p in pieces], axis=1)
        right = jnp.concatenate([p[1] for p in pieces], axis=1)
        total[...] += dot(left, right, NT)

    def step(i, carry):
        base = pl.multiple_of(i * 8, 8)
        rows = places[pl.ds(base, 8), :]
        for pair in range(4):
            add(rows, base, pair)
        return carry

    lax.fori_loop(0, ROWS // 8, step, 0)
    add(places[ROWS - 2 : ROWS, :], ROWS - 2, 0)


def scatter_kernel(core_ref, places, keep, came, mine, other, total, line, sectors):
    total[...] = jnp.zeros_like(total)
    add_pairs(places, keep, came, total)
    for b in range(BLOCKS):
        line[:, b * 256 : b * 256 + 256] = (
            total[b * 16 : b * 16 + 8, :] + total[b * 16 + 8 : b * 16 + 16, :]
        )
    line[:, BLOCKS * 256 :] = jnp.zeros((8, 256), F32)
    for m in range(32):
        chip, core, half = m // 4, m // 2 % 2, m % 2
        start_at = m * HALF_SECTOR
        base, shift = start_at // 128 * 128, start_at % 128
        piece = line[:, base : base + 512]
        if shift:
            piece = pltpu.roll(piece, 512 - shift, 1)
        sectors[core, chip, half * 8 : half * 8 + 8, :] = piece[:, :256]
    mine[...] = sectors[core_ref[0]]
    other[...] = sectors[1 - core_ref[0]]


def scatter(core, places, keep, came):
    return pl.pallas_call(
        scatter_kernel,
        out_shape=[shape(8, 16, 256)] * 2,
        in_specs=[scalar()] + whole(3),
        out_specs=whole(2),
        scratch_shapes=[
            pltpu.VMEM((BLOCKS * 16, 256), F32),
            pltpu.VMEM((8, BLOCKS * 256 + 256), F32),
            pltpu.VMEM((2, 8, 16, 256), F32),
        ],
        compiler_params=params(),
        cost_estimate=cost(SCATTER_COST),
        name="scatter",
    )(core, places, keep, came)


def split_kernel(odd, keep, came, own, send_a, send_b):
    def columns(bit):
        cols = slice(512 * bit, 512 * bit + 512)
        return keep[:, cols] + came[:, cols]

    for bit in range(2):

        @pl.when(odd[0] == bit)
        def _():
            send_a[...] = columns(1 - bit)
            send_b[...] = columns(2 + bit)
            own[:, 0:512] = columns(bit)
            own[:, 512:1024] = columns(3 - bit)


def split(odd, keep, came):
    return pl.pallas_call(
        split_kernel,
        out_shape=[shape(256, 1024), shape(256, 512), shape(256, 512)],
        in_specs=[scalar()] + whole(2),
        out_specs=whole(3),
        compiler_params=params(),
        name="split",
    )(odd, keep, came)


def join_kernel(core_ref, own, came_a, came_b, table_keep, table_came, out):
    for i in range(8):
        rows = slice(i * 32, i * 32 + 32)
        out[i, :, 0:512] = own[rows, 0:512] + came_a[rows, :]
        out[i, :, 512:1024] = own[rows, 512:1024] + came_b[rows, :]
    first = core_ref[0] == 0
    mine, other = table_keep[...], table_came[...]
    out[:, 0:16, 1024:] = jnp.where(first, mine, other)
    out[:, 16:32, 1024:] = jnp.where(first, other, mine)


def join(core, *parts):
    return pl.pallas_call(
        join_kernel,
        out_shape=shape(8, 32, 1280),
        in_specs=[scalar()] + whole(5),
        out_specs=pl.BlockSpec(memory_space=pltpu.VMEM),
        compiler_params=params(),
        name="join",
    )(core, *parts)


def fold_lon_kernel(parts, out, total):
    value = parts[0]
    for i in range(1, 8):
        value = value + parts[i]
    total[...] = value
    for i in range(8):
        out[i] = total[4 * i : 4 * i + 4, :]


def fold_lon(parts):
    return pl.pallas_call(
        fold_lon_kernel,
        out_shape=shape(8, 4, 1280),
        in_specs=whole(1),
        out_specs=pl.BlockSpec(memory_space=pltpu.VMEM),
        scratch_shapes=[pltpu.VMEM((32, 1280), F32)],
        compiler_params=params(),
        name="fold_lon",
    )(parts)


def fold_lat_kernel(parts, out):
    total = parts[0]
    for i in range(1, 8):
        total = total + parts[i]
    for i in range(16):
        out[i] = total


def fold_lat(parts):
    return pl.pallas_call(
        fold_lat_kernel,
        out_shape=shape(16, 4, 1280),
        in_specs=whole(1),
        out_specs=pl.BlockSpec(memory_space=pltpu.VMEM),
        compiler_params=params(),
        name="fold_lat",
    )(parts)


def unpack_kernel(parts, grad_in, grad_out, grad_bias, table):
    for rank in range(8):
        rows = slice(4 * rank, 4 * rank + 4)
        even = (rank // 2) * 4 + rank % 2
        odd = even + 2
        grad_in[rows, 0:512] = parts[even, :, 0:512]
        grad_in[rows, 512:1024] = parts[odd, :, 0:512]
        grad_in[rows, 1024:1536] = parts[odd, :, 512:1024]
        grad_out[rows, :] = parts[even, :, 512:1024]
        table[rows, :] = parts[even, :, 1024:] + parts[odd, :, 1024:]
    for core in range(2):
        for half in range(2):
            base = core * 16 + half * 8
            grad_bias[core * 8 : core * 8 + 8, half * HALF_SECTOR : (half + 1) * HALF_SECTOR] = (
                table[base : base + 8, :HALF_SECTOR]
            )


def unpack(parts):
    return pl.pallas_call(
        unpack_kernel,
        out_shape=[shape(32, 3 * WIDTH), shape(32, WIDTH), shape(HEADS, 2 * HALF_SECTOR)],
        in_specs=whole(1),
        out_specs=whole(3),
        scratch_shapes=[pltpu.VMEM((32, 256), F32)],
        compiler_params=params(),
        name="unpack",
    )(parts)


def place_kernel(grad_out, own, beside, below, out):
    plan = ((own, 0, 0, 3), (beside, QUAD, 0, 0), (below, 0, 6, 3), (below, QUAD, 6, 0))
    for ref, base, row0, col0 in plan:
        for row in range(6):
            for col in range(3):
                spot = base + row * 6 + col * 2
                out[row0 + row, col0 + col] = (
                    grad_out[row0 + row, col0 + col] + ref[spot : spot + 2, :]
                )


def place(grad_out, own, beside, below):
    return pl.pallas_call(
        place_kernel,
        out_shape=jax.ShapeDtypeStruct(grad_out.shape, F32),
        in_specs=whole(4),
        out_specs=pl.BlockSpec(memory_space=pltpu.VMEM),
        compiler_params=params(),
        name="place",
    )(grad_out, own, beside, below)


LAT = ("z", "y_lo")
LON = ("x", "y_hi", "core")


def body(fields, grad_out, region_ids, bias_index, bias_table, in_weight, out_weight):
    everything = LAT + LON
    lat = lax.axis_index(LAT)
    core = lax.axis_index("core").reshape(1)
    odd = lax.rem(lax.axis_index("z"), 2).reshape(1)

    def moves(down, right):
        return [
            (i * 16 + j, (i + down) % 16 * 16 + (j + right) % 16)
            for i in range(16)
            for j in range(16)
        ]

    swap = [(0, 1), (1, 0)]
    last = jnp.where(lat == 15, 3, 0).reshape(1)
    grad_out = jnp.transpose(grad_out, (1, 2, 0, 3))
    own, down, left = pack(
        last, jnp.transpose(fields, (1, 2, 0, 3)), grad_out, jnp.transpose(region_ids, (2, 0, 1))
    )
    above = lax.ppermute(down, everything, moves(1, 0))
    bias_start, places, matrix = lookup_start(core, bias_index, bias_table)
    above, places = lax.optimization_barrier((above, places))
    beside = lax.ppermute(stack(above, (80, 160), left, (0, 80)), everything, moves(0, -1))
    bias_end = lookup_end(places, matrix)
    beside, bias_end = lax.optimization_barrier((beside, bias_end))
    keep, send, keep_scores, send_scores, grad_above, grad_own, grad_beside = window(
        core, own, above, beside, bias_start, bias_end, in_weight, out_weight
    )
    came = lax.ppermute(send, "core", swap)
    came_scores = lax.ppermute(send_scores, "core", swap)
    back_beside = lax.ppermute(grad_beside, everything, moves(0, 1))
    part, send_a, send_b = split(odd, keep, came)
    came_a = lax.ppermute(send_a, "z", [(i, i ^ 1) for i in range(8)])
    came_b = lax.ppermute(send_b, "z", [(i, ((i + 1) % 8 ^ 1) + 7 & 7) for i in range(8)])
    back_beside, part = lax.optimization_barrier((back_beside, part))
    back_below = lax.ppermute(
        stack(grad_above, (0, QUAD), back_beside, (0, QUAD)), everything, moves(-1, 0)
    )
    part, places = lax.optimization_barrier((part, places))
    mine, other = scatter(core, places, keep_scores, came_scores)
    came_table = lax.ppermute(other, "core", swap)
    mine, grad_own = lax.optimization_barrier((mine, grad_own))
    grad_fields = place(grad_out, grad_own, back_beside, back_below)
    part, grad_fields = lax.optimization_barrier((part, grad_fields))
    joined = join(core, part, came_a, came_b, mine, came_table)
    parts = lax.all_to_all(joined, ("x", "y_hi"), 0, 0)
    parity = [[z * 2 + y for z in range(bit, 8, 2) for y in range(2)] for bit in range(2)]
    parts = lax.all_to_all(fold_lon(parts), LAT, 0, 0, axis_index_groups=parity)
    parts = lax.all_to_all(fold_lat(parts), LAT, 0, 0)
    grad_in_weight, grad_out_weight, grad_bias = unpack(parts)
    return jnp.transpose(grad_fields, (2, 0, 1, 3)), grad_in_weight, grad_out_weight, grad_bias.T


def solution(mesh):
    split = Mesh(mesh.devices.reshape(8, 2, 4, 2, 2), LAT + LON)
    tokens = P(None, LAT, LON, None)
    in_specs = (tokens, tokens, P(None, LAT, LON), P(), P(), P(), P())
    out_specs = (tokens, P(LON, None), P(LON, None), P(LON, None))
    return jax.shard_map(body, mesh=split, in_specs=in_specs, out_specs=out_specs, check_vma=False)
```

```python
import functools

import jax
import jax.numpy as jnp
from jax import lax
from jax.experimental import pallas as pl
from jax.experimental.pallas import tpu as pltpu
from jax.sharding import Mesh
from jax.sharding import PartitionSpec as P

WIDTH = 512
HEADS = 16
HEAD_DIM = 32
TOKENS = 144
QUAD = 36
BIAS_ROWS = 6336
HALF_SECTOR = 198
BLOCKS = 25
PACK_MIB = 56
ROWS = 162
LOOKUP_COST = 13
WINDOW_COST = 0
SCATTER_COST = 9
FACTOR = HEAD_DIM ** (-0.5)
F32 = jnp.float32
BF16 = jnp.bfloat16
MEGA = 1 << 20


def params(mib=16):
    return pltpu.CompilerParams(vmem_limit_bytes=mib * MEGA)


def cost(micros):
    return pl.CostEstimate(flops=int(micros * 1e9), bytes_accessed=0, transcendentals=0)


def whole(count):
    return [pl.BlockSpec(memory_space=pltpu.VMEM)] * count


def scalar():
    return pl.BlockSpec(memory_space=pltpu.SMEM)


def halves(x):
    high = x.astype(BF16)
    low = (x - high.astype(F32)).astype(BF16)
    return high, low


def dot(a, b, dims):
    return lax.dot_general(a, b, (dims, ((), ())), preferred_element_type=F32)


NN = ((1,), (0,))
NT = ((1,), (1,))
TN = ((0,), (0,))


def dot3(a, b, dims):
    ah, al = a
    bh, bl = b
    return dot(ah, bh, dims) + (dot(ah, bl, dims) + dot(al, bh, dims))


def token_order():
    place = lax.broadcasted_iota(jnp.int32, (TOKENS, TOKENS), 0)
    token = lax.broadcasted_iota(jnp.int32, (TOKENS, TOKENS), 1)

    def steps(value, size, count):
        total = jnp.zeros_like(value)
        for i in range(1, count):
            total = total + jnp.where(value >= i * size, 1, 0)
        return total

    quad = steps(place, QUAD, 4)
    rest = place - QUAD * quad
    row = steps(rest, 6, 6)
    rest = rest - 6 * row
    col = steps(rest, 2, 3)
    level = rest - 2 * col
    row_half = steps(quad, 2, 2)
    col_half = quad - 2 * row_half
    source = level * 72 + (6 * row_half + row) * 6 + 3 * col_half + col
    return jnp.where(source == token, 1.0, 0.0).astype(BF16)


def pack_kernel(last, fields, grads, ids, own, left, below, corner):
    lanes = lax.broadcasted_iota(jnp.int32, (2, WIDTH), 1)
    level = lax.broadcasted_iota(jnp.int32, (2, WIDTH), 0)
    bump = last[0]
    plan = (
        (own, 0, 3, 2, None),
        (left, 0, 0, 3, None),
        (below, 6, 3, 0, bump),
        (corner, 6, 0, 1, bump),
    )
    for ref, row0, col0, quadrant, offset in plan:
        label = jnp.zeros((2, WIDTH), jnp.int32)
        for row in range(6):
            for col in range(3):
                spot = row * 6 + col * 2
                ref[spot : spot + 2, :] = fields[row0 + row, col0 + col]
                ref[QUAD + spot : QUAD + spot + 2, :] = grads[row0 + row, col0 + col]
                value = ids[col0 + col, :, row0 + row : row0 + row + 1] + 1
                if offset is not None:
                    value = value + offset
                place = quadrant * QUAD + spot
                label = jnp.where(
                    lanes == level + place, jnp.broadcast_to(value, (2, WIDTH)), label
                )
        total = jnp.sum(label.astype(F32), axis=0, keepdims=True)
        ref[72:80, :] = jnp.broadcast_to(total, (8, WIDTH))


def pack(last, fields, grads, ids):
    shape = jax.ShapeDtypeStruct((80, WIDTH), F32)
    return pl.pallas_call(
        pack_kernel,
        out_shape=[shape] * 4,
        in_specs=[scalar()] + whole(3),
        out_specs=whole(4),
        compiler_params=params(PACK_MIB),
        cost_estimate=cost(1),
        name="pack",
    )(last, fields, grads, ids)


def stack_kernel(spans, first, second, out):
    (start1, stop1), (start2, stop2) = spans
    out[0 : stop1 - start1, :] = first[start1:stop1, :]
    out[stop1 - start1 :, :] = second[start2:stop2, :]


def stack(first, span1, second, span2):
    rows = span1[1] - span1[0] + span2[1] - span2[0]
    return pl.pallas_call(
        functools.partial(stack_kernel, (span1, span2)),
        out_shape=jax.ShapeDtypeStruct((rows, WIDTH), F32),
        in_specs=whole(2),
        out_specs=pl.BlockSpec(memory_space=pltpu.VMEM),
        compiler_params=params(),
        name="stack",
    )(first, second)


def one_hot(row, lines):
    low = (row & 255).astype(F32).astype(BF16)
    hit = lines == jnp.broadcast_to(low, (256, 128))
    return jnp.where(hit, jnp.ones((256, 128), BF16), jnp.zeros((256, 128), BF16))


def line_numbers():
    return lax.broadcasted_iota(jnp.int32, (256, 128), 0).astype(F32).astype(BF16)


def lookup_kernel(core_ref, index, table, bias, places, left):
    value = index[...]
    high = (value >> 7).astype(F32).astype(BF16)
    low = (value & 127).astype(F32).astype(BF16)
    move = token_order()

    def moved(part):
        return dot(dot(move, part, NN).astype(BF16), move, NT)

    result = moved(high) * 128.0 + moved(low)
    places[0:TOKENS, :] = result[:, :128].astype(jnp.int32)
    tail = jnp.concatenate([result[:, 128:], jnp.zeros((TOKENS, 112), F32)], axis=1)
    for i in range(18):
        spread = pltpu.roll(tail[8 * i : 8 * i + 8, :], 0, 1, stride=16, stride_axis=0)
        places[TOKENS + i : TOKENS + i + 1, :] = jnp.sum(spread, axis=0, keepdims=True).astype(jnp.int32)

    first = core_ref[0] == 0
    for block in range(BLOCKS):
        count = min(256, BIAS_ROWS - block * 256)
        top = table[0:8, block * 256 : block * 256 + count]
        bottom = table[8:16, block * 256 : block * 256 + count]
        part = jnp.concatenate(
            [jnp.where(first, bottom, top), jnp.where(first, top, bottom)], axis=0
        )
        if count < 256:
            part = jnp.concatenate([part, jnp.zeros((16, 256 - count), F32)], axis=1)
        left[block * 32 : block * 32 + 16, :], left[block * 32 + 16 : block * 32 + 32, :] = halves(
            part
        )
    lines = line_numbers()
    matrix = left[...]

    def find(rows):
        right = jnp.concatenate([one_hot(row, lines) for row in rows], axis=1)
        found = dot(matrix, right, NN)
        block = jnp.concatenate([row >> 8 for row in rows], axis=1)
        block = jnp.broadcast_to(block, (32, 256))
        total = jnp.zeros((32, 256), F32)
        for b in range(BLOCKS):
            total = jnp.where(block == b, found[b * 32 : b * 32 + 32], total)
        return total[:16] + total[16:]

    def step(i, carry):
        base = pl.multiple_of(i * 8, 8)
        rows = places[pl.ds(base, 8), :]
        for pair in range(4):
            found = find([rows[2 * pair + j : 2 * pair + j + 1, :] for j in range(2)])
            for j in range(2):
                bias[base + 2 * pair + j, :, 0:128] = found[:, j * 128 : j * 128 + 128]
        return carry

    lax.fori_loop(0, 18, step, 0)
    for pair in range(9):
        at = TOKENS + 2 * pair
        found = find([places[at + j : at + j + 1, :] for j in range(2)])
        for j in range(16):
            bias[16 * pair + j, :, 128:144] = found[:, 16 * j : 16 * j + 16]


def lookup(core, bias_index, bias_table):
    return pl.pallas_call(
        lookup_kernel,
        out_shape=[
            jax.ShapeDtypeStruct((TOKENS, HEADS, TOKENS), F32),
            jax.ShapeDtypeStruct((ROWS, 128), jnp.int32),
        ],
        in_specs=[scalar()] + whole(2),
        out_specs=whole(2),
        scratch_shapes=[pltpu.VMEM((BLOCKS * 32, 256), BF16)],
        compiler_params=params(),
        cost_estimate=cost(LOOKUP_COST),
        name="lookup",
    )(core, bias_index, bias_table.T)


def main_kernel(
    core_ref,
    own,
    quad0,
    quad1,
    quad3,
    bias,
    in_weight,
    out_weight,
    keep,
    send,
    keep_scores,
    send_scores,
    grad_above,
    grad_own,
    grad_beside,
    tokens,
    cotangent,
    proj,
    gatt,
    gproj,
    att,
    normed_t,
    tails,
):
    core = core_ref[0]
    row = jnp.zeros((1, WIDTH), F32)
    for slot, (quad, start) in enumerate(((quad0, 0), (quad1, 0), (own, 0), (quad3, 0))):
        at = slot * QUAD
        tokens[at : at + QUAD, :] = quad[start : start + QUAD, :]
        cotangent[at : at + QUAD, :] = quad[start + QUAD : start + 2 * QUAD, :]
        row = row + quad[start + 72 : start + 73, :]
    row = row[:, :TOKENS]
    side = lax.broadcasted_iota(jnp.int32, (TOKENS, TOKENS), 0)
    along = lax.broadcasted_iota(jnp.int32, (TOKENS, TOKENS), 1)
    spread = jnp.broadcast_to(row, (TOKENS, TOKENS))
    column = jnp.sum(jnp.where(side == along, spread, 0.0), axis=1, keepdims=True)
    allowed = column == spread

    inputs = tokens[...]
    centered = inputs - jnp.mean(inputs, axis=1, keepdims=True)
    variance = jnp.mean(centered * centered, axis=1, keepdims=True)
    inv_std = lax.rsqrt(variance + 1e-05)
    normed = centered * inv_std
    tokens[...] = normed
    normed_t[...] = normed.T
    halves_normed = halves(normed)
    for part in range(3):
        at = part * WIDTH
        weight = halves(in_weight[:, at : at + WIDTH])
        proj[at : at + WIDTH, :] = dot3(halves_normed, weight, NN).T
    halves_cotangent = halves(cotangent[...])
    gatt[...] = dot3(halves(out_weight[...]), halves_cotangent, NT)

    def stacked(*parts):
        return jnp.concatenate(parts, axis=0)

    def product(high, low, right_high, right_low, dims):
        both = dot(stacked(high, low), right_high, dims)
        return both[:HEAD_DIM] + (both[HEAD_DIM:] + dot(high, right_low, dims))

    def some_heads(heads):
        ats = [pl.multiple_of(head * HEAD_DIM, HEAD_DIM) for head, _ in heads]
        q = [halves(proj[pl.ds(at, HEAD_DIM), :] * FACTOR) for at in ats]
        k = [halves(proj[pl.ds(at + WIDTH, HEAD_DIM), :]) for at in ats]
        v = [halves(proj[pl.ds(at + 2 * WIDTH, HEAD_DIM), :]) for at in ats]
        g = [halves(gatt[pl.ds(at, HEAD_DIM), :]) for at in ats]

        def outer(left, right):
            return dot(
                stacked(left[0], left[0], left[1]), stacked(right[0], right[1], right[0]), TN
            )

        scores = [
            outer(q[i], k[i]) + bias[:, slot, :]
            for i, (_, slot) in enumerate(heads)
        ]
        grad_probs = [outer(g[i], v[i]) for i in range(len(heads))]
        scores = [jnp.where(allowed, x, -1000000000.0) for x in scores]
        exponent = [jnp.exp(x - jnp.max(x, axis=1, keepdims=True)) for x in scores]
        probs = [x * (1.0 / jnp.sum(x, axis=1, keepdims=True)) for x in exponent]
        p = [halves(x) for x in probs]
        for i, at in enumerate(ats):
            att[pl.ds(at, HEAD_DIM), :] = product(*v[i], *p[i], NT)
            gproj[pl.ds(at + 2 * WIDTH, HEAD_DIM), :] = product(*g[i], *p[i], NN)
        grad_scores = [
            x * (y - jnp.sum(x * y, axis=1, keepdims=True)) for x, y in zip(probs, grad_probs)
        ]
        s = [halves(x) for x in grad_scores]
        for i, at in enumerate(ats):
            gproj[pl.ds(at, HEAD_DIM), :] = product(*k[i], *s[i], NT) * FACTOR
            gproj[pl.ds(at + WIDTH, HEAD_DIM), :] = product(*q[i], *s[i], NN)
        for i, (_, slot) in enumerate(heads):
            target = send_scores if slot < 8 else keep_scores
            target[0:TOKENS, slot % 8, :] = grad_scores[i][:, :128]
            tails[:, slot, 0:16] = grad_scores[i][:, 128:]

    tails[...] = jnp.zeros_like(tails)
    order = [((1 - core) * 8 + slot, slot) for slot in range(8)]
    order += [(core * 8 + slot, 8 + slot) for slot in range(8)]
    for first in range(0, 16, 4):
        some_heads(order[first : first + 4])

    for i in range(18):
        total = tails[8 * i]
        for j in range(1, 8):
            total = total + pltpu.roll(tails[8 * i + j], 16 * j, 1)
        send_scores[TOKENS + i] = total[0:8]
        keep_scores[TOKENS + i] = total[8:16]

    for target, bit in ((send, 1 - core), (keep, core)):
        rows = [pl.ds(pl.multiple_of(64 * i + 32 * bit, 32), 32) for i in range(8)]
        left = halves(jnp.concatenate([normed_t[r, :] for r in rows], axis=0))
        for part in range(3):
            at = part * WIDTH
            target[:, at : at + WIDTH] = dot3(left, halves(gproj[at : at + WIDTH, :]), NT)
        left = halves(jnp.concatenate([att[r, :] for r in rows], axis=0))
        target[:, 3 * WIDTH :] = dot3(left, halves_cotangent, NN)

    grad_normed = jnp.zeros((WIDTH, TOKENS), F32)
    for part in range(3):
        at = part * WIDTH
        grad_normed = grad_normed + dot3(
            halves(in_weight[:, at : at + WIDTH]), halves(gproj[at : at + WIDTH, :]), NN
        )
    grad_normed = grad_normed.T
    normed = tokens[...]
    result = inv_std * (
        grad_normed
        - jnp.mean(grad_normed, axis=1, keepdims=True)
        - normed * jnp.mean(grad_normed * normed, axis=1, keepdims=True)
    )
    tokens[...] = result
    grad_above[...] = tokens[0:QUAD, :]
    grad_beside[0:QUAD, :] = tokens[QUAD : 2 * QUAD, :]
    grad_own[...] = tokens[2 * QUAD : 3 * QUAD, :]
    grad_beside[QUAD:, :] = tokens[3 * QUAD :, :]


def shape(*dims):
    return jax.ShapeDtypeStruct(dims, F32)


def window(core, own, quad0, quad1, quad3, bias, in_weight, out_weight):
    grad = shape(QUAD, WIDTH)
    return pl.pallas_call(
        main_kernel,
        out_shape=[
            shape(256, 4 * WIDTH),
            shape(256, 4 * WIDTH),
            shape(ROWS, 8, 128),
            shape(ROWS, 8, 128),
            grad,
            grad,
            shape(2 * QUAD, WIDTH),
        ],
        in_specs=[scalar()] + whole(7),
        out_specs=whole(7),
        scratch_shapes=[
            pltpu.VMEM((TOKENS, WIDTH), F32),
            pltpu.VMEM((TOKENS, WIDTH), F32),
            pltpu.VMEM((3 * WIDTH, TOKENS), F32),
            pltpu.VMEM((WIDTH, TOKENS), F32),
            pltpu.VMEM((3 * WIDTH, TOKENS), F32),
            pltpu.VMEM((WIDTH, TOKENS), F32),
            pltpu.VMEM((WIDTH, TOKENS), F32),
            pltpu.VMEM((TOKENS, HEADS, 128), F32),
        ],
        compiler_params=params(26),
        cost_estimate=cost(WINDOW_COST),
        name="window",
    )(core, own, quad0, quad1, quad3, bias, in_weight, out_weight)


def add_pairs(places, keep, came, total):
    lines = line_numbers()

    def sides(row, values):
        block = (row >> 8).astype(F32).astype(BF16)
        both = jnp.concatenate(halves(values), axis=0)
        spread = jnp.broadcast_to(block, (16, 128))
        left = jnp.concatenate(
            [jnp.where(spread == float(b), both, jnp.zeros_like(both)) for b in range(BLOCKS)],
            axis=0,
        )
        return left, one_hot(row, lines)

    def add(rows, base, pair):
        pieces = [
            sides(rows[j : j + 1, :], keep[base + j] + came[base + j])
            for j in (2 * pair, 2 * pair + 1)
        ]
        left = jnp.concatenate([p[0] for p in pieces], axis=1)
        right = jnp.concatenate([p[1] for p in pieces], axis=1)
        total[...] += dot(left, right, NT)

    def step(i, carry):
        base = pl.multiple_of(i * 8, 8)
        rows = places[pl.ds(base, 8), :]
        for pair in range(4):
            add(rows, base, pair)
        return carry

    lax.fori_loop(0, ROWS // 8, step, 0)
    add(places[ROWS - 2 : ROWS, :], ROWS - 2, 0)


def scatter_kernel(core_ref, places, keep, came, mine, other, total, line, sectors):
    total[...] = jnp.zeros_like(total)
    add_pairs(places, keep, came, total)
    for b in range(BLOCKS):
        line[:, b * 256 : b * 256 + 256] = (
            total[b * 16 : b * 16 + 8, :] + total[b * 16 + 8 : b * 16 + 16, :]
        )
    line[:, BLOCKS * 256 :] = jnp.zeros((8, 256), F32)
    for m in range(32):
        chip, core, half = m // 4, m // 2 % 2, m % 2
        start_at = m * HALF_SECTOR
        base, shift = start_at // 128 * 128, start_at % 128
        piece = line[:, base : base + 512]
        if shift:
            piece = pltpu.roll(piece, 512 - shift, 1)
        sectors[core, chip, half * 8 : half * 8 + 8, :] = piece[:, :256]
    mine[...] = sectors[core_ref[0]]
    other[...] = sectors[1 - core_ref[0]]


def scatter(core, places, keep, came):
    return pl.pallas_call(
        scatter_kernel,
        out_shape=[shape(8, 16, 256)] * 2,
        in_specs=[scalar()] + whole(3),
        out_specs=whole(2),
        scratch_shapes=[
            pltpu.VMEM((BLOCKS * 16, 256), F32),
            pltpu.VMEM((8, BLOCKS * 256 + 256), F32),
            pltpu.VMEM((2, 8, 16, 256), F32),
        ],
        compiler_params=params(),
        cost_estimate=cost(SCATTER_COST),
        name="scatter",
    )(core, places, keep, came)


def split_kernel(odd, keep, came, own, send_a, send_b):
    def columns(bit):
        cols = slice(512 * bit, 512 * bit + 512)
        return keep[:, cols] + came[:, cols]

    for bit in range(2):

        @pl.when(odd[0] == bit)
        def _():
            send_a[...] = columns(1 - bit)
            send_b[...] = columns(2 + bit)
            own[:, 0:512] = columns(bit)
            own[:, 512:1024] = columns(3 - bit)


def split(odd, keep, came):
    return pl.pallas_call(
        split_kernel,
        out_shape=[shape(256, 1024), shape(256, 512), shape(256, 512)],
        in_specs=[scalar()] + whole(2),
        out_specs=whole(3),
        compiler_params=params(),
        name="split",
    )(odd, keep, came)


def join_kernel(core_ref, own, came_a, came_b, table_keep, table_came, out):
    for i in range(8):
        rows = slice(i * 32, i * 32 + 32)
        out[i, :, 0:512] = own[rows, 0:512] + came_a[rows, :]
        out[i, :, 512:1024] = own[rows, 512:1024] + came_b[rows, :]
    first = core_ref[0] == 0
    mine, other = table_keep[...], table_came[...]
    out[:, 0:16, 1024:] = jnp.where(first, mine, other)
    out[:, 16:32, 1024:] = jnp.where(first, other, mine)


def join(core, *parts):
    return pl.pallas_call(
        join_kernel,
        out_shape=shape(8, 32, 1280),
        in_specs=[scalar()] + whole(5),
        out_specs=pl.BlockSpec(memory_space=pltpu.VMEM),
        compiler_params=params(),
        name="join",
    )(core, *parts)


def fold_lon_kernel(parts, out, total):
    value = parts[0]
    for i in range(1, 8):
        value = value + parts[i]
    total[...] = value
    for i in range(8):
        out[i] = total[4 * i : 4 * i + 4, :]


def fold_lon(parts):
    return pl.pallas_call(
        fold_lon_kernel,
        out_shape=shape(8, 4, 1280),
        in_specs=whole(1),
        out_specs=pl.BlockSpec(memory_space=pltpu.VMEM),
        scratch_shapes=[pltpu.VMEM((32, 1280), F32)],
        compiler_params=params(),
        name="fold_lon",
    )(parts)


def fold_lat_kernel(parts, out):
    total = parts[0]
    for i in range(1, 8):
        total = total + parts[i]
    for i in range(16):
        out[i] = total


def fold_lat(parts):
    return pl.pallas_call(
        fold_lat_kernel,
        out_shape=shape(16, 4, 1280),
        in_specs=whole(1),
        out_specs=pl.BlockSpec(memory_space=pltpu.VMEM),
        compiler_params=params(),
        name="fold_lat",
    )(parts)


def unpack_kernel(parts, grad_in, grad_out, grad_bias, table):
    for rank in range(8):
        rows = slice(4 * rank, 4 * rank + 4)
        even = (rank // 2) * 4 + rank % 2
        odd = even + 2
        grad_in[rows, 0:512] = parts[even, :, 0:512]
        grad_in[rows, 512:1024] = parts[odd, :, 0:512]
        grad_in[rows, 1024:1536] = parts[odd, :, 512:1024]
        grad_out[rows, :] = parts[even, :, 512:1024]
        table[rows, :] = parts[even, :, 1024:] + parts[odd, :, 1024:]
    for core in range(2):
        for half in range(2):
            base = core * 16 + half * 8
            grad_bias[core * 8 : core * 8 + 8, half * HALF_SECTOR : (half + 1) * HALF_SECTOR] = (
                table[base : base + 8, :HALF_SECTOR]
            )


def unpack(parts):
    return pl.pallas_call(
        unpack_kernel,
        out_shape=[shape(32, 3 * WIDTH), shape(32, WIDTH), shape(HEADS, 2 * HALF_SECTOR)],
        in_specs=whole(1),
        out_specs=whole(3),
        scratch_shapes=[pltpu.VMEM((32, 256), F32)],
        compiler_params=params(),
        name="unpack",
    )(parts)


def place_kernel(grad_out, own, beside, below, out):
    plan = ((own, 0, 0, 3), (beside, QUAD, 0, 0), (below, 0, 6, 3), (below, QUAD, 6, 0))
    for ref, base, row0, col0 in plan:
        for row in range(6):
            for col in range(3):
                spot = base + row * 6 + col * 2
                out[row0 + row, col0 + col] = (
                    grad_out[row0 + row, col0 + col] + ref[spot : spot + 2, :]
                )


def place(grad_out, own, beside, below):
    return pl.pallas_call(
        place_kernel,
        out_shape=jax.ShapeDtypeStruct(grad_out.shape, F32),
        in_specs=whole(4),
        out_specs=pl.BlockSpec(memory_space=pltpu.VMEM),
        compiler_params=params(),
        name="place",
    )(grad_out, own, beside, below)


LAT = ("z", "y_lo")
LON = ("x", "y_hi", "core")


def body(fields, grad_out, region_ids, bias_index, bias_table, in_weight, out_weight):
    everything = LAT + LON
    lat = lax.axis_index(LAT)
    core = lax.axis_index("core").reshape(1)
    odd = lax.rem(lax.axis_index("z"), 2).reshape(1)

    def moves(down, right):
        return [
            (i * 16 + j, (i + down) % 16 * 16 + (j + right) % 16)
            for i in range(16)
            for j in range(16)
        ]

    swap = [(0, 1), (1, 0)]
    last = jnp.where(lat == 15, 3, 0).reshape(1)
    grad_out = jnp.transpose(grad_out, (1, 2, 0, 3))
    own, left, below, corner = pack(
        last, jnp.transpose(fields, (1, 2, 0, 3)), grad_out, jnp.transpose(region_ids, (2, 0, 1))
    )
    quad3 = lax.ppermute(left, everything, moves(0, -1))
    quad0 = lax.ppermute(below, everything, moves(1, 0))
    quad1 = lax.ppermute(corner, everything, moves(1, -1))
    bias, places = lookup(core, bias_index, bias_table)
    keep, send, keep_scores, send_scores, grad_above, grad_own, grad_beside = window(
        core, own, quad0, quad1, quad3, bias, in_weight, out_weight
    )
    came = lax.ppermute(send, "core", swap)
    came_scores = lax.ppermute(send_scores, "core", swap)
    part, send_a, send_b = split(odd, keep, came)
    came_a = lax.ppermute(send_a, "z", [(i, i ^ 1) for i in range(8)])
    came_b = lax.ppermute(send_b, "z", [(i, ((i + 1) % 8 ^ 1) + 7 & 7) for i in range(8)])
    part, places = lax.optimization_barrier((part, places))
    mine, other = scatter(core, places, keep_scores, came_scores)
    came_table = lax.ppermute(other, "core", swap)
    grad_beside, mine = lax.optimization_barrier((grad_beside, mine))
    back_beside = lax.ppermute(grad_beside, everything, moves(0, 1))
    joined = join(core, part, came_a, came_b, mine, came_table)
    parts = lax.all_to_all(joined, ("x", "y_hi"), 0, 0)
    parts, back_beside = lax.optimization_barrier((parts, back_beside))
    back_below = lax.ppermute(
        stack(grad_above, (0, QUAD), back_beside, (0, QUAD)), everything, moves(-1, 0)
    )
    parity = [[z * 2 + y for z in range(bit, 8, 2) for y in range(2)] for bit in range(2)]
    parts = lax.all_to_all(fold_lon(parts), LAT, 0, 0, axis_index_groups=parity)
    parts = lax.all_to_all(fold_lat(parts), LAT, 0, 0)
    parts, back_below = lax.optimization_barrier((parts, back_below))
    grad_fields = place(grad_out, grad_own, back_beside, back_below)
    grad_in_weight, grad_out_weight, grad_bias = unpack(parts)
    return jnp.transpose(grad_fields, (2, 0, 1, 3)), grad_in_weight, grad_out_weight, grad_bias.T


def solution(mesh):
    split = Mesh(mesh.devices.reshape(8, 2, 4, 2, 2), LAT + LON)
    tokens = P(None, LAT, LON, None)
    in_specs = (tokens, tokens, P(None, LAT, LON), P(), P(), P(), P())
    out_specs = (tokens, P(LON, None), P(LON, None), P(LON, None))
    return jax.shard_map(body, mesh=split, in_specs=in_specs, out_specs=out_specs, check_vma=False)
```

```python
import jax
import jax.numpy as jnp
from jax import lax
from jax.experimental import pallas as pl
from jax.experimental.pallas import tpu as pltpu
from jax.sharding import Mesh
from jax.sharding import PartitionSpec as P

WIDTH = 512
HEADS = 16
HEAD_DIM = 32
TOKENS = 144
QUAD = 36
BIAS_ROWS = 6336
HALF_SECTOR = 198
BLOCKS = 25
PACK_MIB = 56
ROWS = 162
LOOKUP_COST = 13
WINDOW_COST = 0
SCATTER_COST = 9
FACTOR = HEAD_DIM ** (-0.5)
F32 = jnp.float32
BF16 = jnp.bfloat16
MEGA = 1 << 20


def params(mib=16):
    return pltpu.CompilerParams(vmem_limit_bytes=mib * MEGA)


def cost(micros):
    return pl.CostEstimate(flops=int(micros * 1e9), bytes_accessed=0, transcendentals=0)


def whole(count):
    return [pl.BlockSpec(memory_space=pltpu.VMEM)] * count


def scalar():
    return pl.BlockSpec(memory_space=pltpu.SMEM)


def halves(x):
    high = x.astype(BF16)
    low = (x - high.astype(F32)).astype(BF16)
    return high, low


def dot(a, b, dims):
    return lax.dot_general(a, b, (dims, ((), ())), preferred_element_type=F32)


NN = ((1,), (0,))
NT = ((1,), (1,))
TN = ((0,), (0,))


def dot3(a, b, dims):
    ah, al = a
    bh, bl = b
    return dot(ah, bh, dims) + (dot(ah, bl, dims) + dot(al, bh, dims))


def token_order():
    place = lax.broadcasted_iota(jnp.int32, (TOKENS, TOKENS), 0)
    token = lax.broadcasted_iota(jnp.int32, (TOKENS, TOKENS), 1)

    def steps(value, size, count):
        total = jnp.zeros_like(value)
        for i in range(1, count):
            total = total + jnp.where(value >= i * size, 1, 0)
        return total

    quad = steps(place, QUAD, 4)
    rest = place - QUAD * quad
    row = steps(rest, 6, 6)
    rest = rest - 6 * row
    col = steps(rest, 2, 3)
    level = rest - 2 * col
    row_half = steps(quad, 2, 2)
    col_half = quad - 2 * row_half
    source = level * 72 + (6 * row_half + row) * 6 + 3 * col_half + col
    return jnp.where(source == token, 1.0, 0.0).astype(BF16)


def pack_kernel(last, fields, grads, ids, own, left, below, corner):
    lanes = lax.broadcasted_iota(jnp.int32, (2, WIDTH), 1)
    level = lax.broadcasted_iota(jnp.int32, (2, WIDTH), 0)
    bump = last[0]
    plan = (
        (own, 0, 3, 2, None),
        (left, 0, 0, 3, None),
        (below, 6, 3, 0, bump),
        (corner, 6, 0, 1, bump),
    )
    for ref, row0, col0, quadrant, offset in plan:
        label = jnp.zeros((2, WIDTH), jnp.int32)
        for row in range(6):
            for col in range(3):
                spot = row * 6 + col * 2
                ref[spot : spot + 2, :] = fields[row0 + row, col0 + col]
                ref[QUAD + spot : QUAD + spot + 2, :] = grads[row0 + row, col0 + col]
                value = ids[col0 + col, :, row0 + row : row0 + row + 1] + 1
                if offset is not None:
                    value = value + offset
                place = quadrant * QUAD + spot
                label = jnp.where(
                    lanes == level + place, jnp.broadcast_to(value, (2, WIDTH)), label
                )
        total = jnp.sum(label.astype(F32), axis=0, keepdims=True)
        ref[72:80, :] = jnp.broadcast_to(total, (8, WIDTH))


def pack(last, fields, grads, ids):
    shape = jax.ShapeDtypeStruct((80, WIDTH), F32)
    return pl.pallas_call(
        pack_kernel,
        out_shape=[shape] * 4,
        in_specs=[scalar()] + whole(3),
        out_specs=whole(4),
        compiler_params=params(PACK_MIB),
        cost_estimate=cost(1),
        name="pack",
    )(last, fields, grads, ids)


def one_hot(row, lines):
    low = (row & 255).astype(F32).astype(BF16)
    hit = lines == jnp.broadcast_to(low, (256, 128))
    return jnp.where(hit, jnp.ones((256, 128), BF16), jnp.zeros((256, 128), BF16))


def line_numbers():
    return lax.broadcasted_iota(jnp.int32, (256, 128), 0).astype(F32).astype(BF16)


def lookup_kernel(core_ref, index, table, bias, places, left):
    value = index[...]
    high = (value >> 7).astype(F32).astype(BF16)
    low = (value & 127).astype(F32).astype(BF16)
    move = token_order()

    def moved(part):
        return dot(dot(move, part, NN).astype(BF16), move, NT)

    result = moved(high) * 128.0 + moved(low)
    places[0:TOKENS, :] = result[:, :128].astype(jnp.int32)
    tail = jnp.concatenate([result[:, 128:], jnp.zeros((TOKENS, 112), F32)], axis=1)
    for i in range(18):
        spread = pltpu.roll(tail[8 * i : 8 * i + 8, :], 0, 1, stride=16, stride_axis=0)
        places[TOKENS + i : TOKENS + i + 1, :] = jnp.sum(spread, axis=0, keepdims=True).astype(jnp.int32)

    first = core_ref[0] == 0
    for block in range(BLOCKS):
        count = min(256, BIAS_ROWS - block * 256)
        top = table[0:8, block * 256 : block * 256 + count]
        bottom = table[8:16, block * 256 : block * 256 + count]
        part = jnp.concatenate(
            [jnp.where(first, bottom, top), jnp.where(first, top, bottom)], axis=0
        )
        if count < 256:
            part = jnp.concatenate([part, jnp.zeros((16, 256 - count), F32)], axis=1)
        left[block * 32 : block * 32 + 16, :], left[block * 32 + 16 : block * 32 + 32, :] = halves(
            part
        )
    lines = line_numbers()
    matrix = left[...]

    def find(rows):
        right = jnp.concatenate([one_hot(row, lines) for row in rows], axis=1)
        found = dot(matrix, right, NN)
        block = jnp.concatenate([row >> 8 for row in rows], axis=1)
        block = jnp.broadcast_to(block, (32, 256))
        total = jnp.zeros((32, 256), F32)
        for b in range(BLOCKS):
            total = jnp.where(block == b, found[b * 32 : b * 32 + 32], total)
        return total[:16] + total[16:]

    def step(i, carry):
        base = pl.multiple_of(i * 8, 8)
        rows = places[pl.ds(base, 8), :]
        for pair in range(4):
            found = find([rows[2 * pair + j : 2 * pair + j + 1, :] for j in range(2)])
            for j in range(2):
                bias[base + 2 * pair + j, :, 0:128] = found[:, j * 128 : j * 128 + 128]
        return carry

    lax.fori_loop(0, 18, step, 0)
    for pair in range(9):
        at = TOKENS + 2 * pair
        found = find([places[at + j : at + j + 1, :] for j in range(2)])
        for j in range(16):
            bias[16 * pair + j, :, 128:144] = found[:, 16 * j : 16 * j + 16]


def lookup(core, bias_index, bias_table):
    return pl.pallas_call(
        lookup_kernel,
        out_shape=[
            jax.ShapeDtypeStruct((TOKENS, HEADS, TOKENS), F32),
            jax.ShapeDtypeStruct((ROWS, 128), jnp.int32),
        ],
        in_specs=[scalar()] + whole(2),
        out_specs=whole(2),
        scratch_shapes=[pltpu.VMEM((BLOCKS * 32, 256), BF16)],
        compiler_params=params(),
        cost_estimate=cost(LOOKUP_COST),
        name="lookup",
    )(core, bias_index, bias_table.T)


def main_kernel(
    core_ref,
    own,
    quad0,
    quad1,
    quad3,
    bias,
    in_weight,
    out_weight,
    keep,
    send,
    keep_scores,
    send_scores,
    grad0,
    grad1,
    grad2,
    grad3,
    tokens,
    cotangent,
    proj,
    gatt,
    gproj,
    att,
    normed_t,
    tails,
):
    core = core_ref[0]
    row = jnp.zeros((1, WIDTH), F32)
    for slot, (quad, start) in enumerate(((quad0, 0), (quad1, 0), (own, 0), (quad3, 0))):
        at = slot * QUAD
        tokens[at : at + QUAD, :] = quad[start : start + QUAD, :]
        cotangent[at : at + QUAD, :] = quad[start + QUAD : start + 2 * QUAD, :]
        row = row + quad[start + 72 : start + 73, :]
    row = row[:, :TOKENS]
    side = lax.broadcasted_iota(jnp.int32, (TOKENS, TOKENS), 0)
    along = lax.broadcasted_iota(jnp.int32, (TOKENS, TOKENS), 1)
    spread = jnp.broadcast_to(row, (TOKENS, TOKENS))
    column = jnp.sum(jnp.where(side == along, spread, 0.0), axis=1, keepdims=True)
    allowed = column == spread

    inputs = tokens[...]
    centered = inputs - jnp.mean(inputs, axis=1, keepdims=True)
    variance = jnp.mean(centered * centered, axis=1, keepdims=True)
    inv_std = lax.rsqrt(variance + 1e-05)
    normed = centered * inv_std
    tokens[...] = normed
    normed_t[...] = normed.T
    halves_normed = halves(normed)
    for part in range(3):
        at = part * WIDTH
        weight = halves(in_weight[:, at : at + WIDTH])
        proj[at : at + WIDTH, :] = dot3(halves_normed, weight, NN).T
    halves_cotangent = halves(cotangent[...])
    gatt[...] = dot3(halves(out_weight[...]), halves_cotangent, NT)

    def stacked(*parts):
        return jnp.concatenate(parts, axis=0)

    def product(high, low, right_high, right_low, dims):
        both = dot(stacked(high, low), right_high, dims)
        return both[:HEAD_DIM] + (both[HEAD_DIM:] + dot(high, right_low, dims))

    def some_heads(heads):
        ats = [pl.multiple_of(head * HEAD_DIM, HEAD_DIM) for head, _ in heads]
        q = [halves(proj[pl.ds(at, HEAD_DIM), :] * FACTOR) for at in ats]
        k = [halves(proj[pl.ds(at + WIDTH, HEAD_DIM), :]) for at in ats]
        v = [halves(proj[pl.ds(at + 2 * WIDTH, HEAD_DIM), :]) for at in ats]
        g = [halves(gatt[pl.ds(at, HEAD_DIM), :]) for at in ats]

        def outer(left, right):
            return dot(
                stacked(left[0], left[0], left[1]), stacked(right[0], right[1], right[0]), TN
            )

        scores = [
            outer(q[i], k[i]) + bias[:, slot, :]
            for i, (_, slot) in enumerate(heads)
        ]
        grad_probs = [outer(g[i], v[i]) for i in range(len(heads))]
        scores = [jnp.where(allowed, x, -1000000000.0) for x in scores]
        exponent = [jnp.exp(x - jnp.max(x, axis=1, keepdims=True)) for x in scores]
        probs = [x * (1.0 / jnp.sum(x, axis=1, keepdims=True)) for x in exponent]
        p = [halves(x) for x in probs]
        for i, at in enumerate(ats):
            att[pl.ds(at, HEAD_DIM), :] = product(*v[i], *p[i], NT)
            gproj[pl.ds(at + 2 * WIDTH, HEAD_DIM), :] = product(*g[i], *p[i], NN)
        grad_scores = [
            x * (y - jnp.sum(x * y, axis=1, keepdims=True)) for x, y in zip(probs, grad_probs)
        ]
        s = [halves(x) for x in grad_scores]
        for i, at in enumerate(ats):
            gproj[pl.ds(at, HEAD_DIM), :] = product(*k[i], *s[i], NT) * FACTOR
            gproj[pl.ds(at + WIDTH, HEAD_DIM), :] = product(*q[i], *s[i], NN)
        for i, (_, slot) in enumerate(heads):
            target = send_scores if slot < 8 else keep_scores
            target[0:TOKENS, slot % 8, :] = grad_scores[i][:, :128]
            tails[:, slot, 0:16] = grad_scores[i][:, 128:]

    tails[...] = jnp.zeros_like(tails)
    order = [((1 - core) * 8 + slot, slot) for slot in range(8)]
    order += [(core * 8 + slot, 8 + slot) for slot in range(8)]
    for first in range(0, 16, 4):
        some_heads(order[first : first + 4])

    for i in range(18):
        total = tails[8 * i]
        for j in range(1, 8):
            total = total + pltpu.roll(tails[8 * i + j], 16 * j, 1)
        send_scores[TOKENS + i] = total[0:8]
        keep_scores[TOKENS + i] = total[8:16]

    for target, bit in ((send, 1 - core), (keep, core)):
        rows = [pl.ds(pl.multiple_of(64 * i + 32 * bit, 32), 32) for i in range(8)]
        left = halves(jnp.concatenate([normed_t[r, :] for r in rows], axis=0))
        for part in range(3):
            at = part * WIDTH
            target[:, at : at + WIDTH] = dot3(left, halves(gproj[at : at + WIDTH, :]), NT)
        left = halves(jnp.concatenate([att[r, :] for r in rows], axis=0))
        target[:, 3 * WIDTH :] = dot3(left, halves_cotangent, NN)

    grad_normed = jnp.zeros((WIDTH, TOKENS), F32)
    for part in range(3):
        at = part * WIDTH
        grad_normed = grad_normed + dot3(
            halves(in_weight[:, at : at + WIDTH]), halves(gproj[at : at + WIDTH, :]), NN
        )
    grad_normed = grad_normed.T
    normed = tokens[...]
    result = inv_std * (
        grad_normed
        - jnp.mean(grad_normed, axis=1, keepdims=True)
        - normed * jnp.mean(grad_normed * normed, axis=1, keepdims=True)
    )
    tokens[...] = result
    for slot, target in enumerate((grad0, grad1, grad2, grad3)):
        target[...] = tokens[slot * QUAD : slot * QUAD + QUAD, :]


def shape(*dims):
    return jax.ShapeDtypeStruct(dims, F32)


def window(core, own, quad0, quad1, quad3, bias, in_weight, out_weight):
    grad = shape(QUAD, WIDTH)
    return pl.pallas_call(
        main_kernel,
        out_shape=[
            shape(256, 4 * WIDTH),
            shape(256, 4 * WIDTH),
            shape(ROWS, 8, 128),
            shape(ROWS, 8, 128),
            grad,
            grad,
            grad,
            grad,
        ],
        in_specs=[scalar()] + whole(7),
        out_specs=whole(8),
        scratch_shapes=[
            pltpu.VMEM((TOKENS, WIDTH), F32),
            pltpu.VMEM((TOKENS, WIDTH), F32),
            pltpu.VMEM((3 * WIDTH, TOKENS), F32),
            pltpu.VMEM((WIDTH, TOKENS), F32),
            pltpu.VMEM((3 * WIDTH, TOKENS), F32),
            pltpu.VMEM((WIDTH, TOKENS), F32),
            pltpu.VMEM((WIDTH, TOKENS), F32),
            pltpu.VMEM((TOKENS, HEADS, 128), F32),
        ],
        compiler_params=params(26),
        cost_estimate=cost(WINDOW_COST),
        name="window",
    )(core, own, quad0, quad1, quad3, bias, in_weight, out_weight)


def add_pairs(places, keep, came, total):
    lines = line_numbers()

    def sides(row, values):
        block = (row >> 8).astype(F32).astype(BF16)
        both = jnp.concatenate(halves(values), axis=0)
        spread = jnp.broadcast_to(block, (16, 128))
        left = jnp.concatenate(
            [jnp.where(spread == float(b), both, jnp.zeros_like(both)) for b in range(BLOCKS)],
            axis=0,
        )
        return left, one_hot(row, lines)

    def add(rows, base, pair):
        pieces = [
            sides(rows[j : j + 1, :], keep[base + j] + came[base + j])
            for j in (2 * pair, 2 * pair + 1)
        ]
        left = jnp.concatenate([p[0] for p in pieces], axis=1)
        right = jnp.concatenate([p[1] for p in pieces], axis=1)
        total[...] += dot(left, right, NT)

    def step(i, carry):
        base = pl.multiple_of(i * 8, 8)
        rows = places[pl.ds(base, 8), :]
        for pair in range(4):
            add(rows, base, pair)
        return carry

    lax.fori_loop(0, ROWS // 8, step, 0)
    add(places[ROWS - 2 : ROWS, :], ROWS - 2, 0)


def scatter_kernel(core_ref, places, keep, came, mine, other, total, line, sectors):
    total[...] = jnp.zeros_like(total)
    add_pairs(places, keep, came, total)
    for b in range(BLOCKS):
        line[:, b * 256 : b * 256 + 256] = (
            total[b * 16 : b * 16 + 8, :] + total[b * 16 + 8 : b * 16 + 16, :]
        )
    line[:, BLOCKS * 256 :] = jnp.zeros((8, 256), F32)
    for m in range(32):
        chip, core, half = m // 4, m // 2 % 2, m % 2
        start_at = m * HALF_SECTOR
        base, shift = start_at // 128 * 128, start_at % 128
        piece = line[:, base : base + 512]
        if shift:
            piece = pltpu.roll(piece, 512 - shift, 1)
        sectors[core, chip, half * 8 : half * 8 + 8, :] = piece[:, :256]
    mine[...] = sectors[core_ref[0]]
    other[...] = sectors[1 - core_ref[0]]


def scatter(core, places, keep, came):
    return pl.pallas_call(
        scatter_kernel,
        out_shape=[shape(8, 16, 256)] * 2,
        in_specs=[scalar()] + whole(3),
        out_specs=whole(2),
        scratch_shapes=[
            pltpu.VMEM((BLOCKS * 16, 256), F32),
            pltpu.VMEM((8, BLOCKS * 256 + 256), F32),
            pltpu.VMEM((2, 8, 16, 256), F32),
        ],
        compiler_params=params(),
        cost_estimate=cost(SCATTER_COST),
        name="scatter",
    )(core, places, keep, came)


def split_kernel(odd, keep, came, own, send_a, send_b):
    def columns(bit):
        cols = slice(512 * bit, 512 * bit + 512)
        return keep[:, cols] + came[:, cols]

    for bit in range(2):

        @pl.when(odd[0] == bit)
        def _():
            send_a[...] = columns(1 - bit)
            send_b[...] = columns(2 + bit)
            own[:, 0:512] = columns(bit)
            own[:, 512:1024] = columns(3 - bit)


def split(odd, keep, came):
    def rows(width):
        return pl.BlockSpec((64, width), lambda i: (i, 0))

    return pl.pallas_call(
        split_kernel,
        out_shape=[shape(256, 1024), shape(256, 512), shape(256, 512)],
        grid=(4,),
        in_specs=[scalar(), rows(2048), rows(2048)],
        out_specs=[rows(1024), rows(512), rows(512)],
        compiler_params=params(),
        name="split",
    )(odd, keep, came)


def join_kernel(core_ref, own, came_a, came_b, table_keep, table_came, out):
    for i in range(8):
        rows = slice(i * 32, i * 32 + 32)
        out[i, :, 0:512] = own[rows, 0:512] + came_a[rows, :]
        out[i, :, 512:1024] = own[rows, 512:1024] + came_b[rows, :]
    first = core_ref[0] == 0
    mine, other = table_keep[...], table_came[...]
    out[:, 0:16, 1024:] = jnp.where(first, mine, other)
    out[:, 16:32, 1024:] = jnp.where(first, other, mine)


def join(core, *parts):
    return pl.pallas_call(
        join_kernel,
        out_shape=shape(8, 32, 1280),
        in_specs=[scalar()] + whole(5),
        out_specs=pl.BlockSpec(memory_space=pltpu.VMEM),
        compiler_params=params(),
        name="join",
    )(core, *parts)


def fold_lon_kernel(parts, out, total):
    value = parts[0]
    for i in range(1, 8):
        value = value + parts[i]
    total[...] = value
    for i in range(8):
        out[i] = total[4 * i : 4 * i + 4, :]


def fold_lon(parts):
    return pl.pallas_call(
        fold_lon_kernel,
        out_shape=shape(8, 4, 1280),
        in_specs=whole(1),
        out_specs=pl.BlockSpec(memory_space=pltpu.VMEM),
        scratch_shapes=[pltpu.VMEM((32, 1280), F32)],
        compiler_params=params(),
        name="fold_lon",
    )(parts)


def fold_lat_kernel(parts, out):
    total = parts[0]
    for i in range(1, 8):
        total = total + parts[i]
    for i in range(16):
        out[i] = total


def fold_lat(parts):
    return pl.pallas_call(
        fold_lat_kernel,
        out_shape=shape(16, 4, 1280),
        in_specs=whole(1),
        out_specs=pl.BlockSpec(memory_space=pltpu.VMEM),
        compiler_params=params(),
        name="fold_lat",
    )(parts)


def unpack_kernel(parts, grad_in, grad_out, grad_bias, table):
    for rank in range(8):
        rows = slice(4 * rank, 4 * rank + 4)
        even = (rank // 2) * 4 + rank % 2
        odd = even + 2
        grad_in[rows, 0:512] = parts[even, :, 0:512]
        grad_in[rows, 512:1024] = parts[odd, :, 0:512]
        grad_in[rows, 1024:1536] = parts[odd, :, 512:1024]
        grad_out[rows, :] = parts[even, :, 512:1024]
        table[rows, :] = parts[even, :, 1024:] + parts[odd, :, 1024:]
    for core in range(2):
        for half in range(2):
            base = core * 16 + half * 8
            grad_bias[core * 8 : core * 8 + 8, half * HALF_SECTOR : (half + 1) * HALF_SECTOR] = (
                table[base : base + 8, :HALF_SECTOR]
            )


def unpack(parts):
    return pl.pallas_call(
        unpack_kernel,
        out_shape=[shape(32, 3 * WIDTH), shape(32, WIDTH), shape(HEADS, 2 * HALF_SECTOR)],
        in_specs=whole(1),
        out_specs=whole(3),
        scratch_shapes=[pltpu.VMEM((32, 256), F32)],
        compiler_params=params(),
        name="unpack",
    )(parts)


def place_kernel(grad_out, own, left, below, corner, out):
    for ref, row0, col0 in ((own, 0, 3), (left, 0, 0), (below, 6, 3), (corner, 6, 0)):
        for row in range(6):
            for col in range(3):
                spot = row * 6 + col * 2
                out[row0 + row, col0 + col] = (
                    grad_out[row0 + row, col0 + col] + ref[spot : spot + 2, :]
                )


def place(grad_out, own, left, below, corner):
    return pl.pallas_call(
        place_kernel,
        out_shape=jax.ShapeDtypeStruct(grad_out.shape, F32),
        in_specs=whole(5),
        out_specs=pl.BlockSpec(memory_space=pltpu.VMEM),
        compiler_params=params(),
        name="place",
    )(grad_out, own, left, below, corner)


LAT = ("z", "y_lo")
LON = ("x", "y_hi", "core")


def body(fields, grad_out, region_ids, bias_index, bias_table, in_weight, out_weight):
    everything = LAT + LON
    lat = lax.axis_index(LAT)
    core = lax.axis_index("core").reshape(1)
    odd = lax.rem(lax.axis_index("z"), 2).reshape(1)

    def moves(down, right):
        return [
            (i * 16 + j, (i + down) % 16 * 16 + (j + right) % 16)
            for i in range(16)
            for j in range(16)
        ]

    swap = [(0, 1), (1, 0)]
    last = jnp.where(lat == 15, 3, 0).reshape(1)
    grad_out = jnp.transpose(grad_out, (1, 2, 0, 3))
    own, left, below, corner = pack(
        last, jnp.transpose(fields, (1, 2, 0, 3)), grad_out, jnp.transpose(region_ids, (2, 0, 1))
    )
    quad3 = lax.ppermute(left, everything, moves(0, -1))
    quad0 = lax.ppermute(below, everything, moves(1, 0))
    quad1 = lax.ppermute(corner, everything, moves(1, -1))
    bias, places = lookup(core, bias_index, bias_table)
    keep, send, keep_scores, send_scores, grad0, grad1, grad2, grad3 = window(
        core, own, quad0, quad1, quad3, bias, in_weight, out_weight
    )
    came = lax.ppermute(send, "core", swap)
    came_scores = lax.ppermute(send_scores, "core", swap)
    back = (
        lax.ppermute(grad3, everything, moves(0, 1)),
        lax.ppermute(grad0, everything, moves(-1, 0)),
        lax.ppermute(grad1, everything, moves(-1, 1)),
    )
    part, send_a, send_b = split(odd, keep, came)
    came_a = lax.ppermute(send_a, "z", [(i, i ^ 1) for i in range(8)])
    came_b = lax.ppermute(send_b, "z", [(i, ((i + 1) % 8 ^ 1) + 7 & 7) for i in range(8)])
    part, places, back = lax.optimization_barrier((part, places, back))
    mine, other = scatter(core, places, keep_scores, came_scores)
    came_table = lax.ppermute(other, "core", swap)
    mine, grad2 = lax.optimization_barrier((mine, grad2))
    grad_fields = place(grad_out, grad2, *back)
    part, grad_fields = lax.optimization_barrier((part, grad_fields))
    joined = join(core, part, came_a, came_b, mine, came_table)
    parts = lax.all_to_all(joined, ("x", "y_hi"), 0, 0)
    parity = [[z * 2 + y for z in range(bit, 8, 2) for y in range(2)] for bit in range(2)]
    parts = lax.all_to_all(fold_lon(parts), LAT, 0, 0, axis_index_groups=parity)
    parts = lax.all_to_all(fold_lat(parts), LAT, 0, 0)
    grad_in_weight, grad_out_weight, grad_bias = unpack(parts)
    return jnp.transpose(grad_fields, (2, 0, 1, 3)), grad_in_weight, grad_out_weight, grad_bias.T


def solution(mesh):
    split = Mesh(mesh.devices.reshape(8, 2, 4, 2, 2), LAT + LON)
    tokens = P(None, LAT, LON, None)
    in_specs = (tokens, tokens, P(None, LAT, LON), P(), P(), P(), P())
    out_specs = (tokens, P(LON, None), P(LON, None), P(LON, None))
    return jax.shard_map(body, mesh=split, in_specs=in_specs, out_specs=out_specs, check_vma=False)
```

```python
import jax
import jax.numpy as jnp
from jax import lax
from jax.experimental import pallas as pl
from jax.experimental.pallas import tpu as pltpu
from jax.sharding import Mesh
from jax.sharding import PartitionSpec as P

WIDTH = 512
HEADS = 16
HEAD_DIM = 32
TOKENS = 144
QUAD = 36
BIAS_ROWS = 6336
HALF_SECTOR = 198
BLOCKS = 25
PACK_MIB = 56
ROWS = 162
LOOKUP_COST = 13
WINDOW_COST = 0
SCATTER_COST = 9
FACTOR = HEAD_DIM ** (-0.5)
F32 = jnp.float32
BF16 = jnp.bfloat16
MEGA = 1 << 20


def params(mib=16):
    return pltpu.CompilerParams(vmem_limit_bytes=mib * MEGA)


def cost(micros):
    return pl.CostEstimate(flops=int(micros * 1e9), bytes_accessed=0, transcendentals=0)


def whole(count):
    return [pl.BlockSpec(memory_space=pltpu.VMEM)] * count


def scalar():
    return pl.BlockSpec(memory_space=pltpu.SMEM)


def halves(x):
    high = x.astype(BF16)
    low = (x - high.astype(F32)).astype(BF16)
    return high, low


def dot(a, b, dims):
    return lax.dot_general(a, b, (dims, ((), ())), preferred_element_type=F32)


NN = ((1,), (0,))
NT = ((1,), (1,))
TN = ((0,), (0,))


def dot3(a, b, dims):
    ah, al = a
    bh, bl = b
    return dot(ah, bh, dims) + (dot(ah, bl, dims) + dot(al, bh, dims))


def token_order():
    place = lax.broadcasted_iota(jnp.int32, (TOKENS, TOKENS), 0)
    token = lax.broadcasted_iota(jnp.int32, (TOKENS, TOKENS), 1)

    def steps(value, size, count):
        total = jnp.zeros_like(value)
        for i in range(1, count):
            total = total + jnp.where(value >= i * size, 1, 0)
        return total

    quad = steps(place, QUAD, 4)
    rest = place - QUAD * quad
    row = steps(rest, 6, 6)
    rest = rest - 6 * row
    col = steps(rest, 2, 3)
    level = rest - 2 * col
    row_half = steps(quad, 2, 2)
    col_half = quad - 2 * row_half
    source = level * 72 + (6 * row_half + row) * 6 + 3 * col_half + col
    return jnp.where(source == token, 1.0, 0.0).astype(BF16)


def pack_kernel(last, fields, grads, ids, own, left, below, corner):
    lanes = lax.broadcasted_iota(jnp.int32, (2, WIDTH), 1)
    level = lax.broadcasted_iota(jnp.int32, (2, WIDTH), 0)
    bump = last[0]
    plan = (
        (own, 0, 3, 2, None),
        (left, 0, 0, 3, None),
        (below, 6, 3, 0, bump),
        (corner, 6, 0, 1, bump),
    )
    for ref, row0, col0, quadrant, offset in plan:
        label = jnp.zeros((2, WIDTH), jnp.int32)
        for row in range(6):
            for col in range(3):
                spot = row * 6 + col * 2
                ref[spot : spot + 2, :] = fields[row0 + row, col0 + col]
                ref[QUAD + spot : QUAD + spot + 2, :] = grads[row0 + row, col0 + col]
                value = ids[col0 + col, :, row0 + row : row0 + row + 1] + 1
                if offset is not None:
                    value = value + offset
                place = quadrant * QUAD + spot
                label = jnp.where(
                    lanes == level + place, jnp.broadcast_to(value, (2, WIDTH)), label
                )
        total = jnp.sum(label.astype(F32), axis=0, keepdims=True)
        ref[72:80, :] = jnp.broadcast_to(total, (8, WIDTH))


def pack(last, fields, grads, ids):
    shape = jax.ShapeDtypeStruct((80, WIDTH), F32)
    return pl.pallas_call(
        pack_kernel,
        out_shape=[shape] * 4,
        in_specs=[scalar()] + whole(3),
        out_specs=whole(4),
        compiler_params=params(PACK_MIB),
        cost_estimate=cost(1),
        name="pack",
    )(last, fields, grads, ids)


def one_hot(row, lines):
    low = (row & 255).astype(F32).astype(BF16)
    hit = lines == jnp.broadcast_to(low, (256, 128))
    return jnp.where(hit, jnp.ones((256, 128), BF16), jnp.zeros((256, 128), BF16))


def line_numbers():
    return lax.broadcasted_iota(jnp.int32, (256, 128), 0).astype(F32).astype(BF16)


def lookup_kernel(core_ref, index, table, bias, places, left):
    value = index[...]
    high = (value >> 7).astype(F32).astype(BF16)
    low = (value & 127).astype(F32).astype(BF16)
    move = token_order()

    def moved(part):
        return dot(dot(move, part, NN).astype(BF16), move, NT)

    result = moved(high) * 128.0 + moved(low)
    places[0:TOKENS, :] = result[:, :128].astype(jnp.int32)
    tail = jnp.concatenate([result[:, 128:], jnp.zeros((TOKENS, 112), F32)], axis=1)
    for i in range(18):
        spread = pltpu.roll(tail[8 * i : 8 * i + 8, :], 0, 1, stride=16, stride_axis=0)
        places[TOKENS + i : TOKENS + i + 1, :] = jnp.sum(spread, axis=0, keepdims=True).astype(jnp.int32)

    first = core_ref[0] == 0
    for block in range(BLOCKS):
        count = min(256, BIAS_ROWS - block * 256)
        top = table[0:8, block * 256 : block * 256 + count]
        bottom = table[8:16, block * 256 : block * 256 + count]
        part = jnp.concatenate(
            [jnp.where(first, bottom, top), jnp.where(first, top, bottom)], axis=0
        )
        if count < 256:
            part = jnp.concatenate([part, jnp.zeros((16, 256 - count), F32)], axis=1)
        left[block * 32 : block * 32 + 16, :], left[block * 32 + 16 : block * 32 + 32, :] = halves(
            part
        )
    lines = line_numbers()
    matrix = left[...]

    def find(rows):
        right = jnp.concatenate([one_hot(row, lines) for row in rows], axis=1)
        found = dot(matrix, right, NN)
        block = jnp.concatenate([row >> 8 for row in rows], axis=1)
        block = jnp.broadcast_to(block, (32, 256))
        total = jnp.zeros((32, 256), F32)
        for b in range(BLOCKS):
            total = jnp.where(block == b, found[b * 32 : b * 32 + 32], total)
        return total[:16] + total[16:]

    def step(i, carry):
        base = pl.multiple_of(i * 8, 8)
        rows = places[pl.ds(base, 8), :]
        for pair in range(4):
            found = find([rows[2 * pair + j : 2 * pair + j + 1, :] for j in range(2)])
            for j in range(2):
                bias[base + 2 * pair + j, :, 0:128] = found[:, j * 128 : j * 128 + 128]
        return carry

    lax.fori_loop(0, 18, step, 0, unroll=9)
    for pair in range(9):
        at = TOKENS + 2 * pair
        found = find([places[at + j : at + j + 1, :] for j in range(2)])
        for j in range(16):
            bias[16 * pair + j, :, 128:144] = found[:, 16 * j : 16 * j + 16]


def lookup(core, bias_index, bias_table):
    return pl.pallas_call(
        lookup_kernel,
        out_shape=[
            jax.ShapeDtypeStruct((TOKENS, HEADS, TOKENS), F32),
            jax.ShapeDtypeStruct((ROWS, 128), jnp.int32),
        ],
        in_specs=[scalar()] + whole(2),
        out_specs=whole(2),
        scratch_shapes=[pltpu.VMEM((BLOCKS * 32, 256), BF16)],
        compiler_params=params(),
        cost_estimate=cost(LOOKUP_COST),
        name="lookup",
    )(core, bias_index, bias_table.T)


def main_kernel(
    core_ref,
    own,
    quad0,
    quad1,
    quad3,
    bias,
    in_weight,
    out_weight,
    keep,
    send,
    keep_scores,
    send_scores,
    grad0,
    grad1,
    grad2,
    grad3,
    tokens,
    cotangent,
    proj,
    gatt,
    gproj,
    att,
    normed_t,
    tails,
):
    core = core_ref[0]
    row = jnp.zeros((1, WIDTH), F32)
    for slot, (quad, start) in enumerate(((quad0, 0), (quad1, 0), (own, 0), (quad3, 0))):
        at = slot * QUAD
        tokens[at : at + QUAD, :] = quad[start : start + QUAD, :]
        cotangent[at : at + QUAD, :] = quad[start + QUAD : start + 2 * QUAD, :]
        row = row + quad[start + 72 : start + 73, :]
    row = row[:, :TOKENS]
    side = lax.broadcasted_iota(jnp.int32, (TOKENS, TOKENS), 0)
    along = lax.broadcasted_iota(jnp.int32, (TOKENS, TOKENS), 1)
    spread = jnp.broadcast_to(row, (TOKENS, TOKENS))
    column = jnp.sum(jnp.where(side == along, spread, 0.0), axis=1, keepdims=True)
    allowed = column == spread

    inputs = tokens[...]
    centered = inputs - jnp.mean(inputs, axis=1, keepdims=True)
    variance = jnp.mean(centered * centered, axis=1, keepdims=True)
    inv_std = lax.rsqrt(variance + 1e-05)
    normed = centered * inv_std
    tokens[...] = normed
    normed_t[...] = normed.T
    halves_normed = halves(normed)
    for part in range(3):
        at = part * WIDTH
        weight = halves(in_weight[:, at : at + WIDTH])
        proj[at : at + WIDTH, :] = dot3(halves_normed, weight, NN).T
    halves_cotangent = halves(cotangent[...])
    gatt[...] = dot3(halves(out_weight[...]), halves_cotangent, NT)

    def stacked(*parts):
        return jnp.concatenate(parts, axis=0)

    def product(high, low, right_high, right_low, dims):
        both = dot(stacked(high, low), right_high, dims)
        return both[:HEAD_DIM] + (both[HEAD_DIM:] + dot(high, right_low, dims))

    def some_heads(heads):
        ats = [pl.multiple_of(head * HEAD_DIM, HEAD_DIM) for head, _ in heads]
        q = [halves(proj[pl.ds(at, HEAD_DIM), :] * FACTOR) for at in ats]
        k = [halves(proj[pl.ds(at + WIDTH, HEAD_DIM), :]) for at in ats]
        v = [halves(proj[pl.ds(at + 2 * WIDTH, HEAD_DIM), :]) for at in ats]
        g = [halves(gatt[pl.ds(at, HEAD_DIM), :]) for at in ats]

        def outer(left, right):
            return dot(
                stacked(left[0], left[0], left[1]), stacked(right[0], right[1], right[0]), TN
            )

        scores = [
            outer(q[i], k[i]) + bias[:, slot, :]
            for i, (_, slot) in enumerate(heads)
        ]
        grad_probs = [outer(g[i], v[i]) for i in range(len(heads))]
        scores = [jnp.where(allowed, x, -1000000000.0) for x in scores]
        exponent = [jnp.exp(x - jnp.max(x, axis=1, keepdims=True)) for x in scores]
        probs = [x * (1.0 / jnp.sum(x, axis=1, keepdims=True)) for x in exponent]
        p = [halves(x) for x in probs]
        for i, at in enumerate(ats):
            att[pl.ds(at, HEAD_DIM), :] = product(*v[i], *p[i], NT)
            gproj[pl.ds(at + 2 * WIDTH, HEAD_DIM), :] = product(*g[i], *p[i], NN)
        grad_scores = [
            x * (y - jnp.sum(x * y, axis=1, keepdims=True)) for x, y in zip(probs, grad_probs)
        ]
        s = [halves(x) for x in grad_scores]
        for i, at in enumerate(ats):
            gproj[pl.ds(at, HEAD_DIM), :] = product(*k[i], *s[i], NT) * FACTOR
            gproj[pl.ds(at + WIDTH, HEAD_DIM), :] = product(*q[i], *s[i], NN)
        for i, (_, slot) in enumerate(heads):
            target = send_scores if slot < 8 else keep_scores
            target[0:TOKENS, slot % 8, :] = grad_scores[i][:, :128]
            tails[:, slot, 0:16] = grad_scores[i][:, 128:]

    tails[...] = jnp.zeros_like(tails)
    order = [((1 - core) * 8 + slot, slot) for slot in range(8)]
    order += [(core * 8 + slot, 8 + slot) for slot in range(8)]
    for first in range(0, 16, 4):
        some_heads(order[first : first + 4])

    for i in range(18):
        total = tails[8 * i]
        for j in range(1, 8):
            total = total + pltpu.roll(tails[8 * i + j], 16 * j, 1)
        send_scores[TOKENS + i] = total[0:8]
        keep_scores[TOKENS + i] = total[8:16]

    for target, bit in ((send, 1 - core), (keep, core)):
        rows = [pl.ds(pl.multiple_of(64 * i + 32 * bit, 32), 32) for i in range(8)]
        left = halves(jnp.concatenate([normed_t[r, :] for r in rows], axis=0))
        for part in range(3):
            at = part * WIDTH
            target[:, at : at + WIDTH] = dot3(left, halves(gproj[at : at + WIDTH, :]), NT)
        left = halves(jnp.concatenate([att[r, :] for r in rows], axis=0))
        target[:, 3 * WIDTH :] = dot3(left, halves_cotangent, NN)

    grad_normed = jnp.zeros((WIDTH, TOKENS), F32)
    for part in range(3):
        at = part * WIDTH
        grad_normed = grad_normed + dot3(
            halves(in_weight[:, at : at + WIDTH]), halves(gproj[at : at + WIDTH, :]), NN
        )
    grad_normed = grad_normed.T
    normed = tokens[...]
    result = inv_std * (
        grad_normed
        - jnp.mean(grad_normed, axis=1, keepdims=True)
        - normed * jnp.mean(grad_normed * normed, axis=1, keepdims=True)
    )
    tokens[...] = result
    for slot, target in enumerate((grad0, grad1, grad2, grad3)):
        target[...] = tokens[slot * QUAD : slot * QUAD + QUAD, :]


def shape(*dims):
    return jax.ShapeDtypeStruct(dims, F32)


def window(core, own, quad0, quad1, quad3, bias, in_weight, out_weight):
    grad = shape(QUAD, WIDTH)
    return pl.pallas_call(
        main_kernel,
        out_shape=[
            shape(256, 4 * WIDTH),
            shape(256, 4 * WIDTH),
            shape(ROWS, 8, 128),
            shape(ROWS, 8, 128),
            grad,
            grad,
            grad,
            grad,
        ],
        in_specs=[scalar()] + whole(7),
        out_specs=whole(8),
        scratch_shapes=[
            pltpu.VMEM((TOKENS, WIDTH), F32),
            pltpu.VMEM((TOKENS, WIDTH), F32),
            pltpu.VMEM((3 * WIDTH, TOKENS), F32),
            pltpu.VMEM((WIDTH, TOKENS), F32),
            pltpu.VMEM((3 * WIDTH, TOKENS), F32),
            pltpu.VMEM((WIDTH, TOKENS), F32),
            pltpu.VMEM((WIDTH, TOKENS), F32),
            pltpu.VMEM((TOKENS, HEADS, 128), F32),
        ],
        compiler_params=params(26),
        cost_estimate=cost(WINDOW_COST),
        name="window",
    )(core, own, quad0, quad1, quad3, bias, in_weight, out_weight)


def add_pairs(places, keep, came, total):
    lines = line_numbers()

    def sides(row, values):
        block = (row >> 8).astype(F32).astype(BF16)
        both = jnp.concatenate(halves(values), axis=0)
        spread = jnp.broadcast_to(block, (16, 128))
        left = jnp.concatenate(
            [jnp.where(spread == float(b), both, jnp.zeros_like(both)) for b in range(BLOCKS)],
            axis=0,
        )
        return left, one_hot(row, lines)

    def add(rows, base, pair):
        pieces = [
            sides(rows[j : j + 1, :], keep[base + j] + came[base + j])
            for j in (2 * pair, 2 * pair + 1)
        ]
        left = jnp.concatenate([p[0] for p in pieces], axis=1)
        right = jnp.concatenate([p[1] for p in pieces], axis=1)
        total[...] += dot(left, right, NT)

    def step(i, carry):
        base = pl.multiple_of(i * 8, 8)
        rows = places[pl.ds(base, 8), :]
        for pair in range(4):
            add(rows, base, pair)
        return carry

    lax.fori_loop(0, ROWS // 8, step, 0, unroll=10)
    add(places[ROWS - 2 : ROWS, :], ROWS - 2, 0)


def scatter_kernel(core_ref, places, keep, came, mine, other, total, line, sectors):
    total[...] = jnp.zeros_like(total)
    add_pairs(places, keep, came, total)
    for b in range(BLOCKS):
        line[:, b * 256 : b * 256 + 256] = (
            total[b * 16 : b * 16 + 8, :] + total[b * 16 + 8 : b * 16 + 16, :]
        )
    line[:, BLOCKS * 256 :] = jnp.zeros((8, 256), F32)
    for m in range(32):
        chip, core, half = m // 4, m // 2 % 2, m % 2
        start_at = m * HALF_SECTOR
        base, shift = start_at // 128 * 128, start_at % 128
        piece = line[:, base : base + 512]
        if shift:
            piece = pltpu.roll(piece, 512 - shift, 1)
        sectors[core, chip, half * 8 : half * 8 + 8, :] = piece[:, :256]
    mine[...] = sectors[core_ref[0]]
    other[...] = sectors[1 - core_ref[0]]


def scatter(core, places, keep, came):
    return pl.pallas_call(
        scatter_kernel,
        out_shape=[shape(8, 16, 256)] * 2,
        in_specs=[scalar()] + whole(3),
        out_specs=whole(2),
        scratch_shapes=[
            pltpu.VMEM((BLOCKS * 16, 256), F32),
            pltpu.VMEM((8, BLOCKS * 256 + 256), F32),
            pltpu.VMEM((2, 8, 16, 256), F32),
        ],
        compiler_params=params(),
        cost_estimate=cost(SCATTER_COST),
        name="scatter",
    )(core, places, keep, came)


def split_kernel(odd, keep, came, own, send_a, send_b):
    def columns(bit):
        cols = slice(512 * bit, 512 * bit + 512)
        return keep[:, cols] + came[:, cols]

    for bit in range(2):

        @pl.when(odd[0] == bit)
        def _():
            send_a[...] = columns(1 - bit)
            send_b[...] = columns(2 + bit)
            own[:, 0:512] = columns(bit)
            own[:, 512:1024] = columns(3 - bit)


def split(odd, keep, came):
    return pl.pallas_call(
        split_kernel,
        out_shape=[shape(256, 1024), shape(256, 512), shape(256, 512)],
        in_specs=[scalar()] + whole(2),
        out_specs=whole(3),
        compiler_params=params(),
        name="split",
    )(odd, keep, came)


def join_kernel(core_ref, own, came_a, came_b, table_keep, table_came, out):
    for i in range(8):
        rows = slice(i * 32, i * 32 + 32)
        out[i, :, 0:512] = own[rows, 0:512] + came_a[rows, :]
        out[i, :, 512:1024] = own[rows, 512:1024] + came_b[rows, :]
    first = core_ref[0] == 0
    mine, other = table_keep[...], table_came[...]
    out[:, 0:16, 1024:] = jnp.where(first, mine, other)
    out[:, 16:32, 1024:] = jnp.where(first, other, mine)


def join(core, *parts):
    return pl.pallas_call(
        join_kernel,
        out_shape=shape(8, 32, 1280),
        in_specs=[scalar()] + whole(5),
        out_specs=pl.BlockSpec(memory_space=pltpu.VMEM),
        compiler_params=params(),
        name="join",
    )(core, *parts)


def fold_lon_kernel(parts, out, total):
    value = parts[0]
    for i in range(1, 8):
        value = value + parts[i]
    total[...] = value
    for i in range(8):
        out[i] = total[4 * i : 4 * i + 4, :]


def fold_lon(parts):
    return pl.pallas_call(
        fold_lon_kernel,
        out_shape=shape(8, 4, 1280),
        in_specs=whole(1),
        out_specs=pl.BlockSpec(memory_space=pltpu.VMEM),
        scratch_shapes=[pltpu.VMEM((32, 1280), F32)],
        compiler_params=params(),
        name="fold_lon",
    )(parts)


def fold_lat_kernel(parts, out):
    total = parts[0]
    for i in range(1, 8):
        total = total + parts[i]
    for i in range(16):
        out[i] = total


def fold_lat(parts):
    return pl.pallas_call(
        fold_lat_kernel,
        out_shape=shape(16, 4, 1280),
        in_specs=whole(1),
        out_specs=pl.BlockSpec(memory_space=pltpu.VMEM),
        compiler_params=params(),
        name="fold_lat",
    )(parts)


def unpack_kernel(parts, grad_in, grad_out, grad_bias, table):
    for rank in range(8):
        rows = slice(4 * rank, 4 * rank + 4)
        even = (rank // 2) * 4 + rank % 2
        odd = even + 2
        grad_in[rows, 0:512] = parts[even, :, 0:512]
        grad_in[rows, 512:1024] = parts[odd, :, 0:512]
        grad_in[rows, 1024:1536] = parts[odd, :, 512:1024]
        grad_out[rows, :] = parts[even, :, 512:1024]
        table[rows, :] = parts[even, :, 1024:] + parts[odd, :, 1024:]
    for core in range(2):
        for half in range(2):
            base = core * 16 + half * 8
            grad_bias[core * 8 : core * 8 + 8, half * HALF_SECTOR : (half + 1) * HALF_SECTOR] = (
                table[base : base + 8, :HALF_SECTOR]
            )


def unpack(parts):
    return pl.pallas_call(
        unpack_kernel,
        out_shape=[shape(32, 3 * WIDTH), shape(32, WIDTH), shape(HEADS, 2 * HALF_SECTOR)],
        in_specs=whole(1),
        out_specs=whole(3),
        scratch_shapes=[pltpu.VMEM((32, 256), F32)],
        compiler_params=params(),
        name="unpack",
    )(parts)


def place_kernel(grad_out, own, left, below, corner, out):
    for ref, row0, col0 in ((own, 0, 3), (left, 0, 0), (below, 6, 3), (corner, 6, 0)):
        for row in range(6):
            for col in range(3):
                spot = row * 6 + col * 2
                out[row0 + row, col0 + col] = (
                    grad_out[row0 + row, col0 + col] + ref[spot : spot + 2, :]
                )


def place(grad_out, own, left, below, corner):
    return pl.pallas_call(
        place_kernel,
        out_shape=jax.ShapeDtypeStruct(grad_out.shape, F32),
        in_specs=whole(5),
        out_specs=pl.BlockSpec(memory_space=pltpu.VMEM),
        compiler_params=params(),
        name="place",
    )(grad_out, own, left, below, corner)


LAT = ("z", "y_lo")
LON = ("x", "y_hi", "core")


def body(fields, grad_out, region_ids, bias_index, bias_table, in_weight, out_weight):
    everything = LAT + LON
    lat = lax.axis_index(LAT)
    core = lax.axis_index("core").reshape(1)
    odd = lax.rem(lax.axis_index("z"), 2).reshape(1)

    def moves(down, right):
        return [
            (i * 16 + j, (i + down) % 16 * 16 + (j + right) % 16)
            for i in range(16)
            for j in range(16)
        ]

    swap = [(0, 1), (1, 0)]
    last = jnp.where(lat == 15, 3, 0).reshape(1)
    grad_out = jnp.transpose(grad_out, (1, 2, 0, 3))
    own, left, below, corner = pack(
        last, jnp.transpose(fields, (1, 2, 0, 3)), grad_out, jnp.transpose(region_ids, (2, 0, 1))
    )
    quad3 = lax.ppermute(left, everything, moves(0, -1))
    quad0 = lax.ppermute(below, everything, moves(1, 0))
    quad1 = lax.ppermute(corner, everything, moves(1, -1))
    bias, places = lookup(core, bias_index, bias_table)
    keep, send, keep_scores, send_scores, grad0, grad1, grad2, grad3 = window(
        core, own, quad0, quad1, quad3, bias, in_weight, out_weight
    )
    came = lax.ppermute(send, "core", swap)
    came_scores = lax.ppermute(send_scores, "core", swap)
    back = (
        lax.ppermute(grad3, everything, moves(0, 1)),
        lax.ppermute(grad0, everything, moves(-1, 0)),
        lax.ppermute(grad1, everything, moves(-1, 1)),
    )
    part, send_a, send_b = split(odd, keep, came)
    came_a = lax.ppermute(send_a, "z", [(i, i ^ 1) for i in range(8)])
    came_b = lax.ppermute(send_b, "z", [(i, ((i + 1) % 8 ^ 1) + 7 & 7) for i in range(8)])
    part, places, back = lax.optimization_barrier((part, places, back))
    mine, other = scatter(core, places, keep_scores, came_scores)
    came_table = lax.ppermute(other, "core", swap)
    mine, grad2 = lax.optimization_barrier((mine, grad2))
    grad_fields = place(grad_out, grad2, *back)
    part, grad_fields = lax.optimization_barrier((part, grad_fields))
    joined = join(core, part, came_a, came_b, mine, came_table)
    parts = lax.all_to_all(joined, ("x", "y_hi"), 0, 0)
    parity = [[z * 2 + y for z in range(bit, 8, 2) for y in range(2)] for bit in range(2)]
    parts = lax.all_to_all(fold_lon(parts), LAT, 0, 0, axis_index_groups=parity)
    parts = lax.all_to_all(fold_lat(parts), LAT, 0, 0)
    grad_in_weight, grad_out_weight, grad_bias = unpack(parts)
    return jnp.transpose(grad_fields, (2, 0, 1, 3)), grad_in_weight, grad_out_weight, grad_bias.T


def solution(mesh):
    split = Mesh(mesh.devices.reshape(8, 2, 4, 2, 2), LAT + LON)
    tokens = P(None, LAT, LON, None)
    in_specs = (tokens, tokens, P(None, LAT, LON), P(), P(), P(), P())
    out_specs = (tokens, P(LON, None), P(LON, None), P(LON, None))
    return jax.shard_map(body, mesh=split, in_specs=in_specs, out_specs=out_specs, check_vma=False)
```

```python
import jax
import jax.numpy as jnp
from jax import lax
from jax.experimental import pallas as pl
from jax.experimental.pallas import tpu as pltpu
from jax.sharding import Mesh
from jax.sharding import PartitionSpec as P

WIDTH = 512
HEADS = 16
HEAD_DIM = 32
TOKENS = 144
QUAD = 36
BIAS_ROWS = 6336
HALF_SECTOR = 198
BLOCKS = 25
PACK_MIB = 56
ROWS = 162
LOOKUP_COST = 13
WINDOW_COST = 0
SCATTER_COST = 9
FACTOR = HEAD_DIM ** (-0.5)
F32 = jnp.float32
BF16 = jnp.bfloat16
MEGA = 1 << 20


def params(mib=16):
    return pltpu.CompilerParams(vmem_limit_bytes=mib * MEGA)


def cost(micros):
    return pl.CostEstimate(flops=int(micros * 1e9), bytes_accessed=0, transcendentals=0)


def whole(count):
    return [pl.BlockSpec(memory_space=pltpu.VMEM)] * count


def scalar():
    return pl.BlockSpec(memory_space=pltpu.SMEM)


def halves(x):
    high = x.astype(BF16)
    low = (x - high.astype(F32)).astype(BF16)
    return high, low


def dot(a, b, dims):
    return lax.dot_general(a, b, (dims, ((), ())), preferred_element_type=F32)


NN = ((1,), (0,))
NT = ((1,), (1,))
TN = ((0,), (0,))


def dot3(a, b, dims):
    ah, al = a
    bh, bl = b
    return dot(ah, bh, dims) + (dot(ah, bl, dims) + dot(al, bh, dims))


def token_order():
    place = lax.broadcasted_iota(jnp.int32, (TOKENS, TOKENS), 0)
    token = lax.broadcasted_iota(jnp.int32, (TOKENS, TOKENS), 1)

    def steps(value, size, count):
        total = jnp.zeros_like(value)
        for i in range(1, count):
            total = total + jnp.where(value >= i * size, 1, 0)
        return total

    quad = steps(place, QUAD, 4)
    rest = place - QUAD * quad
    row = steps(rest, 6, 6)
    rest = rest - 6 * row
    col = steps(rest, 2, 3)
    level = rest - 2 * col
    row_half = steps(quad, 2, 2)
    col_half = quad - 2 * row_half
    source = level * 72 + (6 * row_half + row) * 6 + 3 * col_half + col
    return jnp.where(source == token, 1.0, 0.0).astype(BF16)


def pack_kernel(last, fields, grads, ids, own, left, below, corner):
    lanes = lax.broadcasted_iota(jnp.int32, (2, WIDTH), 1)
    level = lax.broadcasted_iota(jnp.int32, (2, WIDTH), 0)
    bump = last[0]
    plan = (
        (own, 0, 3, 2, None),
        (left, 0, 0, 3, None),
        (below, 6, 3, 0, bump),
        (corner, 6, 0, 1, bump),
    )
    for ref, row0, col0, quadrant, offset in plan:
        label = jnp.zeros((2, WIDTH), jnp.int32)
        for row in range(6):
            for col in range(3):
                spot = row * 6 + col * 2
                ref[spot : spot + 2, :] = fields[row0 + row, col0 + col]
                ref[QUAD + spot : QUAD + spot + 2, :] = grads[row0 + row, col0 + col]
                value = ids[col0 + col, :, row0 + row : row0 + row + 1] + 1
                if offset is not None:
                    value = value + offset
                place = quadrant * QUAD + spot
                label = jnp.where(
                    lanes == level + place, jnp.broadcast_to(value, (2, WIDTH)), label
                )
        total = jnp.sum(label.astype(F32), axis=0, keepdims=True)
        ref[72:80, :] = jnp.broadcast_to(total, (8, WIDTH))


def pack(last, fields, grads, ids):
    shape = jax.ShapeDtypeStruct((80, WIDTH), F32)
    return pl.pallas_call(
        pack_kernel,
        out_shape=[shape] * 4,
        in_specs=[scalar()] + whole(3),
        out_specs=whole(4),
        compiler_params=params(PACK_MIB),
        cost_estimate=cost(1),
        name="pack",
    )(last, fields, grads, ids)


def one_hot(row, lines):
    low = (row & 255).astype(F32).astype(BF16)
    hit = lines == jnp.broadcast_to(low, (256, 128))
    return jnp.where(hit, jnp.ones((256, 128), BF16), jnp.zeros((256, 128), BF16))


def line_numbers():
    return lax.broadcasted_iota(jnp.int32, (256, 128), 0).astype(F32).astype(BF16)


def lookup_kernel(core_ref, index, table, bias, places, left):
    value = index[...]
    high = (value >> 7).astype(F32).astype(BF16)
    low = (value & 127).astype(F32).astype(BF16)
    move = token_order()

    def moved(part):
        return dot(dot(move, part, NN).astype(BF16), move, NT)

    result = moved(high) * 128.0 + moved(low)
    places[0:TOKENS, :] = result[:, :128].astype(jnp.int32)
    tail = jnp.concatenate([result[:, 128:], jnp.zeros((TOKENS, 112), F32)], axis=1)
    for i in range(18):
        spread = pltpu.roll(tail[8 * i : 8 * i + 8, :], 0, 1, stride=16, stride_axis=0)
        places[TOKENS + i : TOKENS + i + 1, :] = jnp.sum(spread, axis=0, keepdims=True).astype(jnp.int32)

    first = core_ref[0] == 0
    for block in range(BLOCKS):
        count = min(256, BIAS_ROWS - block * 256)
        top = table[0:8, block * 256 : block * 256 + count]
        bottom = table[8:16, block * 256 : block * 256 + count]
        part = jnp.concatenate(
            [jnp.where(first, bottom, top), jnp.where(first, top, bottom)], axis=0
        )
        if count < 256:
            part = jnp.concatenate([part, jnp.zeros((16, 256 - count), F32)], axis=1)
        left[block * 32 : block * 32 + 16, :], left[block * 32 + 16 : block * 32 + 32, :] = halves(
            part
        )
    lines = line_numbers()
    matrix = left[...]

    def find(rows):
        right = jnp.concatenate([one_hot(row, lines) for row in rows], axis=1)
        found = dot(matrix, right, NN)
        block = jnp.concatenate([row >> 8 for row in rows], axis=1)
        block = jnp.broadcast_to(block, (32, 256))
        total = jnp.zeros((32, 256), F32)
        for b in range(BLOCKS):
            total = jnp.where(block == b, found[b * 32 : b * 32 + 32], total)
        return total[:16] + total[16:]

    def step(i, carry):
        base = pl.multiple_of(i * 8, 8)
        rows = places[pl.ds(base, 8), :]
        for pair in range(4):
            found = find([rows[2 * pair + j : 2 * pair + j + 1, :] for j in range(2)])
            for j in range(2):
                bias[base + 2 * pair + j, :, 0:128] = found[:, j * 128 : j * 128 + 128]
        return carry

    lax.fori_loop(0, 18, step, 0, unroll=18)
    for pair in range(9):
        at = TOKENS + 2 * pair
        found = find([places[at + j : at + j + 1, :] for j in range(2)])
        for j in range(16):
            bias[16 * pair + j, :, 128:144] = found[:, 16 * j : 16 * j + 16]


def lookup(core, bias_index, bias_table):
    return pl.pallas_call(
        lookup_kernel,
        out_shape=[
            jax.ShapeDtypeStruct((TOKENS, HEADS, TOKENS), F32),
            jax.ShapeDtypeStruct((ROWS, 128), jnp.int32),
        ],
        in_specs=[scalar()] + whole(2),
        out_specs=whole(2),
        scratch_shapes=[pltpu.VMEM((BLOCKS * 32, 256), BF16)],
        compiler_params=params(),
        cost_estimate=cost(LOOKUP_COST),
        name="lookup",
    )(core, bias_index, bias_table.T)


def main_kernel(
    core_ref,
    own,
    quad0,
    quad1,
    quad3,
    bias,
    in_weight,
    out_weight,
    keep,
    send,
    keep_scores,
    send_scores,
    grad0,
    grad1,
    grad2,
    grad3,
    tokens,
    cotangent,
    proj,
    gatt,
    gproj,
    att,
    normed_t,
    tails,
):
    core = core_ref[0]
    row = jnp.zeros((1, WIDTH), F32)
    for slot, (quad, start) in enumerate(((quad0, 0), (quad1, 0), (own, 0), (quad3, 0))):
        at = slot * QUAD
        tokens[at : at + QUAD, :] = quad[start : start + QUAD, :]
        cotangent[at : at + QUAD, :] = quad[start + QUAD : start + 2 * QUAD, :]
        row = row + quad[start + 72 : start + 73, :]
    row = row[:, :TOKENS]
    side = lax.broadcasted_iota(jnp.int32, (TOKENS, TOKENS), 0)
    along = lax.broadcasted_iota(jnp.int32, (TOKENS, TOKENS), 1)
    spread = jnp.broadcast_to(row, (TOKENS, TOKENS))
    column = jnp.sum(jnp.where(side == along, spread, 0.0), axis=1, keepdims=True)
    allowed = column == spread

    inputs = tokens[...]
    centered = inputs - jnp.mean(inputs, axis=1, keepdims=True)
    variance = jnp.mean(centered * centered, axis=1, keepdims=True)
    inv_std = lax.rsqrt(variance + 1e-05)
    normed = centered * inv_std
    tokens[...] = normed
    normed_t[...] = normed.T
    halves_normed = halves(normed)
    for part in range(3):
        at = part * WIDTH
        weight = halves(in_weight[:, at : at + WIDTH])
        proj[at : at + WIDTH, :] = dot3(halves_normed, weight, NN).T
    halves_cotangent = halves(cotangent[...])
    gatt[...] = dot3(halves(out_weight[...]), halves_cotangent, NT)

    def stacked(*parts):
        return jnp.concatenate(parts, axis=0)

    def product(high, low, right_high, right_low, dims):
        both = dot(stacked(high, low), right_high, dims)
        return both[:HEAD_DIM] + (both[HEAD_DIM:] + dot(high, right_low, dims))

    def some_heads(heads):
        ats = [pl.multiple_of(head * HEAD_DIM, HEAD_DIM) for head, _ in heads]
        q = [halves(proj[pl.ds(at, HEAD_DIM), :] * FACTOR) for at in ats]
        k = [halves(proj[pl.ds(at + WIDTH, HEAD_DIM), :]) for at in ats]
        v = [halves(proj[pl.ds(at + 2 * WIDTH, HEAD_DIM), :]) for at in ats]
        g = [halves(gatt[pl.ds(at, HEAD_DIM), :]) for at in ats]

        def outer(left, right):
            return dot(
                stacked(left[0], left[0], left[1]), stacked(right[0], right[1], right[0]), TN
            )

        scores = [
            outer(q[i], k[i]) + bias[:, slot, :]
            for i, (_, slot) in enumerate(heads)
        ]
        grad_probs = [outer(g[i], v[i]) for i in range(len(heads))]
        scores = [jnp.where(allowed, x, -1000000000.0) for x in scores]
        exponent = [jnp.exp(x - jnp.max(x, axis=1, keepdims=True)) for x in scores]
        probs = [x * (1.0 / jnp.sum(x, axis=1, keepdims=True)) for x in exponent]
        p = [halves(x) for x in probs]
        for i, at in enumerate(ats):
            att[pl.ds(at, HEAD_DIM), :] = product(*v[i], *p[i], NT)
            gproj[pl.ds(at + 2 * WIDTH, HEAD_DIM), :] = product(*g[i], *p[i], NN)
        grad_scores = [
            x * (y - jnp.sum(x * y, axis=1, keepdims=True)) for x, y in zip(probs, grad_probs)
        ]
        s = [halves(x) for x in grad_scores]
        for i, at in enumerate(ats):
            gproj[pl.ds(at, HEAD_DIM), :] = product(*k[i], *s[i], NT) * FACTOR
            gproj[pl.ds(at + WIDTH, HEAD_DIM), :] = product(*q[i], *s[i], NN)
        for i, (_, slot) in enumerate(heads):
            target = send_scores if slot < 8 else keep_scores
            target[0:TOKENS, slot % 8, :] = grad_scores[i][:, :128]
            tails[:, slot, 0:16] = grad_scores[i][:, 128:]

    tails[...] = jnp.zeros_like(tails)
    order = [((1 - core) * 8 + slot, slot) for slot in range(8)]
    order += [(core * 8 + slot, 8 + slot) for slot in range(8)]
    for first in range(0, 16, 8):
        some_heads(order[first : first + 8])

    for i in range(18):
        total = tails[8 * i]
        for j in range(1, 8):
            total = total + pltpu.roll(tails[8 * i + j], 16 * j, 1)
        send_scores[TOKENS + i] = total[0:8]
        keep_scores[TOKENS + i] = total[8:16]

    for target, bit in ((send, 1 - core), (keep, core)):
        rows = [pl.ds(pl.multiple_of(64 * i + 32 * bit, 32), 32) for i in range(8)]
        left = halves(jnp.concatenate([normed_t[r, :] for r in rows], axis=0))
        for part in range(3):
            at = part * WIDTH
            target[:, at : at + WIDTH] = dot3(left, halves(gproj[at : at + WIDTH, :]), NT)
        left = halves(jnp.concatenate([att[r, :] for r in rows], axis=0))
        target[:, 3 * WIDTH :] = dot3(left, halves_cotangent, NN)

    grad_normed = jnp.zeros((WIDTH, TOKENS), F32)
    for part in range(3):
        at = part * WIDTH
        grad_normed = grad_normed + dot3(
            halves(in_weight[:, at : at + WIDTH]), halves(gproj[at : at + WIDTH, :]), NN
        )
    grad_normed = grad_normed.T
    normed = tokens[...]
    result = inv_std * (
        grad_normed
        - jnp.mean(grad_normed, axis=1, keepdims=True)
        - normed * jnp.mean(grad_normed * normed, axis=1, keepdims=True)
    )
    tokens[...] = result
    for slot, target in enumerate((grad0, grad1, grad2, grad3)):
        target[...] = tokens[slot * QUAD : slot * QUAD + QUAD, :]


def shape(*dims):
    return jax.ShapeDtypeStruct(dims, F32)


def window(core, own, quad0, quad1, quad3, bias, in_weight, out_weight):
    grad = shape(QUAD, WIDTH)
    return pl.pallas_call(
        main_kernel,
        out_shape=[
            shape(256, 4 * WIDTH),
            shape(256, 4 * WIDTH),
            shape(ROWS, 8, 128),
            shape(ROWS, 8, 128),
            grad,
            grad,
            grad,
            grad,
        ],
        in_specs=[scalar()] + whole(7),
        out_specs=whole(8),
        scratch_shapes=[
            pltpu.VMEM((TOKENS, WIDTH), F32),
            pltpu.VMEM((TOKENS, WIDTH), F32),
            pltpu.VMEM((3 * WIDTH, TOKENS), F32),
            pltpu.VMEM((WIDTH, TOKENS), F32),
            pltpu.VMEM((3 * WIDTH, TOKENS), F32),
            pltpu.VMEM((WIDTH, TOKENS), F32),
            pltpu.VMEM((WIDTH, TOKENS), F32),
            pltpu.VMEM((TOKENS, HEADS, 128), F32),
        ],
        compiler_params=params(26),
        cost_estimate=cost(WINDOW_COST),
        name="window",
    )(core, own, quad0, quad1, quad3, bias, in_weight, out_weight)


def add_pairs(places, keep, came, total):
    lines = line_numbers()

    def sides(row, values):
        block = (row >> 8).astype(F32).astype(BF16)
        both = jnp.concatenate(halves(values), axis=0)
        spread = jnp.broadcast_to(block, (16, 128))
        left = jnp.concatenate(
            [jnp.where(spread == float(b), both, jnp.zeros_like(both)) for b in range(BLOCKS)],
            axis=0,
        )
        return left, one_hot(row, lines)

    def add(rows, base, pair):
        pieces = [
            sides(rows[j : j + 1, :], keep[base + j] + came[base + j])
            for j in (2 * pair, 2 * pair + 1)
        ]
        left = jnp.concatenate([p[0] for p in pieces], axis=1)
        right = jnp.concatenate([p[1] for p in pieces], axis=1)
        total[...] += dot(left, right, NT)

    def step(i, carry):
        base = pl.multiple_of(i * 8, 8)
        rows = places[pl.ds(base, 8), :]
        for pair in range(4):
            add(rows, base, pair)
        return carry

    lax.fori_loop(0, ROWS // 8, step, 0, unroll=10)
    add(places[ROWS - 2 : ROWS, :], ROWS - 2, 0)


def scatter_kernel(core_ref, places, keep, came, mine, other, total, line, sectors):
    total[...] = jnp.zeros_like(total)
    add_pairs(places, keep, came, total)
    for b in range(BLOCKS):
        line[:, b * 256 : b * 256 + 256] = (
            total[b * 16 : b * 16 + 8, :] + total[b * 16 + 8 : b * 16 + 16, :]
        )
    line[:, BLOCKS * 256 :] = jnp.zeros((8, 256), F32)
    for m in range(32):
        chip, core, half = m // 4, m // 2 % 2, m % 2
        start_at = m * HALF_SECTOR
        base, shift = start_at // 128 * 128, start_at % 128
        piece = line[:, base : base + 512]
        if shift:
            piece = pltpu.roll(piece, 512 - shift, 1)
        sectors[core, chip, half * 8 : half * 8 + 8, :] = piece[:, :256]
    mine[...] = sectors[core_ref[0]]
    other[...] = sectors[1 - core_ref[0]]


def scatter(core, places, keep, came):
    return pl.pallas_call(
        scatter_kernel,
        out_shape=[shape(8, 16, 256)] * 2,
        in_specs=[scalar()] + whole(3),
        out_specs=whole(2),
        scratch_shapes=[
            pltpu.VMEM((BLOCKS * 16, 256), F32),
            pltpu.VMEM((8, BLOCKS * 256 + 256), F32),
            pltpu.VMEM((2, 8, 16, 256), F32),
        ],
        compiler_params=params(),
        cost_estimate=cost(SCATTER_COST),
        name="scatter",
    )(core, places, keep, came)


def split_kernel(odd, keep, came, own, send_a, send_b):
    def columns(bit):
        cols = slice(512 * bit, 512 * bit + 512)
        return keep[:, cols] + came[:, cols]

    for bit in range(2):

        @pl.when(odd[0] == bit)
        def _():
            send_a[...] = columns(1 - bit)
            send_b[...] = columns(2 + bit)
            own[:, 0:512] = columns(bit)
            own[:, 512:1024] = columns(3 - bit)


def split(odd, keep, came):
    return pl.pallas_call(
        split_kernel,
        out_shape=[shape(256, 1024), shape(256, 512), shape(256, 512)],
        in_specs=[scalar()] + whole(2),
        out_specs=whole(3),
        compiler_params=params(),
        name="split",
    )(odd, keep, came)


def join_kernel(core_ref, own, came_a, came_b, table_keep, table_came, out):
    for i in range(8):
        rows = slice(i * 32, i * 32 + 32)
        out[i, :, 0:512] = own[rows, 0:512] + came_a[rows, :]
        out[i, :, 512:1024] = own[rows, 512:1024] + came_b[rows, :]
    first = core_ref[0] == 0
    mine, other = table_keep[...], table_came[...]
    out[:, 0:16, 1024:] = jnp.where(first, mine, other)
    out[:, 16:32, 1024:] = jnp.where(first, other, mine)


def join(core, *parts):
    return pl.pallas_call(
        join_kernel,
        out_shape=shape(8, 32, 1280),
        in_specs=[scalar()] + whole(5),
        out_specs=pl.BlockSpec(memory_space=pltpu.VMEM),
        compiler_params=params(),
        name="join",
    )(core, *parts)


def fold_lon_kernel(parts, out, total):
    value = parts[0]
    for i in range(1, 8):
        value = value + parts[i]
    total[...] = value
    for i in range(8):
        out[i] = total[4 * i : 4 * i + 4, :]


def fold_lon(parts):
    return pl.pallas_call(
        fold_lon_kernel,
        out_shape=shape(8, 4, 1280),
        in_specs=whole(1),
        out_specs=pl.BlockSpec(memory_space=pltpu.VMEM),
        scratch_shapes=[pltpu.VMEM((32, 1280), F32)],
        compiler_params=params(),
        name="fold_lon",
    )(parts)


def fold_lat_kernel(parts, out):
    total = parts[0]
    for i in range(1, 8):
        total = total + parts[i]
    for i in range(16):
        out[i] = total


def fold_lat(parts):
    return pl.pallas_call(
        fold_lat_kernel,
        out_shape=shape(16, 4, 1280),
        in_specs=whole(1),
        out_specs=pl.BlockSpec(memory_space=pltpu.VMEM),
        compiler_params=params(),
        name="fold_lat",
    )(parts)


def unpack_kernel(parts, grad_in, grad_out, grad_bias, table):
    for rank in range(8):
        rows = slice(4 * rank, 4 * rank + 4)
        even = (rank // 2) * 4 + rank % 2
        odd = even + 2
        grad_in[rows, 0:512] = parts[even, :, 0:512]
        grad_in[rows, 512:1024] = parts[odd, :, 0:512]
        grad_in[rows, 1024:1536] = parts[odd, :, 512:1024]
        grad_out[rows, :] = parts[even, :, 512:1024]
        table[rows, :] = parts[even, :, 1024:] + parts[odd, :, 1024:]
    for core in range(2):
        for half in range(2):
            base = core * 16 + half * 8
            grad_bias[core * 8 : core * 8 + 8, half * HALF_SECTOR : (half + 1) * HALF_SECTOR] = (
                table[base : base + 8, :HALF_SECTOR]
            )


def unpack(parts):
    return pl.pallas_call(
        unpack_kernel,
        out_shape=[shape(32, 3 * WIDTH), shape(32, WIDTH), shape(HEADS, 2 * HALF_SECTOR)],
        in_specs=whole(1),
        out_specs=whole(3),
        scratch_shapes=[pltpu.VMEM((32, 256), F32)],
        compiler_params=params(),
        name="unpack",
    )(parts)


def place_kernel(grad_out, own, left, below, corner, out):
    for ref, row0, col0 in ((own, 0, 3), (left, 0, 0), (below, 6, 3), (corner, 6, 0)):
        for row in range(6):
            for col in range(3):
                spot = row * 6 + col * 2
                out[row0 + row, col0 + col] = (
                    grad_out[row0 + row, col0 + col] + ref[spot : spot + 2, :]
                )


def place(grad_out, own, left, below, corner):
    return pl.pallas_call(
        place_kernel,
        out_shape=jax.ShapeDtypeStruct(grad_out.shape, F32),
        in_specs=whole(5),
        out_specs=pl.BlockSpec(memory_space=pltpu.VMEM),
        compiler_params=params(),
        name="place",
    )(grad_out, own, left, below, corner)


LAT = ("z", "y_lo")
LON = ("x", "y_hi", "core")


def body(fields, grad_out, region_ids, bias_index, bias_table, in_weight, out_weight):
    everything = LAT + LON
    lat = lax.axis_index(LAT)
    core = lax.axis_index("core").reshape(1)
    odd = lax.rem(lax.axis_index("z"), 2).reshape(1)

    def moves(down, right):
        return [
            (i * 16 + j, (i + down) % 16 * 16 + (j + right) % 16)
            for i in range(16)
            for j in range(16)
        ]

    swap = [(0, 1), (1, 0)]
    last = jnp.where(lat == 15, 3, 0).reshape(1)
    grad_out = jnp.transpose(grad_out, (1, 2, 0, 3))
    own, left, below, corner = pack(
        last, jnp.transpose(fields, (1, 2, 0, 3)), grad_out, jnp.transpose(region_ids, (2, 0, 1))
    )
    quad3 = lax.ppermute(left, everything, moves(0, -1))
    quad0 = lax.ppermute(below, everything, moves(1, 0))
    quad1 = lax.ppermute(corner, everything, moves(1, -1))
    bias, places = lookup(core, bias_index, bias_table)
    keep, send, keep_scores, send_scores, grad0, grad1, grad2, grad3 = window(
        core, own, quad0, quad1, quad3, bias, in_weight, out_weight
    )
    came = lax.ppermute(send, "core", swap)
    came_scores = lax.ppermute(send_scores, "core", swap)
    back = (
        lax.ppermute(grad3, everything, moves(0, 1)),
        lax.ppermute(grad0, everything, moves(-1, 0)),
        lax.ppermute(grad1, everything, moves(-1, 1)),
    )
    part, send_a, send_b = split(odd, keep, came)
    came_a = lax.ppermute(send_a, "z", [(i, i ^ 1) for i in range(8)])
    came_b = lax.ppermute(send_b, "z", [(i, ((i + 1) % 8 ^ 1) + 7 & 7) for i in range(8)])
    part, places, back = lax.optimization_barrier((part, places, back))
    mine, other = scatter(core, places, keep_scores, came_scores)
    came_table = lax.ppermute(other, "core", swap)
    mine, grad2 = lax.optimization_barrier((mine, grad2))
    grad_fields = place(grad_out, grad2, *back)
    part, grad_fields = lax.optimization_barrier((part, grad_fields))
    joined = join(core, part, came_a, came_b, mine, came_table)
    parts = lax.all_to_all(joined, ("x", "y_hi"), 0, 0)
    parity = [[z * 2 + y for z in range(bit, 8, 2) for y in range(2)] for bit in range(2)]
    parts = lax.all_to_all(fold_lon(parts), LAT, 0, 0, axis_index_groups=parity)
    parts = lax.all_to_all(fold_lat(parts), LAT, 0, 0)
    grad_in_weight, grad_out_weight, grad_bias = unpack(parts)
    return jnp.transpose(grad_fields, (2, 0, 1, 3)), grad_in_weight, grad_out_weight, grad_bias.T


def solution(mesh):
    split = Mesh(mesh.devices.reshape(8, 2, 4, 2, 2), LAT + LON)
    tokens = P(None, LAT, LON, None)
    in_specs = (tokens, tokens, P(None, LAT, LON), P(), P(), P(), P())
    out_specs = (tokens, P(LON, None), P(LON, None), P(LON, None))
    return jax.shard_map(body, mesh=split, in_specs=in_specs, out_specs=out_specs, check_vma=False)
```

```python
import jax
import jax.numpy as jnp
from jax import lax
from jax.experimental import pallas as pl
from jax.experimental.pallas import tpu as pltpu
from jax.sharding import Mesh
from jax.sharding import PartitionSpec as P

WIDTH = 512
HEADS = 16
HEAD_DIM = 32
TOKENS = 144
QUAD = 36
BIAS_ROWS = 6336
HALF_SECTOR = 198
BLOCKS = 25
PACK_MIB = 56
ROWS = 162
LOOKUP_COST = 13
WINDOW_COST = 0
SCATTER_COST = 9
FACTOR = HEAD_DIM ** (-0.5)
F32 = jnp.float32
BF16 = jnp.bfloat16
MEGA = 1 << 20


def params(mib=16):
    return pltpu.CompilerParams(vmem_limit_bytes=mib * MEGA)


def cost(micros):
    return pl.CostEstimate(flops=int(micros * 1e9), bytes_accessed=0, transcendentals=0)


def whole(count):
    return [pl.BlockSpec(memory_space=pltpu.VMEM)] * count


def scalar():
    return pl.BlockSpec(memory_space=pltpu.SMEM)


def halves(x):
    high = x.astype(BF16)
    low = (x - high.astype(F32)).astype(BF16)
    return high, low


def dot(a, b, dims):
    return lax.dot_general(a, b, (dims, ((), ())), preferred_element_type=F32)


NN = ((1,), (0,))
NT = ((1,), (1,))
TN = ((0,), (0,))


def dot3(a, b, dims):
    ah, al = a
    bh, bl = b
    return dot(ah, bh, dims) + (dot(ah, bl, dims) + dot(al, bh, dims))


def token_order():
    place = lax.broadcasted_iota(jnp.int32, (TOKENS, TOKENS), 0)
    token = lax.broadcasted_iota(jnp.int32, (TOKENS, TOKENS), 1)

    def steps(value, size, count):
        total = jnp.zeros_like(value)
        for i in range(1, count):
            total = total + jnp.where(value >= i * size, 1, 0)
        return total

    quad = steps(place, QUAD, 4)
    rest = place - QUAD * quad
    row = steps(rest, 6, 6)
    rest = rest - 6 * row
    col = steps(rest, 2, 3)
    level = rest - 2 * col
    row_half = steps(quad, 2, 2)
    col_half = quad - 2 * row_half
    source = level * 72 + (6 * row_half + row) * 6 + 3 * col_half + col
    return jnp.where(source == token, 1.0, 0.0).astype(BF16)


def pack_kernel(last, fields, grads, ids, own, left, below, corner):
    lanes = lax.broadcasted_iota(jnp.int32, (2, WIDTH), 1)
    level = lax.broadcasted_iota(jnp.int32, (2, WIDTH), 0)
    bump = last[0]
    plan = (
        (own, 0, 3, 2, None),
        (left, 0, 0, 3, None),
        (below, 6, 3, 0, bump),
        (corner, 6, 0, 1, bump),
    )
    for ref, row0, col0, quadrant, offset in plan:
        label = jnp.zeros((2, WIDTH), jnp.int32)
        for row in range(6):
            for col in range(3):
                spot = row * 6 + col * 2
                ref[spot : spot + 2, :] = fields[row0 + row, col0 + col]
                ref[QUAD + spot : QUAD + spot + 2, :] = grads[row0 + row, col0 + col]
                value = ids[col0 + col, :, row0 + row : row0 + row + 1] + 1
                if offset is not None:
                    value = value + offset
                place = quadrant * QUAD + spot
                label = jnp.where(
                    lanes == level + place, jnp.broadcast_to(value, (2, WIDTH)), label
                )
        total = jnp.sum(label.astype(F32), axis=0, keepdims=True)
        ref[72:80, :] = jnp.broadcast_to(total, (8, WIDTH))


def pack(last, fields, grads, ids):
    shape = jax.ShapeDtypeStruct((80, WIDTH), F32)
    return pl.pallas_call(
        pack_kernel,
        out_shape=[shape] * 4,
        in_specs=[scalar()] + whole(3),
        out_specs=whole(4),
        compiler_params=params(PACK_MIB),
        cost_estimate=cost(1),
        name="pack",
    )(last, fields, grads, ids)


def one_hot(row, lines):
    low = (row & 255).astype(F32).astype(BF16)
    hit = lines == jnp.broadcast_to(low, (256, 128))
    return jnp.where(hit, jnp.ones((256, 128), BF16), jnp.zeros((256, 128), BF16))


def line_numbers():
    return lax.broadcasted_iota(jnp.int32, (256, 128), 0).astype(F32).astype(BF16)


def lookup_kernel(core_ref, index, table, bias, places, left):
    value = index[...]
    high = (value >> 7).astype(F32).astype(BF16)
    low = (value & 127).astype(F32).astype(BF16)
    move = token_order()

    def moved(part):
        return dot(dot(move, part, NN).astype(BF16), move, NT)

    result = moved(high) * 128.0 + moved(low)
    places[0:TOKENS, :] = result[:, :128].astype(jnp.int32)
    tail = jnp.concatenate([result[:, 128:], jnp.zeros((TOKENS, 112), F32)], axis=1)
    for i in range(18):
        spread = pltpu.roll(tail[8 * i : 8 * i + 8, :], 0, 1, stride=16, stride_axis=0)
        places[TOKENS + i : TOKENS + i + 1, :] = jnp.sum(spread, axis=0, keepdims=True).astype(jnp.int32)

    first = core_ref[0] == 0
    for block in range(BLOCKS):
        count = min(256, BIAS_ROWS - block * 256)
        top = table[0:8, block * 256 : block * 256 + count]
        bottom = table[8:16, block * 256 : block * 256 + count]
        part = jnp.concatenate(
            [jnp.where(first, bottom, top), jnp.where(first, top, bottom)], axis=0
        )
        if count < 256:
            part = jnp.concatenate([part, jnp.zeros((16, 256 - count), F32)], axis=1)
        left[block * 32 : block * 32 + 16, :], left[block * 32 + 16 : block * 32 + 32, :] = halves(
            part
        )
    lines = line_numbers()
    matrix = left[...]

    def find(rows):
        right = jnp.concatenate([one_hot(row, lines) for row in rows], axis=1)
        found = dot(matrix, right, NN)
        block = jnp.concatenate([row >> 8 for row in rows], axis=1)
        block = jnp.broadcast_to(block, (32, 256))
        total = jnp.zeros((32, 256), F32)
        for b in range(BLOCKS):
            total = jnp.where(block == b, found[b * 32 : b * 32 + 32], total)
        return total[:16] + total[16:]

    def step(i, carry):
        base = pl.multiple_of(i * 8, 8)
        rows = places[pl.ds(base, 8), :]
        for pair in range(4):
            found = find([rows[2 * pair + j : 2 * pair + j + 1, :] for j in range(2)])
            for j in range(2):
                bias[base + 2 * pair + j, :, 0:128] = found[:, j * 128 : j * 128 + 128]
        return carry

    lax.fori_loop(0, 18, step, 0, unroll=18)
    for pair in range(9):
        at = TOKENS + 2 * pair
        found = find([places[at + j : at + j + 1, :] for j in range(2)])
        for j in range(16):
            bias[16 * pair + j, :, 128:144] = found[:, 16 * j : 16 * j + 16]


def lookup(core, bias_index, bias_table):
    return pl.pallas_call(
        lookup_kernel,
        out_shape=[
            jax.ShapeDtypeStruct((TOKENS, HEADS, TOKENS), F32),
            jax.ShapeDtypeStruct((ROWS, 128), jnp.int32),
        ],
        in_specs=[scalar()] + whole(2),
        out_specs=whole(2),
        scratch_shapes=[pltpu.VMEM((BLOCKS * 32, 256), BF16)],
        compiler_params=params(),
        cost_estimate=cost(LOOKUP_COST),
        name="lookup",
    )(core, bias_index, bias_table.T)


def main_kernel(
    core_ref,
    own,
    quad0,
    quad1,
    quad3,
    bias,
    in_weight,
    out_weight,
    keep,
    send,
    keep_scores,
    send_scores,
    grad0,
    grad1,
    grad2,
    grad3,
    tokens,
    cotangent,
    proj,
    gatt,
    gproj,
    att,
    normed_t,
    tails,
):
    core = core_ref[0]
    row = jnp.zeros((1, WIDTH), F32)
    for slot, (quad, start) in enumerate(((quad0, 0), (quad1, 0), (own, 0), (quad3, 0))):
        at = slot * QUAD
        tokens[at : at + QUAD, :] = quad[start : start + QUAD, :]
        cotangent[at : at + QUAD, :] = quad[start + QUAD : start + 2 * QUAD, :]
        row = row + quad[start + 72 : start + 73, :]
    row = row[:, :TOKENS]
    side = lax.broadcasted_iota(jnp.int32, (TOKENS, TOKENS), 0)
    along = lax.broadcasted_iota(jnp.int32, (TOKENS, TOKENS), 1)
    spread = jnp.broadcast_to(row, (TOKENS, TOKENS))
    column = jnp.sum(jnp.where(side == along, spread, 0.0), axis=1, keepdims=True)
    allowed = column == spread

    inputs = tokens[...]
    centered = inputs - jnp.mean(inputs, axis=1, keepdims=True)
    variance = jnp.mean(centered * centered, axis=1, keepdims=True)
    inv_std = lax.rsqrt(variance + 1e-05)
    normed = centered * inv_std
    tokens[...] = normed
    normed_t[...] = normed.T
    halves_normed = halves(normed)
    for part in range(3):
        at = part * WIDTH
        weight = halves(in_weight[:, at : at + WIDTH])
        proj[at : at + WIDTH, :] = dot3(halves_normed, weight, NN).T
    halves_cotangent = halves(cotangent[...])
    gatt[...] = dot3(halves(out_weight[...]), halves_cotangent, NT)

    def stacked(*parts):
        return jnp.concatenate(parts, axis=0)

    def product(high, low, right_high, right_low, dims):
        both = dot(stacked(high, low), right_high, dims)
        return both[:HEAD_DIM] + (both[HEAD_DIM:] + dot(high, right_low, dims))

    def some_heads(heads):
        ats = [pl.multiple_of(head * HEAD_DIM, HEAD_DIM) for head, _ in heads]
        q = [halves(proj[pl.ds(at, HEAD_DIM), :] * FACTOR) for at in ats]
        k = [halves(proj[pl.ds(at + WIDTH, HEAD_DIM), :]) for at in ats]
        v = [halves(proj[pl.ds(at + 2 * WIDTH, HEAD_DIM), :]) for at in ats]
        g = [halves(gatt[pl.ds(at, HEAD_DIM), :]) for at in ats]

        def outer(left, right):
            return dot(
                stacked(left[0], left[0], left[1]), stacked(right[0], right[1], right[0]), TN
            )

        scores = [
            outer(q[i], k[i]) + bias[:, slot, :]
            for i, (_, slot) in enumerate(heads)
        ]
        grad_probs = [outer(g[i], v[i]) for i in range(len(heads))]
        scores = [jnp.where(allowed, x, -1000000000.0) for x in scores]
        exponent = [jnp.exp(x - jnp.max(x, axis=1, keepdims=True)) for x in scores]
        probs = [x * pl.reciprocal(jnp.sum(x, axis=1, keepdims=True)) for x in exponent]
        p = [halves(x) for x in probs]
        for i, at in enumerate(ats):
            att[pl.ds(at, HEAD_DIM), :] = product(*v[i], *p[i], NT)
            gproj[pl.ds(at + 2 * WIDTH, HEAD_DIM), :] = product(*g[i], *p[i], NN)
        grad_scores = [
            x * (y - jnp.sum(x * y, axis=1, keepdims=True)) for x, y in zip(probs, grad_probs)
        ]
        s = [halves(x) for x in grad_scores]
        for i, at in enumerate(ats):
            gproj[pl.ds(at, HEAD_DIM), :] = product(*k[i], *s[i], NT) * FACTOR
            gproj[pl.ds(at + WIDTH, HEAD_DIM), :] = product(*q[i], *s[i], NN)
        for i, (_, slot) in enumerate(heads):
            target = send_scores if slot < 8 else keep_scores
            target[0:TOKENS, slot % 8, :] = grad_scores[i][:, :128]
            tails[:, slot, 0:16] = grad_scores[i][:, 128:]

    tails[...] = jnp.zeros_like(tails)
    order = [((1 - core) * 8 + slot, slot) for slot in range(8)]
    order += [(core * 8 + slot, 8 + slot) for slot in range(8)]
    some_heads(order)

    for i in range(18):
        total = tails[8 * i]
        for j in range(1, 8):
            total = total + pltpu.roll(tails[8 * i + j], 16 * j, 1)
        send_scores[TOKENS + i] = total[0:8]
        keep_scores[TOKENS + i] = total[8:16]

    for target, bit in ((send, 1 - core), (keep, core)):
        rows = [pl.ds(pl.multiple_of(64 * i + 32 * bit, 32), 32) for i in range(8)]
        left = halves(jnp.concatenate([normed_t[r, :] for r in rows], axis=0))
        for part in range(3):
            at = part * WIDTH
            target[:, at : at + WIDTH] = dot3(left, halves(gproj[at : at + WIDTH, :]), NT)
        left = halves(jnp.concatenate([att[r, :] for r in rows], axis=0))
        target[:, 3 * WIDTH :] = dot3(left, halves_cotangent, NN)

    grad_normed = jnp.zeros((WIDTH, TOKENS), F32)
    for part in range(3):
        at = part * WIDTH
        grad_normed = grad_normed + dot3(
            halves(in_weight[:, at : at + WIDTH]), halves(gproj[at : at + WIDTH, :]), NN
        )
    grad_normed = grad_normed.T
    normed = tokens[...]
    result = inv_std * (
        grad_normed
        - jnp.mean(grad_normed, axis=1, keepdims=True)
        - normed * jnp.mean(grad_normed * normed, axis=1, keepdims=True)
    )
    tokens[...] = result
    for slot, target in enumerate((grad0, grad1, grad2, grad3)):
        target[...] = tokens[slot * QUAD : slot * QUAD + QUAD, :]


def shape(*dims):
    return jax.ShapeDtypeStruct(dims, F32)


def window(core, own, quad0, quad1, quad3, bias, in_weight, out_weight):
    grad = shape(QUAD, WIDTH)
    return pl.pallas_call(
        main_kernel,
        out_shape=[
            shape(256, 4 * WIDTH),
            shape(256, 4 * WIDTH),
            shape(ROWS, 8, 128),
            shape(ROWS, 8, 128),
            grad,
            grad,
            grad,
            grad,
        ],
        in_specs=[scalar()] + whole(7),
        out_specs=whole(8),
        scratch_shapes=[
            pltpu.VMEM((TOKENS, WIDTH), F32),
            pltpu.VMEM((TOKENS, WIDTH), F32),
            pltpu.VMEM((3 * WIDTH, TOKENS), F32),
            pltpu.VMEM((WIDTH, TOKENS), F32),
            pltpu.VMEM((3 * WIDTH, TOKENS), F32),
            pltpu.VMEM((WIDTH, TOKENS), F32),
            pltpu.VMEM((WIDTH, TOKENS), F32),
            pltpu.VMEM((TOKENS, HEADS, 128), F32),
        ],
        compiler_params=params(26),
        cost_estimate=cost(WINDOW_COST),
        name="window",
    )(core, own, quad0, quad1, quad3, bias, in_weight, out_weight)


def add_pairs(places, keep, came, total):
    lines = line_numbers()

    def sides(row, values):
        block = (row >> 8).astype(F32).astype(BF16)
        both = jnp.concatenate(halves(values), axis=0)
        spread = jnp.broadcast_to(block, (16, 128))
        left = jnp.concatenate(
            [jnp.where(spread == float(b), both, jnp.zeros_like(both)) for b in range(BLOCKS)],
            axis=0,
        )
        return left, one_hot(row, lines)

    def add(rows, base, pair):
        pieces = [
            sides(rows[j : j + 1, :], keep[base + j] + came[base + j])
            for j in (2 * pair, 2 * pair + 1)
        ]
        left = jnp.concatenate([p[0] for p in pieces], axis=1)
        right = jnp.concatenate([p[1] for p in pieces], axis=1)
        total[...] += dot(left, right, NT)

    def step(i, carry):
        base = pl.multiple_of(i * 8, 8)
        rows = places[pl.ds(base, 8), :]
        for pair in range(4):
            add(rows, base, pair)
        return carry

    lax.fori_loop(0, ROWS // 8, step, 0, unroll=20)
    add(places[ROWS - 2 : ROWS, :], ROWS - 2, 0)


def scatter_kernel(core_ref, places, keep, came, mine, other, total, line, sectors):
    total[...] = jnp.zeros_like(total)
    add_pairs(places, keep, came, total)
    for b in range(BLOCKS):
        line[:, b * 256 : b * 256 + 256] = (
            total[b * 16 : b * 16 + 8, :] + total[b * 16 + 8 : b * 16 + 16, :]
        )
    line[:, BLOCKS * 256 :] = jnp.zeros((8, 256), F32)
    for m in range(32):
        chip, core, half = m // 4, m // 2 % 2, m % 2
        start_at = m * HALF_SECTOR
        base, shift = start_at // 128 * 128, start_at % 128
        piece = line[:, base : base + 512]
        if shift:
            piece = pltpu.roll(piece, 512 - shift, 1)
        sectors[core, chip, half * 8 : half * 8 + 8, :] = piece[:, :256]
    mine[...] = sectors[core_ref[0]]
    other[...] = sectors[1 - core_ref[0]]


def scatter(core, places, keep, came):
    return pl.pallas_call(
        scatter_kernel,
        out_shape=[shape(8, 16, 256)] * 2,
        in_specs=[scalar()] + whole(3),
        out_specs=whole(2),
        scratch_shapes=[
            pltpu.VMEM((BLOCKS * 16, 256), F32),
            pltpu.VMEM((8, BLOCKS * 256 + 256), F32),
            pltpu.VMEM((2, 8, 16, 256), F32),
        ],
        compiler_params=params(),
        cost_estimate=cost(SCATTER_COST),
        name="scatter",
    )(core, places, keep, came)


def split_kernel(odd, keep, came, own, send_a, send_b):
    def columns(bit):
        cols = slice(512 * bit, 512 * bit + 512)
        return keep[:, cols] + came[:, cols]

    for bit in range(2):

        @pl.when(odd[0] == bit)
        def _():
            send_a[...] = columns(1 - bit)
            send_b[...] = columns(2 + bit)
            own[:, 0:512] = columns(bit)
            own[:, 512:1024] = columns(3 - bit)


def split(odd, keep, came):
    return pl.pallas_call(
        split_kernel,
        out_shape=[shape(256, 1024), shape(256, 512), shape(256, 512)],
        in_specs=[scalar()] + whole(2),
        out_specs=whole(3),
        compiler_params=params(),
        name="split",
    )(odd, keep, came)


def join_kernel(core_ref, own, came_a, came_b, table_keep, table_came, out):
    for i in range(8):
        rows = slice(i * 32, i * 32 + 32)
        out[i, :, 0:512] = own[rows, 0:512] + came_a[rows, :]
        out[i, :, 512:1024] = own[rows, 512:1024] + came_b[rows, :]
    first = core_ref[0] == 0
    mine, other = table_keep[...], table_came[...]
    out[:, 0:16, 1024:] = jnp.where(first, mine, other)
    out[:, 16:32, 1024:] = jnp.where(first, other, mine)


def join(core, *parts):
    return pl.pallas_call(
        join_kernel,
        out_shape=shape(8, 32, 1280),
        in_specs=[scalar()] + whole(5),
        out_specs=pl.BlockSpec(memory_space=pltpu.VMEM),
        compiler_params=params(),
        name="join",
    )(core, *parts)


def fold_lon_kernel(parts, out, total):
    value = parts[0]
    for i in range(1, 8):
        value = value + parts[i]
    total[...] = value
    for i in range(8):
        out[i] = total[4 * i : 4 * i + 4, :]


def fold_lon(parts):
    return pl.pallas_call(
        fold_lon_kernel,
        out_shape=shape(8, 4, 1280),
        in_specs=whole(1),
        out_specs=pl.BlockSpec(memory_space=pltpu.VMEM),
        scratch_shapes=[pltpu.VMEM((32, 1280), F32)],
        compiler_params=params(),
        name="fold_lon",
    )(parts)


def fold_lat_kernel(parts, out):
    total = parts[0]
    for i in range(1, 8):
        total = total + parts[i]
    for i in range(16):
        out[i] = total


def fold_lat(parts):
    return pl.pallas_call(
        fold_lat_kernel,
        out_shape=shape(16, 4, 1280),
        in_specs=whole(1),
        out_specs=pl.BlockSpec(memory_space=pltpu.VMEM),
        compiler_params=params(),
        name="fold_lat",
    )(parts)


def unpack_kernel(parts, grad_in, grad_out, grad_bias, table):
    for rank in range(8):
        rows = slice(4 * rank, 4 * rank + 4)
        even = (rank // 2) * 4 + rank % 2
        odd = even + 2
        grad_in[rows, 0:512] = parts[even, :, 0:512]
        grad_in[rows, 512:1024] = parts[odd, :, 0:512]
        grad_in[rows, 1024:1536] = parts[odd, :, 512:1024]
        grad_out[rows, :] = parts[even, :, 512:1024]
        table[rows, :] = parts[even, :, 1024:] + parts[odd, :, 1024:]
    for core in range(2):
        for half in range(2):
            base = core * 16 + half * 8
            grad_bias[core * 8 : core * 8 + 8, half * HALF_SECTOR : (half + 1) * HALF_SECTOR] = (
                table[base : base + 8, :HALF_SECTOR]
            )


def unpack(parts):
    return pl.pallas_call(
        unpack_kernel,
        out_shape=[shape(32, 3 * WIDTH), shape(32, WIDTH), shape(HEADS, 2 * HALF_SECTOR)],
        in_specs=whole(1),
        out_specs=whole(3),
        scratch_shapes=[pltpu.VMEM((32, 256), F32)],
        compiler_params=params(),
        name="unpack",
    )(parts)


def place_kernel(grad_out, own, left, below, corner, out):
    for ref, row0, col0 in ((own, 0, 3), (left, 0, 0), (below, 6, 3), (corner, 6, 0)):
        for row in range(6):
            for col in range(3):
                spot = row * 6 + col * 2
                out[row0 + row, col0 + col] = (
                    grad_out[row0 + row, col0 + col] + ref[spot : spot + 2, :]
                )


def place(grad_out, own, left, below, corner):
    return pl.pallas_call(
        place_kernel,
        out_shape=jax.ShapeDtypeStruct(grad_out.shape, F32),
        in_specs=whole(5),
        out_specs=pl.BlockSpec(memory_space=pltpu.VMEM),
        compiler_params=params(),
        name="place",
    )(grad_out, own, left, below, corner)


LAT = ("z", "y_lo")
LON = ("x", "y_hi", "core")


def body(fields, grad_out, region_ids, bias_index, bias_table, in_weight, out_weight):
    everything = LAT + LON
    lat = lax.axis_index(LAT)
    core = lax.axis_index("core").reshape(1)
    odd = lax.rem(lax.axis_index("z"), 2).reshape(1)

    def moves(down, right):
        return [
            (i * 16 + j, (i + down) % 16 * 16 + (j + right) % 16)
            for i in range(16)
            for j in range(16)
        ]

    swap = [(0, 1), (1, 0)]
    last = jnp.where(lat == 15, 3, 0).reshape(1)
    grad_out = jnp.transpose(grad_out, (1, 2, 0, 3))
    own, left, below, corner = pack(
        last, jnp.transpose(fields, (1, 2, 0, 3)), grad_out, jnp.transpose(region_ids, (2, 0, 1))
    )
    quad3 = lax.ppermute(left, everything, moves(0, -1))
    quad0 = lax.ppermute(below, everything, moves(1, 0))
    quad1 = lax.ppermute(corner, everything, moves(1, -1))
    bias, places = lookup(core, bias_index, bias_table)
    keep, send, keep_scores, send_scores, grad0, grad1, grad2, grad3 = window(
        core, own, quad0, quad1, quad3, bias, in_weight, out_weight
    )
    came = lax.ppermute(send, "core", swap)
    came_scores = lax.ppermute(send_scores, "core", swap)
    back = (
        lax.ppermute(grad3, everything, moves(0, 1)),
        lax.ppermute(grad0, everything, moves(-1, 0)),
        lax.ppermute(grad1, everything, moves(-1, 1)),
    )
    part, send_a, send_b = split(odd, keep, came)
    came_a = lax.ppermute(send_a, "z", [(i, i ^ 1) for i in range(8)])
    came_b = lax.ppermute(send_b, "z", [(i, ((i + 1) % 8 ^ 1) + 7 & 7) for i in range(8)])
    part, places, back = lax.optimization_barrier((part, places, back))
    mine, other = scatter(core, places, keep_scores, came_scores)
    came_table = lax.ppermute(other, "core", swap)
    mine, grad2 = lax.optimization_barrier((mine, grad2))
    grad_fields = place(grad_out, grad2, *back)
    part, grad_fields = lax.optimization_barrier((part, grad_fields))
    joined = join(core, part, came_a, came_b, mine, came_table)
    parts = lax.all_to_all(joined, ("x", "y_hi"), 0, 0)
    parity = [[z * 2 + y for z in range(bit, 8, 2) for y in range(2)] for bit in range(2)]
    parts = lax.all_to_all(fold_lon(parts), LAT, 0, 0, axis_index_groups=parity)
    parts = lax.all_to_all(fold_lat(parts), LAT, 0, 0)
    grad_in_weight, grad_out_weight, grad_bias = unpack(parts)
    return jnp.transpose(grad_fields, (2, 0, 1, 3)), grad_in_weight, grad_out_weight, grad_bias.T


def solution(mesh):
    split = Mesh(mesh.devices.reshape(8, 2, 4, 2, 2), LAT + LON)
    tokens = P(None, LAT, LON, None)
    in_specs = (tokens, tokens, P(None, LAT, LON), P(), P(), P(), P())
    out_specs = (tokens, P(LON, None), P(LON, None), P(LON, None))
    return jax.shard_map(body, mesh=split, in_specs=in_specs, out_specs=out_specs, check_vma=False)
```
